128 devices in a mesh: section: 2 (over x_hi), dp: 16 (over z, y), tensor: 4 (over x_lo, core).
Axes of the slice: x: 4 (x_hi: 2, x_lo: 2; x = x_hi * 2 + x_lo), y: 4, z: 4, core: 2. Of those that a mesh axis runs over, the one named last changes fastest.
Arguments:
- hidden_in: bfloat16 [2, 4096, 8192], P('section', 'dp', 'tensor'), may hold values from -3.5 to 3.5
- preact: bfloat16 [2, 4096, 8192], P('section', 'dp', 'tensor'), may hold values from -6 to 6
- norm_gain: float32 [2, 8192], P('section', 'tensor'), may hold values from 0.5 to 1.5
- weight: bfloat16 [2, 8192, 8192], P('section', 'dp', 'tensor')
- bank: float32 [256, 256], replicated, may hold values from -0.18 to 0.18
- mix_index: int32 [2, 2, 128, 2], P('section'), may hold values from 0 to 255
- mix_weight: float32 [2, 2, 128, 2], P('section'), may hold values from 0.1 to 1
- grad_top: bfloat16 [4096, 8192], P('dp', 'tensor'), may hold values from -3.5 to 3.5
Outputs:
- grad_inputs: bfloat16 [2, 4096, 8192], P('section', 'dp', 'tensor')
- bank_grad: float32 [256, 256], replicated
The draws below stay inside these ranges and needn't reach their ends.
All inputs are finite; a program needn't handle non-finite values.
Results may differ from the reference program's by a relative error of at most 0.014.
Values may be sent and summed in bfloat16 or wider, within the bound.
No kernel may reach another device: no remote copies, remote signals or barrier semaphores. Data moves between devices by JAX's collectives and lax.ppermute only.
A program may use at most 128 MiB of HBM per device.

```python
import math
import jax
import jax.numpy as jnp
from jax import lax

MODEL_WIDTH = 8192
RANK = 4
SUB = 256
BANK = 256
LAYERS = 2
TOKENS = 4096
NSUB = 128
N_TENSOR = 4


def shared_rows(key):
    return jax.random.normal(key, (TOKENS, MODEL_WIDTH), jnp.float32)


def column_scale(lowest, ratio):
    columns = lax.broadcasted_iota(jnp.int32, (1, 1, MODEL_WIDTH), 2).astype(jnp.float32)
    return lowest * jnp.exp(math.log(ratio) * columns / (MODEL_WIDTH - 1))


def draw_hidden_in(key, part):
    common = shared_rows(key)
    key = jax.random.fold_in(key, 11)
    own = jax.random.normal(key, (LAYERS, TOKENS, MODEL_WIDTH), jnp.float32)
    scales = column_scale(0.6, 4.0)
    values = (0.8 * common[None] + 0.6 * own) * scales
    return jnp.clip(values, -3.5, 3.5).astype(jnp.bfloat16)


def draw_grad_top(key, part):
    common = shared_rows(key)
    key = jax.random.fold_in(key, 12)
    sign_key, noise_key = jax.random.split(key)
    signs = (jax.random.randint(sign_key, (TOKENS, 1), 0, 2) * 2 - 1).astype(jnp.float32)
    noise = jax.random.normal(noise_key, (TOKENS, MODEL_WIDTH), jnp.float32)
    values = 0.6 * signs * common + 0.8 * noise
    return jnp.clip(values, -3.5, 3.5).astype(jnp.bfloat16)


def draw_weight(key, part):
    key = jax.random.fold_in(key, 13)
    random_part = jnp.clip(jax.random.normal(key, (LAYERS, MODEL_WIDTH, MODEL_WIDTH), jnp.float32), -3.0, 3.0)
    rows = lax.broadcasted_iota(jnp.int32, (1, MODEL_WIDTH, MODEL_WIDTH), 1)
    columns = lax.broadcasted_iota(jnp.int32, (1, MODEL_WIDTH, MODEL_WIDTH), 2)
    diagonal_part = (rows == columns).astype(jnp.float32)
    values = random_part * (1.0 / math.sqrt(MODEL_WIDTH)) + diagonal_part
    return values.astype(jnp.bfloat16)


def place_ends(drawn, key, low, high):
    index_at = [jax.random.randint(jax.random.fold_in(key, axis), (), 0, length) for axis, length in enumerate(drawn.shape)]
    longest = drawn.shape.index(max(drawn.shape))
    beside = index_at[:longest] + [(index_at[longest] + 1) % drawn.shape[longest]] + index_at[longest + 1:]
    return drawn.at[tuple(index_at)].set(low).at[tuple(beside)].set(high)


def steps_of(stream_key, dims, pieces, smallest, high):
    def one(position, blocks):
        draws = jax.random.uniform(jax.random.fold_in(jax.random.fold_in(stream_key, 6), position), (blocks,), jnp.float32, smallest / len(pieces), high / len(pieces))
        return jnp.repeat(jnp.exp(draws), dims[position] // blocks).reshape((-1,) + (1,) * (len(dims) - position - 1))

    factor_of = one(*pieces[0])
    for cut in pieces[1:]:
        factor_of = factor_of * one(*cut)
    return factor_of


def gaussian(key, extent, spread, limit, shards=(), dtype=jnp.bfloat16):
    array = spread * jax.random.normal(key, extent, jnp.float32)
    if shards:
        array = array * steps_of(key, extent, shards, -0.22, 0.18)
    return jnp.clip(array, -limit, limit).astype(dtype)


def setup_inputs(seed: int = 0) -> dict:
    seeds = jax.random.split(jax.random.key(seed), 9)
    return {
        "hidden_in": draw_hidden_in(jax.random.fold_in(seeds[8], 71), 0),
        "preact": gaussian(seeds[1], (LAYERS, TOKENS, MODEL_WIDTH), 1.5, 6.0, ((0, 2), (1, 16), (2, 4))),
        "norm_gain": jnp.clip(1.0 + 0.1 * jax.random.normal(seeds[2], (LAYERS, MODEL_WIDTH), jnp.float32), 0.5, 1.5),
        "weight": draw_weight(jax.random.fold_in(seeds[8], 71), 0),
        "bank": gaussian(seeds[4], (BANK, SUB), 0.03, 0.18, (), jnp.float32),
        "mix_index": place_ends(jax.random.randint(seeds[5], (LAYERS, 2, NSUB, 2), 0, BANK), jax.random.fold_in(seeds[5], 1), 0, BANK - 1).astype(jnp.int32),
        "mix_weight": jnp.clip(0.1 + 0.9 * jax.random.uniform(seeds[6], (LAYERS, 2, NSUB, 2), jnp.float32) ** steps_of(seeds[6], (LAYERS, 2, NSUB, 2), ((0, 2),), -0.2, 0.2), 0.1, 1.0),
        "grad_top": draw_grad_top(jax.random.fold_in(seeds[8], 71), 0),
    }


epsilon = 1e-06

def compose(index_layer, weight_layer, bank):
    columns = lax.broadcasted_iota(jnp.int32, (1, 1, 1, bank.shape[0]), 3)
    onehot = (index_layer[..., None] == columns).astype(jnp.float32)
    return lax.optimization_barrier(jnp.sum(onehot * weight_layer[..., None].astype(jnp.float32), axis=2))

def silu_slope(value):
    sig = jax.nn.sigmoid(value)
    return sig * (1.0 + value * (1.0 - sig))

def reference(hidden_in, preact, norm_gain, weight, bank, mix_index, mix_weight, grad_top):
    high = lax.Precision.HIGHEST
    width = MODEL_WIDTH // N_TENSOR
    upstream_bf = grad_top
    results = []
    bank_acc = jnp.zeros((BANK, SUB), jnp.float32)
    for layer in reversed(range(LAYERS)):
        hidden_state = hidden_in[layer].astype(jnp.float32)
        gain_vector = norm_gain[layer].astype(jnp.float32)
        inverse_norm_scale = lax.rsqrt(lax.optimization_barrier(jnp.sum(hidden_state * hidden_state, axis=1, keepdims=True)) / MODEL_WIDTH + epsilon)
        centered_input = hidden_state * inverse_norm_scale
        normalized_rows = (centered_input * gain_vector).astype(jnp.bfloat16)
        normalized_float = normalized_rows.astype(jnp.float32)
        mixing = compose(mix_index[layer], mix_weight[layer], bank)
        factors = jnp.einsum('fnb,bs->fns', mixing, bank, precision=high)
        a_full = factors[0].reshape(RANK, MODEL_WIDTH)
        b_full = factors[1].reshape(RANK, MODEL_WIDTH)
        projected = jnp.dot(normalized_float, a_full.T, precision=high)
        incoming_gradient = upstream_bf.astype(jnp.float32)
        slope = silu_slope(preact[layer].astype(jnp.float32))
        grad_z = (incoming_gradient * slope).astype(jnp.bfloat16)
        grad_zf = grad_z.astype(jnp.float32)
        residual_gradient = jnp.zeros((TOKENS, MODEL_WIDTH), jnp.float32)
        mixed = jnp.zeros((TOKENS, RANK), jnp.float32)
        for block in range(N_TENSOR):
            lower = block * width
            upper = lower + width
            mixed_part = jnp.dot(grad_zf[:, lower:upper], b_full[:, lower:upper].T, precision=high)
            part = jnp.dot(grad_z[:, lower:upper], weight[layer][:, lower:upper].T, preferred_element_type=jnp.float32)
            part = part + jnp.dot(mixed_part, a_full, precision=high)
            residual_gradient = residual_gradient + lax.optimization_barrier(part.astype(jnp.bfloat16)).astype(jnp.float32)
            mixed = mixed + mixed_part
        row_inner_product = lax.optimization_barrier(jnp.sum(gain_vector * residual_gradient * centered_input, axis=1, keepdims=True))
        hidden_gradient = (incoming_gradient + inverse_norm_scale * (gain_vector * residual_gradient - centered_input * (row_inner_product / MODEL_WIDTH))).astype(jnp.bfloat16)
        grad_a = jnp.dot(mixed.T, normalized_float, precision=high).reshape(-1, SUB)
        grad_b = jnp.dot(projected.T, grad_zf, precision=high).reshape(-1, SUB)
        bank_acc = bank_acc + jnp.dot(mixing[0].T, grad_a, precision=high) + jnp.dot(mixing[1].T, grad_b, precision=high)
        results.append(hidden_gradient)
        upstream_bf = hidden_gradient
    grad_inputs = jnp.stack(results[::-1], axis=0)
    return (grad_inputs, bank_acc / math.sqrt(TOKENS))
```

```python
import math

import jax
import jax.numpy as jnp
from jax import lax
from jax.sharding import Mesh, PartitionSpec as P

MODEL_WIDTH = 8192
RANK = 4
SUB = 256
TOKENS = 4096
RING = 4
CHUNKS = 2

epsilon = 1e-06
HIGH = lax.Precision.HIGHEST


def ring_route(distance, sections=(0, 1)):
    return [(s * RING + i, s * RING + (i + distance) % RING) for s in sections for i in range(RING)]


def gather_ring(block, axis, sections=(0, 1)):
    axes = ("section", axis)
    half = block.shape[0] // 2
    after = lax.ppermute(block, axes, ring_route(-1, sections))
    before = lax.ppermute(block, axes, ring_route(1, sections))
    far_low = lax.ppermute(after[:half], axes, ring_route(-1, sections))
    far_high = lax.ppermute(before[half:], axes, ring_route(1, sections))
    return block, after, far_low, far_high, before


def swap(block, axis, sections=(0, 1)):
    pairs = [(s * 2 + i, s * 2 + 1 - i) for s in sections for i in range(2)]
    return lax.ppermute(block, ("section", axis), pairs)


def butterfly(value, axis, bit):
    size = lax.axis_size(axis)
    return value + lax.ppermute(value, axis, [(i, i ^ bit) for i in range(size)])


def compose(index_layer, weight_layer, rows):
    columns = lax.broadcasted_iota(jnp.int32, (1, 1, 1, 1, rows), 4)
    onehot = (index_layer[..., None] == columns).astype(jnp.float32)
    return jnp.sum(onehot * weight_layer[..., None], axis=3)


def silu_slope(value):
    sig = jax.nn.sigmoid(value)
    return sig * (1.0 + value * (1.0 - sig))


def after(value, earlier):
    return lax.optimization_barrier((value, earlier))[0]


def pick(stack, index):
    return lax.dynamic_index_in_dim(stack, index, 0, keepdims=False)


def shards(hidden_in, preact, norm_gain, weight, bank, mix_index, mix_weight, grad_top):
    section = lax.axis_index("section")
    z, y = lax.axis_index("z"), lax.axis_index("y")
    pair, core = lax.axis_index("pair"), lax.axis_index("core")
    place = pair * 2 + core
    tensor = ("pair", "core")
    bank_rows = bank.shape[0]
    top_layer = section == 1

    tokens, local_width = grad_top.shape
    chunk = tokens // CHUNKS
    seg_local = local_width // SUB
    seg_row = MODEL_WIDTH // SUB

    own_weight = weight[0]
    pieces_w = gather_ring(own_weight, "z")

    slope = silu_slope(preact[0].astype(jnp.float32))
    gain = norm_gain[0]
    hidden = hidden_in[0].astype(jnp.float32)

    def local_pieces(array):
        array = array.reshape(2, RANK, seg_row, 2)
        return lax.dynamic_slice_in_dim(array, place * seg_local, seg_local, 2)

    mixing = compose(local_pieces(mix_index[0]), local_pieces(mix_weight[0]), bank_rows)
    mixing = mixing.reshape(2, RANK * seg_local, bank_rows)
    factors = jnp.einsum("fnb,bs->fns", mixing, bank, precision=HIGH)
    a_local = factors[0].reshape(RANK, local_width)
    b_local = factors[1].reshape(RANK, local_width)

    def make_dz(incoming, c):
        rows = slice(c * chunk, (c + 1) * chunk)
        return (incoming.astype(jnp.float32) * slope[rows]).astype(jnp.bfloat16)

    top = [grad_top[c * chunk:(c + 1) * chunk] for c in range(CHUNKS)]
    dz_top = [make_dz(top[c], c) for c in range(CHUNKS)]
    dz_top_all = jnp.concatenate(dz_top, axis=0)

    sums = lax.psum(
        jnp.concatenate(
            [
                jnp.sum(hidden * hidden, axis=1, keepdims=True),
                jnp.dot(hidden * gain, a_local.T, precision=HIGH),
                jnp.dot(dz_top_all.astype(jnp.float32), b_local.T, precision=HIGH),
            ],
            axis=1,
        ),
        tensor,
    )
    scale = lax.rsqrt(sums[:, :1] / MODEL_WIDTH + epsilon)
    projected = sums[:, 1:1 + RANK] * scale
    mixed_top = sums[:, 1 + RANK:]
    xhat = hidden * scale
    x = (xhat * gain).astype(jnp.bfloat16)

    def projection_gradient(dz, sections):
        gathered = jnp.concatenate(gather_ring(dz, "y", sections), axis=0)

        def product(piece):
            return lax.dot_general(
                gathered, piece, (((1,), (1,)), ((), ())), preferred_element_type=jnp.float32
            ).astype(jnp.bfloat16)

        own, after, far_low, far_high, before = pieces_w
        parts = jnp.stack(
            [
                product(own),
                product(after),
                jnp.concatenate([product(far_low), product(far_high)], axis=1),
                product(before),
            ]
        )
        odd = (core - z) % 2
        parts = parts.reshape(2, 2, *parts.shape[1:])
        keep = lax.dynamic_index_in_dim(parts, odd, 1, keepdims=False)
        send = lax.dynamic_index_in_dim(parts, 1 - odd, 1, keepdims=False)
        got = swap(send, "core", sections)
        high_of = (place - z) % 4 // 2
        high_other = (place ^ 2) - z
        high_other = high_other % 4 // 2
        mine = pick(keep, high_of).astype(jnp.float32) + pick(got, high_of).astype(jnp.float32)
        theirs = pick(keep, high_other).astype(jnp.float32) + pick(got, high_other).astype(jnp.float32)
        other = swap(theirs.astype(jnp.bfloat16), "pair", sections)
        total = (mine + other.astype(jnp.float32)).astype(jnp.bfloat16)
        total = total.reshape(RING, chunk, total.shape[1])
        axes = ("section", "y")
        from_before = lax.ppermute(total[1], axes, ring_route(1, sections))
        from_far = lax.ppermute(total[2], axes, ring_route(2, sections))
        from_after = lax.ppermute(total[3], axes, ring_route(-1, sections))
        got = jnp.stack([total[0], from_after, from_far, from_before])
        return jnp.concatenate([pick(got, (j - y) % 4) for j in range(RING)], axis=1).astype(jnp.float32)

    def layer(incoming, dz, mixed, c, sections, earlier):
        rows = slice(c * chunk, (c + 1) * chunk)
        dx = projection_gradient(dz, sections) + jnp.dot(mixed, a_local, precision=HIGH)
        scaled = gain * dx
        inner = lax.psum(after(jnp.sum(scaled * xhat[rows], axis=1), earlier), tensor)
        return (
            incoming.astype(jnp.float32)
            + scale[rows] * (scaled - xhat[rows] * (inner / MODEL_WIDTH)[:, None])
        ).astype(jnp.bfloat16)

    top_grads = []
    earlier = mixed_top
    low_in = []
    for c in range(CHUNKS):
        rows = slice(c * chunk, (c + 1) * chunk)
        grad = layer(top[c], dz_top[c], mixed_top[rows], c, (1,), earlier)
        earlier = grad
        top_grads.append(grad)
        low_in.append(lax.ppermute(grad, "section", [(1, 0)]))
    low_grads, low_dz, low_mixed = [], [], []
    for c in range(CHUNKS):
        dz = make_dz(low_in[c], c)
        mixed = jnp.dot(dz.astype(jnp.float32), b_local.T, precision=HIGH)
        mixed = lax.psum(after(mixed, earlier), tensor)
        low_grads.append(layer(low_in[c], dz, mixed, c, (0,), mixed))
        earlier = low_grads[-1]
        low_dz.append(dz)
        low_mixed.append(mixed)

    result = jnp.where(top_layer, jnp.concatenate(top_grads, axis=0), jnp.concatenate(low_grads, axis=0))

    dz = jnp.where(top_layer, dz_top_all, jnp.concatenate(low_dz, axis=0))
    mixed = jnp.where(top_layer, mixed_top, jnp.concatenate(low_mixed, axis=0))
    grad_a = jnp.dot(mixed.T, x.astype(jnp.float32), precision=HIGH)
    grad_b = jnp.dot(projected.T, dz.astype(jnp.float32), precision=HIGH)
    grads = jnp.concatenate([grad_a, grad_b], axis=0)
    for axis, bit in (("y", 1), ("y", 2), ("z", 1), ("z", 2)):
        grads = butterfly(grads, axis, bit)
    grads = grads.reshape(2 * RANK * seg_local, SUB)
    bank_grad = jnp.dot(mixing.reshape(2 * RANK * seg_local, bank_rows).T, grads, precision=HIGH)
    bank_grad = bank_grad / math.sqrt(TOKENS)
    for axis in ("core", "pair", "section"):
        bank_grad = butterfly(bank_grad, axis, 1)
    return (result[None], bank_grad)


def solution(mesh):
    fine = Mesh(
        mesh.devices.reshape(2, RING, RING, 2, 2), ("section", "z", "y", "pair", "core")
    )
    rows, columns = ("z", "y"), ("pair", "core")
    return jax.shard_map(
        shards,
        mesh=fine,
        in_specs=(
            P("section", rows, columns),
            P("section", rows, columns),
            P("section", columns),
            P("section", rows, columns),
            P(),
            P("section", None, None, None),
            P("section", None, None, None),
            P(rows, columns),
        ),
        out_specs=(P("section", rows, columns), P()),
        check_vma=False,
    )
```

```python
import functools
import math

import jax
import jax.numpy as jnp
from jax import lax
from jax.experimental import pallas as pl
from jax.experimental.pallas import tpu as pltpu
from jax.sharding import Mesh, PartitionSpec as P

MODEL_WIDTH = 8192
RANK = 4
SUB = 256
TOKENS = 4096
RING = 4
LANES = 128

epsilon = 1e-06
HIGH = lax.Precision.HIGHEST
F32 = jnp.float32
BF16 = jnp.bfloat16
ANY = pl.BlockSpec(memory_space=pl.ANY)
SMEM = pl.BlockSpec(memory_space=pltpu.SMEM)
VMEM = pl.BlockSpec(memory_space=pltpu.VMEM)
HBM = pl.BlockSpec(memory_space=pltpu.HBM)
BIG = 48 * 1024 * 1024
LIGHT = pl.CostEstimate(flops=0, bytes_accessed=2 ** 20, transcendentals=0)


def ring_route(distance, sections=(0, 1)):
    return [(s * RING + i, s * RING + (i + distance) % RING) for s in sections for i in range(RING)]


def ring_move(block, axis, distance, sections=(0, 1)):
    return lax.ppermute(block, ("section", axis), ring_route(distance, sections))


def swap(block, axis, sections=(0, 1)):
    pairs = [(s * 2 + i, s * 2 + 1 - i) for s in sections for i in range(2)]
    return lax.ppermute(block, ("section", axis), pairs)


def after(value, earlier):
    return lax.optimization_barrier((value, earlier))[0]


def in_order(kernel, operands, extra):
    return lambda *refs: kernel(*refs[:operands], *refs[operands + extra:])


def compose(index_layer, weight_layer, rows):
    columns = lax.broadcasted_iota(jnp.int32, (1, 1, 1, 1, rows), 4)
    onehot = (index_layer[..., None] == columns).astype(F32)
    return jnp.sum(onehot * weight_layer[..., None], axis=3)


def two_halves(value):
    high = value.astype(BF16)
    return jnp.concatenate([high, (value - high.astype(F32)).astype(BF16)], axis=0)


def activation_gradient(incoming_ref, preact_ref):
    value = preact_ref[...].astype(F32)
    sig = jax.nn.sigmoid(value)
    slope = sig * (1.0 + value * (1.0 - sig))
    return (incoming_ref[...].astype(F32) * slope).astype(BF16)


def dz_kernel(incoming_ref, preact_ref, b_ref, dz_ref, mixed_ref):
    dz = activation_gradient(incoming_ref, preact_ref)
    dz_ref[...] = dz
    both = lax.dot_general(b_ref[...], dz, (((1,), (1,)), ((), ())), preferred_element_type=F32)
    mixed_ref[...] = both[:RANK] + both[RANK:]


def first_kernel(where_ref, incoming_ref, preact_ref, weight_ref, out_ref):
    @pl.when(where_ref[3] == 1)
    def _():
        out_ref[:incoming_ref.shape[0]] = activation_gradient(incoming_ref, preact_ref)

    @pl.when(where_ref[3] == 0)
    def _():
        out_ref[...] = weight_ref[...]


def make_first(where, incoming, preact, weight):
    return pl.pallas_call(
        first_kernel,
        in_specs=[SMEM, VMEM, VMEM, VMEM],
        out_specs=VMEM,
        out_shape=jax.ShapeDtypeStruct(weight.shape, BF16),
        compiler_params=pltpu.CompilerParams(vmem_limit_bytes=BIG),
        cost_estimate=LIGHT,
    )(where, incoming, preact, weight)


def join_kernel(wanted, parts, where_ref, *refs):
    sources, out_ref, sem = refs[:len(parts)], refs[-2], refs[-1]

    def run():
        start = 0
        copies = []
        for i, (first, rows) in enumerate(parts):
            source = sources[i].at[pl.ds(first, rows)]
            copies.append(pltpu.make_async_copy(source, out_ref.at[pl.ds(start, rows)], sem.at[i]))
            start += rows
        for copy in copies:
            copy.start()
        for copy in copies:
            copy.wait()

    if wanted is None:
        run()
    else:
        pl.when(where_ref[3] == wanted)(run)


def join(where, wanted, arrays, parts, *earlier):
    rows = sum(count for _, count in parts)
    return pl.pallas_call(
        in_order(functools.partial(join_kernel, wanted, parts), 1 + len(arrays), len(earlier)),
        in_specs=[SMEM] + [ANY] * (len(arrays) + len(earlier)),
        out_specs=VMEM,
        out_shape=jax.ShapeDtypeStruct((rows, arrays[0].shape[1]), BF16),
        scratch_shapes=[pltpu.SemaphoreType.DMA((len(arrays),))],
        compiler_params=pltpu.CompilerParams(vmem_limit_bytes=BIG),
        cost_estimate=LIGHT,
    )(where, *arrays, *earlier)


def gather_ring(where, block, axis, sections=(0, 1), earlier=()):
    half = block.shape[0] // 2
    wanted = None if len(sections) == 2 else sections[0]
    after = ring_move(block, axis, -1, sections)
    before = ring_move(block, axis, 1, sections)
    far_low = ring_move(join(where, wanted, (after,), ((0, half),), *earlier), axis, -1, sections)
    far_high = ring_move(join(where, wanted, (before,), ((half, half),), *earlier), axis, 1, sections)
    return block, after, far_low, far_high, before


def make_dz(incoming, preact, b_both, c, *earlier):
    rows, width = incoming.shape
    return pl.pallas_call(
        in_order(dz_kernel, 3, len(earlier)),
        grid=(1,),
        in_specs=[
            pl.BlockSpec((rows, width), lambda i: (0, 0)),
            pl.BlockSpec((rows, width), lambda i: (c, 0)),
            pl.BlockSpec((2 * RANK, width), lambda i: (0, 0)),
        ]
        + [ANY] * len(earlier),
        out_specs=[
            pl.BlockSpec((rows, width), lambda i: (0, 0)),
            pl.BlockSpec((RANK, rows), lambda i: (0, 0)),
        ],
        out_shape=[
            jax.ShapeDtypeStruct((rows, width), BF16),
            jax.ShapeDtypeStruct((RANK, rows), F32),
        ],
        compiler_params=pltpu.CompilerParams(vmem_limit_bytes=BIG),
        cost_estimate=LIGHT,
    )(incoming, preact, b_both, *earlier)


def top_product_kernel(rows, where_ref, *refs):
    dz_refs, w_refs = refs[:4], refs[4:9]
    keep_ref, send_ref, dz_all, w_all, dz_sem, w_sem = refs[9:]

    @pl.when(where_ref[3] == 1)
    def _():
        copies = [
            pltpu.make_async_copy(ref.at[pl.ds(0, rows)], dz_all.at[pl.ds(i * rows, rows)], dz_sem.at[i])
            for i, ref in enumerate(dz_refs)
        ]
        for copy in copies:
            copy.start()
        own, after, far_low, far_high, before = w_refs
        half = far_low.shape[0]
        pltpu.make_async_copy(own, w_all.at[0], w_sem.at[0]).start()
        pltpu.make_async_copy(after, w_all.at[1], w_sem.at[1]).start()
        pltpu.make_async_copy(far_low, w_all.at[2, pl.ds(0, half)], w_sem.at[2]).start()
        pltpu.make_async_copy(far_high, w_all.at[2, pl.ds(half, half)], w_sem.at[2]).start()
        pltpu.make_async_copy(before, w_all.at[3], w_sem.at[3]).start()
        for copy in copies:
            copy.wait()
        z, place = where_ref[0], where_ref[1]

        @pl.loop(0, RING)
        def _(i):
            pltpu.make_async_copy(own, w_all.at[i], w_sem.at[i]).wait()
            value = lax.dot_general(
                dz_all[...], w_all[i], (((1,), (1,)), ((), ())), preferred_element_type=F32
            ).astype(BF16)
            target = lax.rem(z + i, RING)
            own_core = lax.rem(target, 2) == lax.rem(place, 2)
            far = jnp.where(target // 2 == place // 2, 0, 1)

            @pl.when(own_core)
            def _():
                keep_ref[far] = value

            @pl.when(jnp.logical_not(own_core))
            def _():
                send_ref[far] = value


def top_product(where, rows, dz_pieces, w_pieces, *earlier):
    wide, width = w_pieces[0].shape
    return pl.pallas_call(
        in_order(functools.partial(top_product_kernel, rows), 10, len(earlier)),
        in_specs=[SMEM] + [HBM] * 9 + [ANY] * len(earlier),
        out_specs=[VMEM, VMEM],
        out_shape=[jax.ShapeDtypeStruct((2, RING * rows, wide), BF16)] * 2,
        scratch_shapes=[
            pltpu.VMEM((RING * rows, width), BF16),
            pltpu.VMEM((RING, wide, width), BF16),
            pltpu.SemaphoreType.DMA((4,)),
            pltpu.SemaphoreType.DMA((RING,)),
        ],
        compiler_params=pltpu.CompilerParams(vmem_limit_bytes=BIG),
        cost_estimate=pl.CostEstimate(
            flops=2 * RING * RING * rows * wide * width, bytes_accessed=2 ** 24, transcendentals=0
        ),
    )(where, *dz_pieces, *w_pieces, *earlier)


def low_plan(shard, wide):
    copies, blocks = [], []

    def take(array, row, rows, *names):
        at = sum(rows for *_, rows in copies)
        copies.append((array, row, at, rows))
        blocks.extend(names)

    for base, step in ((0, lambda d, h: (d, 0, h)), (4, lambda d, h: (0, d, h))):
        if base == 0:
            take(0, 0, shard, step(0, 0), step(0, 1))
        take(base + 1, 0, shard, step(1, 0), step(1, 1))
        take(base + 2, 0, wide, step(2, 0))
        take(base + 3, 0, wide, step(2, 1))
        take(base + 4, 0, shard, step(3, 0), step(3, 1))
    corner, y_pair, z_pair = 9, {1: 10, 3: 11}, {1: 12, 3: 13}
    take(corner, 0, shard, (2, 2, 0), (2, 2, 1))
    for d in (1, 3):
        take(y_pair[d], 0, shard, (2, d, 0), (2, d, 1))
        take(z_pair[d], 0, shard, (d, 2, 0), (d, 2, 1))
    slim, rest = wide // 2, shard - wide // 2
    for i, d in enumerate((1, 3)):
        for j, e in enumerate((1, 3)):
            take(y_pair[e], shard + i * slim, slim)
            take(z_pair[d], shard + j * rest, rest, (d, e, 0), (d, e, 1))
    return copies, blocks


def low_product_kernel(plan, where_ref, table_ref, dz_ref, *refs):
    count = len(refs) - 4
    w_refs = refs[:count]
    keep_ref, send_ref, w_all, sem = refs[count:]
    steps, deep = w_all.shape[0], w_all.shape[1]
    wide = deep // 2

    @pl.when(where_ref[3] == 0)
    def _():
        for array, row, at, rows in plan:
            while rows:
                part = min(rows, deep - at % deep)
                pltpu.make_async_copy(
                    w_refs[array].at[pl.ds(row, part)],
                    w_all.at[at // deep, pl.ds(at % deep, part)],
                    sem.at[at // deep],
                ).start()
                row, at, rows = row + part, at + part, rows - part

        @pl.loop(0, steps)
        def _(step):
            pltpu.make_async_copy(w_refs[0], w_all.at[step], sem.at[step]).wait()
            value = lax.dot_general(
                dz_ref[...], w_all[step], (((1,), (1,)), ((), ())), preferred_element_type=F32
            ).astype(BF16)
            for k in range(2):
                entry = table_ref[2 * step + k]
                columns = pl.ds(pl.multiple_of(lax.rem(entry, 2 * RING) * wide, wide), wide)
                far = lax.rem(entry // (2 * RING), 2)
                block = value[:, k * wide:(k + 1) * wide]

                @pl.when(entry < 4 * RING)
                def _():
                    keep_ref[far, :, columns] = block

                @pl.when(entry >= 4 * RING)
                def _():
                    send_ref[far, :, columns] = block


def low_product(where, z, y, place, dz, w_pieces, *earlier):
    rows, width = dz.shape
    shard = w_pieces[0].shape[0]
    wide = shard // 2
    copies, blocks = low_plan(shard, wide)
    steps = [jnp.array(column, jnp.int32) for column in zip(*blocks)]
    target = (z + steps[0]) % RING
    column = (y + steps[1]) % RING * 2 + steps[2]
    other_core = (target % 2 != place % 2).astype(jnp.int32)
    other_pair = (target // 2 != place // 2).astype(jnp.int32)
    table = (other_core * 2 + other_pair) * 2 * RING + column
    return pl.pallas_call(
        in_order(functools.partial(low_product_kernel, copies), 3 + len(w_pieces), len(earlier)),
        in_specs=[SMEM, SMEM, VMEM] + [HBM] * len(w_pieces) + [ANY] * len(earlier),
        out_specs=[VMEM, VMEM],
        out_shape=[jax.ShapeDtypeStruct((2, rows, 2 * RING * wide), BF16)] * 2,
        scratch_shapes=[
            pltpu.VMEM((RING * RING, shard, width), BF16),
            pltpu.SemaphoreType.DMA((RING * RING,)),
        ],
        compiler_params=pltpu.CompilerParams(vmem_limit_bytes=BIG),
        cost_estimate=pl.CostEstimate(
            flops=16 * RING * rows * wide * width, bytes_accessed=2 ** 25, transcendentals=0
        ),
    )(where, table, dz, *w_pieces, *earlier)


def add_kernel(keep_ref, got_ref, out_ref):
    out_ref[...] = (keep_ref[0].astype(F32) + got_ref[0].astype(F32)).astype(BF16)


def add_theirs(keep, got):
    _, rows, wide = keep.shape
    spec = pl.BlockSpec((1, rows, wide), lambda i: (1, 0, 0))
    return pl.pallas_call(
        add_kernel,
        grid=(1,),
        in_specs=[spec, spec],
        out_specs=pl.BlockSpec((rows, wide), lambda i: (0, 0)),
        out_shape=jax.ShapeDtypeStruct((rows, wide), BF16),
        compiler_params=pltpu.CompilerParams(vmem_limit_bytes=BIG),
        cost_estimate=LIGHT,
    )(keep, got)


def total_kernel(keep_ref, got_ref, other_ref, *out_refs):
    rows = out_refs[0].shape[0]
    for i, ref in enumerate(out_refs):
        part = pl.ds(i * rows, rows)
        ref[...] = (
            keep_ref[0, part].astype(F32) + got_ref[0, part].astype(F32) + other_ref[part].astype(F32)
        ).astype(BF16)


def add_mine(keep, got, other):
    _, rows, wide = keep.shape
    spec = pl.BlockSpec((1, rows, wide), lambda i: (0, 0, 0))
    return pl.pallas_call(
        total_kernel,
        grid=(1,),
        in_specs=[spec, spec, pl.BlockSpec((rows, wide), lambda i: (0, 0))],
        out_specs=[pl.BlockSpec((rows // RING, wide), lambda i: (0, 0))] * RING,
        out_shape=[jax.ShapeDtypeStruct((rows // RING, wide), BF16)] * RING,
        compiler_params=pltpu.CompilerParams(vmem_limit_bytes=BIG),
        cost_estimate=LIGHT,
    )(keep, got, other)


def as_row(column):
    square = jnp.broadcast_to(column, (column.shape[0], LANES))
    return jnp.transpose(square)[:8]


def as_column(row):
    square = jnp.concatenate([row] * (LANES // 8), axis=0)
    return jnp.transpose(square)[:, :1]


def scaled_kernel(where_ref, own, after, far, before, mixed_ref, a_ref, gain_ref, hidden_ref, scale_ref, scaled_ref, inner_ref):
    wide = own.shape[1]
    mixed = mixed_ref[...]
    inner = jnp.zeros((own.shape[0], 1), F32)
    for r, piece in enumerate((own, after, far, before)):
        at = pl.ds(pl.multiple_of(lax.rem(where_ref[2] + r, RING) * wide, wide), wide)
        low_rank = lax.dot_general(
            mixed, a_ref[:, at], (((0,), (0,)), ((), ())), precision=HIGH, preferred_element_type=F32
        )
        scaled = gain_ref[:, at] * (piece[...].astype(F32) + low_rank)
        scaled_ref[:, at] = scaled
        inner = inner + jnp.sum(scaled * hidden_ref[:, at].astype(F32), axis=1, keepdims=True)
    inner_ref[...] = as_row(inner * scale_ref[...])


def make_scaled(where, pieces, mixed, a_local, gain, hidden, scale):
    rows, width = hidden.shape
    return pl.pallas_call(
        scaled_kernel,
        in_specs=[SMEM] + [VMEM] * 9,
        out_specs=[VMEM, VMEM],
        out_shape=[jax.ShapeDtypeStruct((rows, width), F32), jax.ShapeDtypeStruct((8, rows), F32)],
        compiler_params=pltpu.CompilerParams(vmem_limit_bytes=BIG),
        cost_estimate=LIGHT,
    )(where, *pieces, mixed, a_local, gain, hidden, scale)


def low_scaled_kernel(keep_ref, got_ref, other_ref, mixed_ref, a_ref, gain_ref, hidden_ref, scale_ref, scaled_ref, inner_ref):
    low_rank = lax.dot_general(
        mixed_ref[...], a_ref[...], (((0,), (0,)), ((), ())), precision=HIGH, preferred_element_type=F32
    )
    total = keep_ref[0].astype(F32) + got_ref[0].astype(F32) + other_ref[...].astype(F32)
    scaled = gain_ref[...] * (total + low_rank)
    scaled_ref[...] = scaled
    inner = jnp.sum(scaled * hidden_ref[...].astype(F32), axis=1, keepdims=True)
    inner_ref[...] = as_row(inner * scale_ref[...])


def low_scaled(keep, got, other, mixed, a_local, gain, hidden, scale):
    rows, width = hidden.shape
    whole = lambda shape: pl.BlockSpec(shape, lambda i: (0, 0))
    mine = pl.BlockSpec((1, rows, width), lambda i: (0, 0, 0))
    return pl.pallas_call(
        low_scaled_kernel,
        grid=(1,),
        in_specs=[
            mine, mine, whole((rows, width)), whole((RANK, rows)), whole((RANK, width)),
            whole((1, width)), whole((rows, width)), whole((rows, 1)),
        ],
        out_specs=[whole((rows, width)), whole((8, rows))],
        out_shape=[jax.ShapeDtypeStruct((rows, width), F32), jax.ShapeDtypeStruct((8, rows), F32)],
        compiler_params=pltpu.CompilerParams(vmem_limit_bytes=BIG),
        cost_estimate=LIGHT,
    )(keep, got, other, mixed, a_local, gain, hidden, scale)


def hidden_gradient(scaled_ref, inner_ref, hidden_ref, scale_ref, incoming_ref):
    scale = scale_ref[...]
    pull = as_column(inner_ref[...]) * scale / MODEL_WIDTH
    return (
        incoming_ref[...].astype(F32)
        + scale * (scaled_ref[...] - hidden_ref[...].astype(F32) * pull)
    ).astype(BF16)


def top_kernel(scaled_ref, inner_ref, hidden_ref, scale_ref, incoming_ref, out_ref):
    out_ref[...] = hidden_gradient(scaled_ref, inner_ref, hidden_ref, scale_ref, incoming_ref)


def low_kernel(where_ref, scaled_ref, inner_ref, hidden_ref, scale_ref, incoming_ref, top_ref, *rest):
    grad = hidden_gradient(scaled_ref, inner_ref, hidden_ref, scale_ref, incoming_ref)
    rest[-1][...] = jnp.where(where_ref[3] == 1, top_ref[...], grad)


def finish_specs(rows, width, c):
    whole = lambda shape: pl.BlockSpec(shape, lambda i: (0, 0))
    return [
        whole((rows, width)),
        whole((8, rows)),
        pl.BlockSpec((rows, width), lambda i: (c, 0)),
        pl.BlockSpec((rows, 1), lambda i: (c, 0)),
    ]


def finish_top(scaled, inner, hidden, scale, grad_top, c):
    rows, width = scaled.shape
    return pl.pallas_call(
        top_kernel,
        grid=(1,),
        in_specs=finish_specs(rows, width, c) + [pl.BlockSpec((rows, width), lambda i: (c, 0))],
        out_specs=pl.BlockSpec((rows, width), lambda i: (0, 0)),
        out_shape=jax.ShapeDtypeStruct((rows, width), BF16),
        compiler_params=pltpu.CompilerParams(vmem_limit_bytes=BIG),
        cost_estimate=LIGHT,
    )(scaled, inner, hidden, scale, grad_top)


def finish_low(where, scaled, inner, hidden, scale, incoming, top):
    rows, width = scaled.shape
    block = pl.BlockSpec((rows, width), lambda i: (0, 0))
    return pl.pallas_call(
        low_kernel,
        grid=(1,),
        in_specs=[SMEM] + finish_specs(rows, width, 0) + [block, block],
        out_specs=block,
        out_shape=jax.ShapeDtypeStruct((rows, width), BF16),
        compiler_params=pltpu.CompilerParams(vmem_limit_bytes=BIG),
        cost_estimate=LIGHT,
    )(where, scaled, inner, hidden, scale, incoming, top)


def grads_kernel(where_ref, hidden_ref, scale_ref, gain_ref, projected_ref, *refs):
    out_ref = refs[-1]
    top = where_ref[3] == 1
    count = (len(refs) - 2) // 3
    total_a, total_b = 0.0, 0.0
    for c in range(count):
        low_dz, top_mixed, low_mixed = [refs[1 + k * count + c] for k in range(3)]
        rows = pl.ds(c * low_dz.shape[0], low_dz.shape[0])
        dz = jnp.where(top, refs[0][rows], low_dz[...])
        mixed = jnp.where(top, top_mixed[...], low_mixed[...])
        x = (hidden_ref[rows].astype(F32) * scale_ref[rows] * gain_ref[...]).astype(BF16)
        projected = projected_ref[:, rows]

        def both(left, right):
            value = lax.dot_general(
                two_halves(left), right, (((1,), (0,)), ((), ())), preferred_element_type=F32
            )
            return value[:RANK] + value[RANK:]

        total_a = total_a + both(mixed, x)
        total_b = total_b + both(projected, dz)
    out_ref[...] = jnp.concatenate([total_a, total_b], axis=0)


def make_grads(where, hidden, scale, gain, projected, lists, *earlier):
    arrays = [array for arrays in lists for array in arrays]
    return pl.pallas_call(
        in_order(grads_kernel, 5 + len(arrays), len(earlier)),
        in_specs=[SMEM] + [VMEM] * (4 + len(arrays)) + [ANY] * len(earlier),
        out_specs=VMEM,
        out_shape=jax.ShapeDtypeStruct((2 * RANK, hidden.shape[1]), F32),
        compiler_params=pltpu.CompilerParams(vmem_limit_bytes=BIG),
        cost_estimate=LIGHT,
    )(where, hidden, scale, gain, projected, *arrays, *earlier)


def ring_total(value, moved):
    after, far, before = moved
    return (value[...] + far[...]) + (after[...] + before[...])


def ring_kernel(value, after, far, before, out_ref):
    out_ref[...] = ring_total(value, (after, far, before))


def bank_kernel(mixing_ref, value, after, far, before, out_ref):
    total = ring_total(value, (after, far, before))
    count = total.shape[1] // SUB
    pieces = jnp.concatenate([total[:, j * SUB:(j + 1) * SUB] for j in range(count)], axis=0)
    out_ref[...] = lax.dot_general(
        mixing_ref[...], pieces, (((0,), (0,)), ((), ())), precision=HIGH, preferred_element_type=F32
    )


def round_kernel(factor, left, right, out_ref):
    out_ref[...] = ((left[...].astype(F32) + right[...].astype(F32)) * factor).astype(out_ref.dtype)


def small_call(kernel, out, operands, *earlier):
    return pl.pallas_call(
        in_order(kernel, len(operands), len(earlier)),
        in_specs=[VMEM] * len(operands) + [ANY] * len(earlier),
        out_specs=VMEM,
        out_shape=out,
        compiler_params=pltpu.CompilerParams(vmem_limit_bytes=BIG),
        cost_estimate=LIGHT,
    )(*operands, *earlier)


def ring_moves(value, axis):
    return [ring_move(value, axis, d) for d in (-1, 2, 1)]


def shards(hidden_in, preact, norm_gain, weight, bank, mix_index, mix_weight, grad_top):
    section = lax.axis_index("section")
    z, y = lax.axis_index("z"), lax.axis_index("y")
    place = lax.axis_index("pair") * 2 + lax.axis_index("core")
    where = jnp.stack([z, place, y, section]).astype(jnp.int32)
    tensor = ("pair", "core")
    bank_rows = bank.shape[0]

    tokens, local_width = grad_top.shape
    seg_local = local_width // SUB
    seg_row = MODEL_WIDTH // SUB
    own_weight = weight[0]
    shard = own_weight.shape[0]
    half = shard // 2

    first = make_first(where, grad_top, preact[0], own_weight)
    hidden, preact = hidden_in[0], preact[0]

    def local_pieces(array):
        array = array.reshape(2, RANK, seg_row, 2)
        return lax.dynamic_slice_in_dim(array, place * seg_local, seg_local, 2)

    mixing = compose(local_pieces(mix_index[0]), local_pieces(mix_weight[0]), bank_rows)
    mixing = mixing.reshape(2, RANK * seg_local, bank_rows)
    factors = jnp.einsum("fnb,bs->fns", mixing, bank, precision=HIGH)
    a_local = factors[0].reshape(RANK, local_width)
    b_both = two_halves(factors[1].reshape(RANK, local_width))

    hidden_f = hidden.astype(F32)
    sums = lax.psum(
        jnp.concatenate(
            [
                jnp.sum(hidden_f * hidden_f, axis=1)[None],
                jnp.dot(a_local, (hidden_f * norm_gain).T, precision=HIGH),
                jnp.dot(factors[1].reshape(RANK, local_width), first[:tokens].astype(F32).T, precision=HIGH),
            ],
            axis=0,
        ),
        tensor,
    )
    scale_row = lax.rsqrt(sums[:1] / MODEL_WIDTH + epsilon)
    projected = sums[1:1 + RANK] * scale_row
    scale = scale_row.reshape(tokens, 1)
    top_mixed = sums[1 + RANK:]

    z_ring = gather_ring(where, own_weight, "z", earlier=(scale,))
    y_ring = gather_ring(where, first, "y", earlier=(scale,))

    dz_pieces = (y_ring[0], y_ring[1], y_ring[2], y_ring[4])
    keep, send = top_product(where, tokens, dz_pieces, z_ring, y_ring[3])
    got = swap(send, "core", (1,))
    theirs = add_theirs(keep, got)
    other = swap(theirs, "pair", (1,))

    own, to_after, to_far, to_before = add_mine(keep, got, other)
    from_before = ring_move(to_after, "y", 1, (1,))
    from_far = ring_move(to_far, "y", 2, (1,))
    from_after = ring_move(to_before, "y", -1, (1,))

    _, z_after, z_far_low, z_far_high, z_before = z_ring
    _, y_after, y_far_low, y_far_high, y_before = y_ring
    slim, rest = half // 2, shard - half // 2
    corner = join(where, 0, (z_far_low, z_far_high), ((0, half), (0, half)), own)
    corner = ring_move(corner, "y", 2, (0,))
    along_z = join(
        where, None, (y_far_low, y_far_high, y_after, y_before),
        ((0, half), (0, half), (slim, rest), (slim, rest)), own,
    )
    z_pair = (ring_move(along_z, "z", -1), ring_move(along_z, "z", 1))
    along_y = join(
        where, 0, (z_far_low, z_far_high, z_after, z_before),
        ((0, half), (0, half), (0, slim), (0, slim)), corner,
    )
    y_pair = (ring_move(along_y, "y", -1, (0,)), ring_move(along_y, "y", 1, (0,)))
    w_pieces = (*z_ring, *y_ring[1:], corner, *y_pair, *z_pair)

    pieces = (own, from_after, from_far, from_before)
    scaled, inner = make_scaled(where, pieces, top_mixed, a_local, norm_gain, hidden, scale)
    top_grad = finish_top(scaled, lax.psum(inner, tensor), hidden, scale, grad_top, 0)
    low_in = lax.ppermute(top_grad, "section", [(1, 0)])

    low_dz, part = make_dz(low_in, preact, b_both, 0)
    low_mixed = lax.psum(part, tensor)
    keep, send = low_product(where, z, y, place, low_dz, w_pieces, low_mixed)
    got = swap(send, "core", (0,))
    theirs = add_theirs(keep, got)
    other = swap(theirs, "pair", (0,))
    scaled, inner = low_scaled(keep, got, other, low_mixed, a_local, norm_gain, hidden, scale)
    result = finish_low(where, scaled, lax.psum(inner, tensor), hidden, scale, low_in, top_grad)

    grads = make_grads(
        where, hidden, scale, norm_gain, projected, ([first], [low_dz], [top_mixed], [low_mixed])
    )
    over_y = ring_moves(grads, "y")
    grads = small_call(ring_kernel, jax.ShapeDtypeStruct(grads.shape, F32), (grads, *over_y), send)
    over_z = ring_moves(grads, "z")
    flat = mixing.reshape(2, RANK, seg_local, bank_rows).transpose(2, 0, 1, 3)
    flat = flat.reshape(2 * RANK * seg_local, bank_rows)
    bank_shape = (bank_rows, SUB)
    share = small_call(bank_kernel, jax.ShapeDtypeStruct(bank_shape, F32), (flat, grads, *over_z), theirs)
    core_share = swap(share, "core")
    half_shape = jax.ShapeDtypeStruct(bank_shape, BF16)
    add_up = functools.partial(round_kernel, 1.0 / math.sqrt(TOKENS))
    share = small_call(add_up, half_shape, (share, core_share))
    pair_share = swap(share, "pair")
    add_up = functools.partial(round_kernel, 1.0)
    share = small_call(add_up, half_shape, (share, pair_share))
    other_share = lax.ppermute(share, "section", [(0, 1), (1, 0)])
    bank_grad = small_call(add_up, jax.ShapeDtypeStruct(bank_shape, F32), (share, other_share), result)
    return (result[None], bank_grad)


def solution(mesh):
    fine = Mesh(
        mesh.devices.reshape(2, RING, RING, 2, 2), ("section", "z", "y", "pair", "core")
    )
    rows, columns = ("z", "y"), ("pair", "core")
    return jax.shard_map(
        shards,
        mesh=fine,
        in_specs=(
            P("section", rows, columns),
            P("section", rows, columns),
            P("section", columns),
            P("section", rows, columns),
            P(),
            P("section", None, None, None),
            P("section", None, None, None),
            P(rows, columns),
        ),
        out_specs=(P("section", rows, columns), P()),
        check_vma=False,
    )
```

```python
import functools
import math

import jax
import jax.numpy as jnp
from jax import lax
from jax.experimental import pallas as pl
from jax.experimental.pallas import tpu as pltpu
from jax.sharding import Mesh, PartitionSpec as P

MODEL_WIDTH = 8192
RANK = 4
SUB = 256
TOKENS = 4096
RING = 4
LANES = 128

epsilon = 1e-06
HIGH = lax.Precision.HIGHEST
F32 = jnp.float32
BF16 = jnp.bfloat16
ANY = pl.BlockSpec(memory_space=pl.ANY)
SMEM = pl.BlockSpec(memory_space=pltpu.SMEM)
VMEM = pl.BlockSpec(memory_space=pltpu.VMEM)
HBM = pl.BlockSpec(memory_space=pltpu.HBM)
BIG = 48 * 1024 * 1024
LIGHT = pl.CostEstimate(flops=0, bytes_accessed=2 ** 20, transcendentals=0)


def ring_route(distance, sections=(0, 1)):
    return [(s * RING + i, s * RING + (i + distance) % RING) for s in sections for i in range(RING)]


def ring_move(block, axis, distance, sections=(0, 1)):
    return lax.ppermute(block, ("section", axis), ring_route(distance, sections))


def swap(block, axis, sections=(0, 1)):
    pairs = [(s * 2 + i, s * 2 + 1 - i) for s in sections for i in range(2)]
    return lax.ppermute(block, ("section", axis), pairs)


def after(value, earlier):
    return lax.optimization_barrier((value, earlier))[0]


def in_order(kernel, operands, extra):
    return lambda *refs: kernel(*refs[:operands], *refs[operands + extra:])


def compose(index_layer, weight_layer, rows):
    columns = lax.broadcasted_iota(jnp.int32, (1, 1, 1, 1, rows), 4)
    onehot = (index_layer[..., None] == columns).astype(F32)
    return jnp.sum(onehot * weight_layer[..., None], axis=3)


def two_halves(value):
    high = value.astype(BF16)
    return jnp.concatenate([high, (value - high.astype(F32)).astype(BF16)], axis=0)


def activation_gradient(incoming_ref, preact_ref):
    value = preact_ref[...].astype(F32)
    sig = jax.nn.sigmoid(value)
    slope = sig * (1.0 + value * (1.0 - sig))
    return (incoming_ref[...].astype(F32) * slope).astype(BF16)


def dz_kernel(incoming_ref, preact_ref, b_ref, dz_ref, mixed_ref):
    dz = activation_gradient(incoming_ref, preact_ref)
    dz_ref[...] = dz
    both = lax.dot_general(b_ref[...], dz, (((1,), (1,)), ((), ())), preferred_element_type=F32)
    mixed_ref[...] = both[:RANK] + both[RANK:]


def first_kernel(where_ref, incoming_ref, preact_ref, weight_ref, out_ref, incoming, preact, sem):
    def fetch(*pairs):
        copies = [pltpu.make_async_copy(*pair, sem.at[i]) for i, pair in enumerate(pairs)]
        for copy in copies:
            copy.start()
        for copy in copies:
            copy.wait()

    @pl.when(where_ref[3] == 1)
    def _():
        fetch((incoming_ref, incoming), (preact_ref, preact))
        out_ref[:incoming.shape[0]] = activation_gradient(incoming, preact)

    @pl.when(where_ref[3] == 0)
    def _():
        fetch((weight_ref, out_ref))


def make_first(where, incoming, preact, weight):
    return pl.pallas_call(
        first_kernel,
        in_specs=[SMEM, HBM, HBM, HBM],
        out_specs=VMEM,
        out_shape=jax.ShapeDtypeStruct(weight.shape, BF16),
        scratch_shapes=[
            pltpu.VMEM(incoming.shape, BF16),
            pltpu.VMEM(incoming.shape, BF16),
            pltpu.SemaphoreType.DMA((2,)),
        ],
        compiler_params=pltpu.CompilerParams(vmem_limit_bytes=BIG),
        cost_estimate=LIGHT,
    )(where, incoming, preact, weight)


def join_kernel(wanted, parts, where_ref, *refs):
    sources, out_ref, sem = refs[:len(parts)], refs[-2], refs[-1]

    def run():
        start = 0
        copies = []
        for i, (first, rows) in enumerate(parts):
            source = sources[i].at[pl.ds(first, rows)]
            copies.append(pltpu.make_async_copy(source, out_ref.at[pl.ds(start, rows)], sem.at[i]))
            start += rows
        for copy in copies:
            copy.start()
        for copy in copies:
            copy.wait()

    if wanted is None:
        run()
    else:
        pl.when(where_ref[3] == wanted)(run)


def join(where, wanted, arrays, parts, *earlier):
    rows = sum(count for _, count in parts)
    return pl.pallas_call(
        in_order(functools.partial(join_kernel, wanted, parts), 1 + len(arrays), len(earlier)),
        in_specs=[SMEM] + [ANY] * (len(arrays) + len(earlier)),
        out_specs=VMEM,
        out_shape=jax.ShapeDtypeStruct((rows, arrays[0].shape[1]), BF16),
        scratch_shapes=[pltpu.SemaphoreType.DMA((len(arrays),))],
        compiler_params=pltpu.CompilerParams(vmem_limit_bytes=BIG),
        cost_estimate=LIGHT,
    )(where, *arrays, *earlier)


def halves_kernel(after_ref, before_ref, low_ref, high_ref, sem):
    half = low_ref.shape[0]
    low = pltpu.make_async_copy(after_ref.at[pl.ds(0, half)], low_ref, sem.at[0])
    high = pltpu.make_async_copy(before_ref.at[pl.ds(half, half)], high_ref, sem.at[1])
    low.start()
    high.start()
    low.wait()
    high.wait()


def gather_ring(block, axis, *earlier):
    rows, width = block.shape
    after = ring_move(block, axis, -1)
    before = ring_move(block, axis, 1)
    low, high = pl.pallas_call(
        in_order(halves_kernel, 2, len(earlier)),
        in_specs=[ANY, ANY] + [ANY] * len(earlier),
        out_specs=[VMEM, VMEM],
        out_shape=[jax.ShapeDtypeStruct((rows // 2, width), BF16)] * 2,
        scratch_shapes=[pltpu.SemaphoreType.DMA((2,))],
        compiler_params=pltpu.CompilerParams(vmem_limit_bytes=BIG),
        cost_estimate=LIGHT,
    )(after, before, *earlier)
    return block, after, ring_move(low, axis, -1), ring_move(high, axis, 1), before


def make_dz(incoming, preact, b_both, c, *earlier):
    rows, width = incoming.shape
    return pl.pallas_call(
        in_order(dz_kernel, 3, len(earlier)),
        grid=(1,),
        in_specs=[
            pl.BlockSpec((rows, width), lambda i: (0, 0)),
            pl.BlockSpec((rows, width), lambda i: (c, 0)),
            pl.BlockSpec((2 * RANK, width), lambda i: (0, 0)),
        ]
        + [ANY] * len(earlier),
        out_specs=[
            pl.BlockSpec((rows, width), lambda i: (0, 0)),
            pl.BlockSpec((RANK, rows), lambda i: (0, 0)),
        ],
        out_shape=[
            jax.ShapeDtypeStruct((rows, width), BF16),
            jax.ShapeDtypeStruct((RANK, rows), F32),
        ],
        compiler_params=pltpu.CompilerParams(vmem_limit_bytes=BIG),
        cost_estimate=LIGHT,
    )(incoming, preact, b_both, *earlier)


def top_product_kernel(rows, where_ref, *refs):
    dz_refs, w_refs = refs[:4], refs[4:9]
    mine_ref, theirs_ref, send_ref, dz_all, w_all, dz_sem, w_sem = refs[9:]

    @pl.when(where_ref[3] == 1)
    def _():
        copies = [
            pltpu.make_async_copy(ref.at[pl.ds(0, rows)], dz_all.at[pl.ds(i * rows, rows)], dz_sem.at[i])
            for i, ref in enumerate(dz_refs)
        ]
        for copy in copies:
            copy.start()
        own, after, far_low, far_high, before = w_refs
        half = far_low.shape[0]
        pltpu.make_async_copy(own, w_all.at[0], w_sem.at[0]).start()
        pltpu.make_async_copy(after, w_all.at[1], w_sem.at[1]).start()
        pltpu.make_async_copy(far_low, w_all.at[2, pl.ds(0, half)], w_sem.at[2]).start()
        pltpu.make_async_copy(far_high, w_all.at[2, pl.ds(half, half)], w_sem.at[2]).start()
        pltpu.make_async_copy(before, w_all.at[3], w_sem.at[3]).start()
        for copy in copies:
            copy.wait()
        z, place = where_ref[0], where_ref[1]

        @pl.loop(0, RING)
        def _(i):
            pltpu.make_async_copy(own, w_all.at[i], w_sem.at[i]).wait()
            value = lax.dot_general(
                dz_all[...], w_all[i], (((1,), (1,)), ((), ())), preferred_element_type=F32
            ).astype(BF16)
            target = lax.rem(z + i, RING)
            own_core = lax.rem(target, 2) == lax.rem(place, 2)
            far = jnp.where(target // 2 == place // 2, 0, 1)

            @pl.when(jnp.logical_and(own_core, far == 0))
            def _():
                mine_ref[...] = value

            @pl.when(jnp.logical_and(own_core, far == 1))
            def _():
                theirs_ref[...] = value

            @pl.when(jnp.logical_not(own_core))
            def _():
                send_ref[far] = value


def top_product(where, rows, dz_pieces, w_pieces, *earlier):
    wide, width = w_pieces[0].shape
    return pl.pallas_call(
        in_order(functools.partial(top_product_kernel, rows), 10, len(earlier)),
        in_specs=[SMEM] + [HBM] * 9 + [ANY] * len(earlier),
        out_specs=[VMEM, VMEM, VMEM],
        out_shape=[jax.ShapeDtypeStruct((RING * rows, wide), BF16)] * 2
        + [jax.ShapeDtypeStruct((2, RING * rows, wide), BF16)],
        scratch_shapes=[
            pltpu.VMEM((RING * rows, width), BF16),
            pltpu.VMEM((RING, wide, width), BF16),
            pltpu.SemaphoreType.DMA((4,)),
            pltpu.SemaphoreType.DMA((RING,)),
        ],
        compiler_params=pltpu.CompilerParams(vmem_limit_bytes=BIG),
        cost_estimate=pl.CostEstimate(
            flops=2 * RING * RING * rows * wide * width, bytes_accessed=2 ** 24, transcendentals=0
        ),
    )(where, *dz_pieces, *w_pieces, *earlier)


def low_plan(shard, wide):
    copies, blocks = [], []

    def take(array, row, rows, *names):
        at = sum(rows for *_, rows in copies)
        copies.append((array, row, at, rows))
        blocks.extend(names)

    for base, step in ((0, lambda d, h: (d, 0, h)), (4, lambda d, h: (0, d, h))):
        if base == 0:
            take(0, 0, shard, step(0, 0), step(0, 1))
        take(base + 1, 0, shard, step(1, 0), step(1, 1))
        take(base + 2, 0, wide, step(2, 0))
        take(base + 3, 0, wide, step(2, 1))
        take(base + 4, 0, shard, step(3, 0), step(3, 1))
    corner, y_pair, z_pair = 9, {1: 10, 3: 11}, {1: 12, 3: 13}
    take(corner, 0, shard, (2, 2, 0), (2, 2, 1))
    for d in (1, 3):
        take(y_pair[d], 0, shard, (2, d, 0), (2, d, 1))
        take(z_pair[d], 0, shard, (d, 2, 0), (d, 2, 1))
    slim, rest = wide // 2, shard - wide // 2
    for i, d in enumerate((1, 3)):
        for j, e in enumerate((1, 3)):
            take(y_pair[e], shard + i * slim, slim)
            take(z_pair[d], shard + j * rest, rest, (d, e, 0), (d, e, 1))
    return copies, blocks


def low_product_kernel(plan, where_ref, table_ref, dz_ref, *refs):
    count = len(refs) - 7
    w_refs = refs[:count]
    mine_ref, theirs_ref, send_ref, dz_all, w_all, dz_sem, sem = refs[count:]
    steps, deep = w_all.shape[0], w_all.shape[1]
    wide = deep // 2

    @pl.when(where_ref[3] == 0)
    def _():
        dz_copy = pltpu.make_async_copy(dz_ref, dz_all, dz_sem)
        dz_copy.start()
        for array, row, at, rows in plan:
            while rows:
                part = min(rows, deep - at % deep)
                pltpu.make_async_copy(
                    w_refs[array].at[pl.ds(row, part)],
                    w_all.at[at // deep, pl.ds(at % deep, part)],
                    sem.at[at // deep],
                ).start()
                row, at, rows = row + part, at + part, rows - part
        dz_copy.wait()

        @pl.loop(0, steps)
        def _(step):
            pltpu.make_async_copy(w_refs[0], w_all.at[step], sem.at[step]).wait()
            value = lax.dot_general(
                dz_all[...], w_all[step], (((1,), (1,)), ((), ())), preferred_element_type=F32
            ).astype(BF16)
            for k in range(2):
                entry = table_ref[2 * step + k]
                columns = pl.ds(pl.multiple_of(lax.rem(entry, 2 * RING) * wide, wide), wide)
                far = lax.rem(entry // (2 * RING), 2)
                block = value[:, k * wide:(k + 1) * wide]

                @pl.when(entry < 2 * RING)
                def _():
                    mine_ref[:, columns] = block

                @pl.when(jnp.logical_and(entry >= 2 * RING, entry < 4 * RING))
                def _():
                    theirs_ref[:, columns] = block

                @pl.when(entry >= 4 * RING)
                def _():
                    send_ref[far, :, columns] = block


def low_product(where, z, y, place, dz, w_pieces, *earlier):
    rows, width = dz.shape
    shard = w_pieces[0].shape[0]
    wide = shard // 2
    copies, blocks = low_plan(shard, wide)
    steps = [jnp.array(column, jnp.int32) for column in zip(*blocks)]
    target = (z + steps[0]) % RING
    column = (y + steps[1]) % RING * 2 + steps[2]
    other_core = (target % 2 != place % 2).astype(jnp.int32)
    other_pair = (target // 2 != place // 2).astype(jnp.int32)
    table = (other_core * 2 + other_pair) * 2 * RING + column
    return pl.pallas_call(
        in_order(functools.partial(low_product_kernel, copies), 3 + len(w_pieces), len(earlier)),
        in_specs=[SMEM, SMEM, HBM] + [HBM] * len(w_pieces) + [ANY] * len(earlier),
        out_specs=[VMEM, VMEM, VMEM],
        out_shape=[jax.ShapeDtypeStruct((rows, 2 * RING * wide), BF16)] * 2
        + [jax.ShapeDtypeStruct((2, rows, 2 * RING * wide), BF16)],
        scratch_shapes=[
            pltpu.VMEM((rows, width), BF16),
            pltpu.VMEM((RING * RING, shard, width), BF16),
            pltpu.SemaphoreType.DMA,
            pltpu.SemaphoreType.DMA((RING * RING,)),
        ],
        compiler_params=pltpu.CompilerParams(vmem_limit_bytes=BIG),
        cost_estimate=pl.CostEstimate(
            flops=16 * RING * rows * wide * width, bytes_accessed=2 ** 25, transcendentals=0
        ),
    )(where, table, dz, *w_pieces, *earlier)


def add_kernel(keep_ref, got_ref, out_ref):
    out_ref[...] = (keep_ref[...].astype(F32) + got_ref[0].astype(F32)).astype(BF16)


def add_theirs(keep, got):
    rows, wide = keep.shape
    whole = pl.BlockSpec((rows, wide), lambda i: (0, 0))
    return pl.pallas_call(
        add_kernel,
        grid=(1,),
        in_specs=[whole, pl.BlockSpec((1, rows, wide), lambda i: (1, 0, 0))],
        out_specs=whole,
        out_shape=jax.ShapeDtypeStruct((rows, wide), BF16),
        compiler_params=pltpu.CompilerParams(vmem_limit_bytes=BIG),
        cost_estimate=LIGHT,
    )(keep, got)


def total_kernel(keep_ref, got_ref, other_ref, *out_refs):
    rows = out_refs[0].shape[0]
    for i, ref in enumerate(out_refs):
        part = pl.ds(i * rows, rows)
        ref[...] = (
            keep_ref[part].astype(F32) + got_ref[0, part].astype(F32) + other_ref[part].astype(F32)
        ).astype(BF16)


def add_mine(keep, got, other, *earlier):
    rows, wide = keep.shape
    whole = pl.BlockSpec((rows, wide), lambda i: (0, 0))
    return pl.pallas_call(
        in_order(total_kernel, 3, len(earlier)),
        grid=(1,),
        in_specs=[whole, pl.BlockSpec((1, rows, wide), lambda i: (0, 0, 0)), whole] + [ANY] * len(earlier),
        out_specs=[pl.BlockSpec((rows // RING, wide), lambda i: (0, 0))] * RING,
        out_shape=[jax.ShapeDtypeStruct((rows // RING, wide), BF16)] * RING,
        compiler_params=pltpu.CompilerParams(vmem_limit_bytes=BIG),
        cost_estimate=LIGHT,
    )(keep, got, other, *earlier)


def as_row(column):
    square = jnp.broadcast_to(column, (column.shape[0], LANES))
    return jnp.transpose(square)[:8]


def as_column(row):
    square = jnp.concatenate([row] * (LANES // 8), axis=0)
    return jnp.transpose(square)[:, :1]


def scaled_kernel(where_ref, own, after, far, before, mixed_ref, a_ref, gain_ref, hidden_ref, scale_ref, scaled_ref, inner_ref):
    wide = own.shape[1]
    mixed = mixed_ref[...]
    inner = jnp.zeros((own.shape[0], 1), F32)
    for r, piece in enumerate((own, after, far, before)):
        at = pl.ds(pl.multiple_of(lax.rem(where_ref[2] + r, RING) * wide, wide), wide)
        low_rank = lax.dot_general(
            mixed, a_ref[:, at], (((0,), (0,)), ((), ())), precision=HIGH, preferred_element_type=F32
        )
        scaled = gain_ref[:, at] * (piece[...].astype(F32) + low_rank)
        scaled_ref[:, at] = scaled.astype(BF16)
        inner = inner + jnp.sum(scaled * hidden_ref[:, at].astype(F32), axis=1, keepdims=True)
    inner_ref[...] = as_row(inner * scale_ref[...])


def make_scaled(where, pieces, mixed, a_local, gain, hidden, scale):
    rows, width = hidden.shape
    return pl.pallas_call(
        scaled_kernel,
        in_specs=[SMEM] + [VMEM] * 9,
        out_specs=[VMEM, VMEM],
        out_shape=[jax.ShapeDtypeStruct((rows, width), BF16), jax.ShapeDtypeStruct((8, rows), F32)],
        compiler_params=pltpu.CompilerParams(vmem_limit_bytes=BIG),
        cost_estimate=LIGHT,
    )(where, *pieces, mixed, a_local, gain, hidden, scale)


def low_scaled_kernel(keep_ref, got_ref, other_ref, mixed_ref, a_ref, gain_ref, hidden_ref, scale_ref, scaled_ref, inner_ref):
    low_rank = lax.dot_general(
        mixed_ref[...], a_ref[...], (((0,), (0,)), ((), ())), precision=HIGH, preferred_element_type=F32
    )
    total = keep_ref[...].astype(F32) + got_ref[0].astype(F32) + other_ref[...].astype(F32)
    scaled = gain_ref[...] * (total + low_rank)
    scaled_ref[...] = scaled.astype(BF16)
    inner = jnp.sum(scaled * hidden_ref[...].astype(F32), axis=1, keepdims=True)
    inner_ref[...] = as_row(inner * scale_ref[...])


def low_scaled(keep, got, other, mixed, a_local, gain, hidden, scale):
    rows, width = hidden.shape
    whole = lambda shape: pl.BlockSpec(shape, lambda i: (0, 0))
    mine = pl.BlockSpec((1, rows, width), lambda i: (0, 0, 0))
    return pl.pallas_call(
        low_scaled_kernel,
        grid=(1,),
        in_specs=[
            whole((rows, width)), mine, whole((rows, width)), whole((RANK, rows)), whole((RANK, width)),
            whole((1, width)), whole((rows, width)), whole((rows, 1)),
        ],
        out_specs=[whole((rows, width)), whole((8, rows))],
        out_shape=[jax.ShapeDtypeStruct((rows, width), BF16), jax.ShapeDtypeStruct((8, rows), F32)],
        compiler_params=pltpu.CompilerParams(vmem_limit_bytes=BIG),
        cost_estimate=LIGHT,
    )(keep, got, other, mixed, a_local, gain, hidden, scale)


def hidden_gradient(scaled_ref, inner_ref, hidden_ref, scale_ref, incoming_ref):
    scale = scale_ref[...]
    pull = as_column(inner_ref[...]) * scale / MODEL_WIDTH
    return (
        incoming_ref[...].astype(F32)
        + scale * (scaled_ref[...].astype(F32) - hidden_ref[...].astype(F32) * pull)
    ).astype(BF16)


def top_kernel(scaled_ref, inner_ref, hidden_ref, scale_ref, incoming_ref, out_ref):
    out_ref[...] = hidden_gradient(scaled_ref, inner_ref, hidden_ref, scale_ref, incoming_ref)


def low_kernel(where_ref, scaled_ref, inner_ref, hidden_ref, scale_ref, incoming_ref, top_ref, *rest):
    grad = hidden_gradient(scaled_ref, inner_ref, hidden_ref, scale_ref, incoming_ref)
    rest[-1][...] = jnp.where(where_ref[3] == 1, top_ref[...], grad)


def finish_specs(rows, width, c):
    whole = lambda shape: pl.BlockSpec(shape, lambda i: (0, 0))
    return [
        whole((rows, width)),
        whole((8, rows)),
        pl.BlockSpec((rows, width), lambda i: (c, 0)),
        pl.BlockSpec((rows, 1), lambda i: (c, 0)),
    ]


def finish_top(scaled, inner, hidden, scale, grad_top, c):
    rows, width = scaled.shape
    return pl.pallas_call(
        top_kernel,
        grid=(1,),
        in_specs=finish_specs(rows, width, c) + [pl.BlockSpec((rows, width), lambda i: (c, 0))],
        out_specs=pl.BlockSpec((rows, width), lambda i: (0, 0)),
        out_shape=jax.ShapeDtypeStruct((rows, width), BF16),
        compiler_params=pltpu.CompilerParams(vmem_limit_bytes=BIG),
        cost_estimate=LIGHT,
    )(scaled, inner, hidden, scale, grad_top)


def finish_low(where, scaled, inner, hidden, scale, incoming, top):
    rows, width = scaled.shape
    block = pl.BlockSpec((rows, width), lambda i: (0, 0))
    return pl.pallas_call(
        low_kernel,
        grid=(1,),
        in_specs=[SMEM] + finish_specs(rows, width, 0) + [block, block],
        out_specs=block,
        out_shape=jax.ShapeDtypeStruct((rows, width), BF16),
        compiler_params=pltpu.CompilerParams(vmem_limit_bytes=BIG),
        cost_estimate=LIGHT,
    )(where, scaled, inner, hidden, scale, incoming, top)


def grads_kernel(where_ref, hidden_ref, scale_ref, gain_ref, projected_ref, *refs):
    out_ref = refs[-1]
    top = where_ref[3] == 1
    count = (len(refs) - 2) // 3
    total_a, total_b = 0.0, 0.0
    for c in range(count):
        low_dz, top_mixed, low_mixed = [refs[1 + k * count + c] for k in range(3)]
        rows = pl.ds(c * low_dz.shape[0], low_dz.shape[0])
        dz = jnp.where(top, refs[0][rows], low_dz[...])
        mixed = jnp.where(top, top_mixed[...], low_mixed[...])
        x = (hidden_ref[rows].astype(F32) * scale_ref[rows] * gain_ref[...]).astype(BF16)
        projected = projected_ref[:, rows]

        def both(left, right):
            value = lax.dot_general(
                two_halves(left), right, (((1,), (0,)), ((), ())), preferred_element_type=F32
            )
            return value[:RANK] + value[RANK:]

        total_a = total_a + both(mixed, x)
        total_b = total_b + both(projected, dz)
    out_ref[...] = jnp.concatenate([total_a, total_b], axis=0)


def make_grads(where, hidden, scale, gain, projected, lists, *earlier):
    arrays = [array for arrays in lists for array in arrays]
    return pl.pallas_call(
        in_order(grads_kernel, 5 + len(arrays), len(earlier)),
        in_specs=[SMEM] + [VMEM] * (4 + len(arrays)) + [ANY] * len(earlier),
        out_specs=VMEM,
        out_shape=jax.ShapeDtypeStruct((2 * RANK, hidden.shape[1]), F32),
        compiler_params=pltpu.CompilerParams(vmem_limit_bytes=BIG),
        cost_estimate=LIGHT,
    )(where, hidden, scale, gain, projected, *arrays, *earlier)


def ring_total(value, moved):
    after, far, before = moved
    return (value[...] + far[...]) + (after[...] + before[...])


def ring_kernel(value, after, far, before, out_ref):
    out_ref[...] = ring_total(value, (after, far, before))


def bank_kernel(mixing_ref, value, after, far, before, out_ref):
    total = ring_total(value, (after, far, before))
    count = total.shape[1] // SUB
    pieces = jnp.concatenate([total[:, j * SUB:(j + 1) * SUB] for j in range(count)], axis=0)
    out_ref[...] = lax.dot_general(
        mixing_ref[...], pieces, (((0,), (0,)), ((), ())), precision=HIGH, preferred_element_type=F32
    )


def round_kernel(factor, left, right, out_ref):
    out_ref[...] = ((left[...].astype(F32) + right[...].astype(F32)) * factor).astype(out_ref.dtype)


def small_call(kernel, out, operands, *earlier):
    return pl.pallas_call(
        in_order(kernel, len(operands), len(earlier)),
        in_specs=[VMEM] * len(operands) + [ANY] * len(earlier),
        out_specs=VMEM,
        out_shape=out,
        compiler_params=pltpu.CompilerParams(vmem_limit_bytes=BIG),
        cost_estimate=LIGHT,
    )(*operands, *earlier)


def ring_moves(value, axis):
    return [ring_move(value, axis, d) for d in (-1, 2, 1)]


def shards(hidden_in, preact, norm_gain, weight, bank, mix_index, mix_weight, grad_top):
    section = lax.axis_index("section")
    z, y = lax.axis_index("z"), lax.axis_index("y")
    place = lax.axis_index("pair") * 2 + lax.axis_index("core")
    where = jnp.stack([z, place, y, section]).astype(jnp.int32)
    tensor = ("pair", "core")
    bank_rows = bank.shape[0]

    tokens, local_width = grad_top.shape
    seg_local = local_width // SUB
    seg_row = MODEL_WIDTH // SUB
    own_weight = weight[0]
    shard = own_weight.shape[0]
    half = shard // 2

    first = make_first(where, grad_top, preact[0], own_weight)
    hidden, preact = hidden_in[0], preact[0]

    def local_pieces(array):
        array = array.reshape(2, RANK, seg_row, 2)
        return lax.dynamic_slice_in_dim(array, place * seg_local, seg_local, 2)

    mixing = compose(local_pieces(mix_index[0]), local_pieces(mix_weight[0]), bank_rows)
    mixing = mixing.reshape(2, RANK * seg_local, bank_rows)
    factors = jnp.einsum("fnb,bs->fns", mixing, bank, precision=HIGH)
    a_local = factors[0].reshape(RANK, local_width)
    b_both = two_halves(factors[1].reshape(RANK, local_width))

    hidden_f = hidden.astype(F32)
    sums = lax.psum(
        jnp.concatenate(
            [
                jnp.sum(hidden_f * hidden_f, axis=1)[None],
                jnp.dot(a_local, (hidden_f * norm_gain).T, precision=HIGH),
                jnp.dot(factors[1].reshape(RANK, local_width), first[:tokens].astype(F32).T, precision=HIGH),
            ],
            axis=0,
        ),
        tensor,
    )
    scale_row = lax.rsqrt(sums[:1] / MODEL_WIDTH + epsilon)
    projected = sums[1:1 + RANK] * scale_row
    scale = scale_row.reshape(tokens, 1)
    top_mixed = sums[1 + RANK:]

    z_ring = gather_ring(own_weight, "z", scale)
    y_ring = gather_ring(first, "y", scale)

    _, z_after, z_far_low, z_far_high, z_before = z_ring
    _, y_after, y_far_low, y_far_high, y_before = y_ring
    slim, rest = half // 2, shard - half // 2
    corner = join(where, 0, (z_far_low, z_far_high), ((0, half), (0, half)), y_far_high)
    corner = ring_move(corner, "y", 2, (0,))

    dz_pieces = (y_ring[0], y_ring[1], y_ring[2], y_ring[4])
    mine, keep, send = top_product(where, tokens, dz_pieces, z_ring, y_far_high)
    got = swap(send, "core", (1,))
    theirs = add_theirs(keep, got)
    other = swap(theirs, "pair", (1,))
    along_z = join(
        where, 0, (y_far_low, y_far_high, y_after, y_before),
        ((0, half), (0, half), (slim, rest), (slim, rest)), theirs,
    )
    z_pair = (ring_move(along_z, "z", -1, (0,)), ring_move(along_z, "z", 1, (0,)))
    own, to_after, to_far, to_before = add_mine(mine, got, other, corner)
    from_before = ring_move(to_after, "y", 1, (1,))
    from_far = ring_move(to_far, "y", 2, (1,))
    from_after = ring_move(to_before, "y", -1, (1,))
    along_y = join(
        where, 0, (z_far_low, z_far_high, z_after, z_before),
        ((0, half), (0, half), (0, slim), (0, slim)), from_before, from_far, from_after,
    )
    y_pair = (ring_move(along_y, "y", -1, (0,)), ring_move(along_y, "y", 1, (0,)))
    w_pieces = (*z_ring, *y_ring[1:], corner, *y_pair, *z_pair)

    pieces = (own, from_after, from_far, from_before)
    scaled, inner = make_scaled(where, pieces, top_mixed, a_local, norm_gain, hidden, scale)
    top_grad = finish_top(scaled, lax.psum(inner, tensor), hidden, scale, grad_top, 0)
    low_in = lax.ppermute(top_grad, "section", [(1, 0)])

    low_dz, part = make_dz(low_in, preact, b_both, 0)
    low_mixed = lax.psum(part, tensor)
    mine, keep, send = low_product(where, z, y, place, low_dz, w_pieces, low_mixed)
    got = swap(send, "core", (0,))
    theirs = add_theirs(keep, got)
    other = swap(theirs, "pair", (0,))
    scaled, inner = low_scaled(mine, got, other, low_mixed, a_local, norm_gain, hidden, scale)
    result = finish_low(where, scaled, lax.psum(inner, tensor), hidden, scale, low_in, top_grad)

    grads = make_grads(
        where, hidden, scale, norm_gain, projected, ([first], [low_dz], [top_mixed], [low_mixed])
    )
    over_y = ring_moves(grads, "y")
    grads = small_call(ring_kernel, jax.ShapeDtypeStruct(grads.shape, F32), (grads, *over_y), send)
    over_z = ring_moves(grads, "z")
    flat = mixing.reshape(2, RANK, seg_local, bank_rows).transpose(2, 0, 1, 3)
    flat = flat.reshape(2 * RANK * seg_local, bank_rows)
    bank_shape = (bank_rows, SUB)
    share = small_call(bank_kernel, jax.ShapeDtypeStruct(bank_shape, F32), (flat, grads, *over_z), theirs)
    core_share = swap(share, "core")
    half_shape = jax.ShapeDtypeStruct(bank_shape, BF16)
    add_up = functools.partial(round_kernel, 1.0 / math.sqrt(TOKENS))
    share = small_call(add_up, half_shape, (share, core_share))
    pair_share = swap(share, "pair")
    add_up = functools.partial(round_kernel, 1.0)
    share = small_call(add_up, half_shape, (share, pair_share))
    other_share = lax.ppermute(share, "section", [(0, 1), (1, 0)])
    bank_grad = small_call(add_up, jax.ShapeDtypeStruct(bank_shape, F32), (share, other_share), result)
    return (result[None], bank_grad)


def solution(mesh):
    fine = Mesh(
        mesh.devices.reshape(2, RING, RING, 2, 2), ("section", "z", "y", "pair", "core")
    )
    rows, columns = ("z", "y"), ("pair", "core")
    return jax.shard_map(
        shards,
        mesh=fine,
        in_specs=(
            P("section", rows, columns),
            P("section", rows, columns),
            P("section", columns),
            P("section", rows, columns),
            P(),
            P("section", None, None, None),
            P("section", None, None, None),
            P(rows, columns),
        ),
        out_specs=(P("section", rows, columns), P()),
        check_vma=False,
    )
```

```python
import functools
import math

import jax
import jax.numpy as jnp
from jax import lax
from jax.experimental import pallas as pl
from jax.experimental.pallas import tpu as pltpu
from jax.sharding import Mesh, PartitionSpec as P

MODEL_WIDTH = 8192
RANK = 4
SUB = 256
TOKENS = 4096
RING = 4
LANES = 128

epsilon = 1e-06
HIGH = lax.Precision.HIGHEST
F32 = jnp.float32
BF16 = jnp.bfloat16
ANY = pl.BlockSpec(memory_space=pl.ANY)
SMEM = pl.BlockSpec(memory_space=pltpu.SMEM)
VMEM = pl.BlockSpec(memory_space=pltpu.VMEM)
HBM = pl.BlockSpec(memory_space=pltpu.HBM)
BIG = 48 * 1024 * 1024
MEDIUM = 20 * 1024 * 1024
SMALL = 12 * 1024 * 1024
LIGHT = pl.CostEstimate(flops=0, bytes_accessed=2 ** 20, transcendentals=0)


def ring_route(distance, sections=(0, 1)):
    return [(s * RING + i, s * RING + (i + distance) % RING) for s in sections for i in range(RING)]


def ring_move(block, axis, distance, sections=(0, 1)):
    return lax.ppermute(block, ("section", axis), ring_route(distance, sections))


def swap(block, axis, sections=(0, 1)):
    pairs = [(s * 2 + i, s * 2 + 1 - i) for s in sections for i in range(2)]
    return lax.ppermute(block, ("section", axis), pairs)


def after(value, earlier):
    return lax.optimization_barrier((value, earlier))[0]


def in_order(kernel, operands, extra):
    return lambda *refs: kernel(*refs[:operands], *refs[operands + extra:])


def compose(index_layer, weight_layer, rows):
    columns = lax.broadcasted_iota(jnp.int32, (1, 1, 1, 1, rows), 4)
    onehot = (index_layer[..., None] == columns).astype(F32)
    return jnp.sum(onehot * weight_layer[..., None], axis=3)


def two_halves(value):
    high = value.astype(BF16)
    return jnp.concatenate([high, (value - high.astype(F32)).astype(BF16)], axis=0)


def activation_gradient(incoming_ref, preact_ref):
    value = preact_ref[...].astype(F32)
    sig = jax.nn.sigmoid(value)
    slope = sig * (1.0 + value * (1.0 - sig))
    return (incoming_ref[...].astype(F32) * slope).astype(BF16)


def dz_kernel(incoming_ref, preact_ref, b_ref, dz_ref, mixed_ref):
    dz = activation_gradient(incoming_ref, preact_ref)
    dz_ref[...] = dz
    both = lax.dot_general(b_ref[...], dz, (((1,), (1,)), ((), ())), preferred_element_type=F32)
    mixed_ref[...] = both[:RANK] + both[RANK:]


def first_kernel(where_ref, incoming_ref, preact_ref, weight_ref, out_ref, incoming, preact, sem):
    def fetch(*pairs):
        copies = [pltpu.make_async_copy(*pair, sem.at[i]) for i, pair in enumerate(pairs)]
        for copy in copies:
            copy.start()
        for copy in copies:
            copy.wait()

    @pl.when(where_ref[3] == 1)
    def _():
        fetch((incoming_ref, incoming), (preact_ref, preact))
        out_ref[:incoming.shape[0]] = activation_gradient(incoming, preact)

    @pl.when(where_ref[3] == 0)
    def _():
        fetch((weight_ref, out_ref))


def make_first(where, incoming, preact, weight):
    return pl.pallas_call(
        first_kernel,
        in_specs=[SMEM, HBM, HBM, HBM],
        out_specs=VMEM,
        out_shape=jax.ShapeDtypeStruct(weight.shape, BF16),
        scratch_shapes=[
            pltpu.VMEM(incoming.shape, BF16),
            pltpu.VMEM(incoming.shape, BF16),
            pltpu.SemaphoreType.DMA((2,)),
        ],
        compiler_params=pltpu.CompilerParams(vmem_limit_bytes=MEDIUM),
        cost_estimate=LIGHT,
    )(where, incoming, preact, weight)


def join_kernel(wanted, parts, where_ref, *refs):
    sources, out_ref, held, sem, out_sem = refs[:len(parts)], *refs[-4:]

    @pl.when(where_ref[3] == wanted)
    def _():
        start = 0
        steps = []
        for i, (first, rows) in enumerate(parts):
            here = held.at[pl.ds(start, rows)]
            fetch = pltpu.make_async_copy(sources[i].at[pl.ds(first, rows)], here, sem.at[i])
            store = pltpu.make_async_copy(here, out_ref.at[pl.ds(start, rows)], out_sem.at[i])
            steps.append((fetch, store))
            start += rows
        for fetch, _ in steps:
            fetch.start()
        for fetch, store in steps:
            fetch.wait()
            store.start()
        for _, store in steps:
            store.wait()


def join(where, wanted, arrays, parts, *earlier):
    rows, width = sum(count for _, count in parts), arrays[0].shape[1]
    return pl.pallas_call(
        in_order(functools.partial(join_kernel, wanted, parts), 1 + len(arrays), len(earlier)),
        in_specs=[SMEM] + [ANY] * (len(arrays) + len(earlier)),
        out_specs=HBM,
        out_shape=jax.ShapeDtypeStruct((rows, width), BF16),
        scratch_shapes=[
            pltpu.VMEM((rows, width), BF16),
            pltpu.SemaphoreType.DMA((len(arrays),)),
            pltpu.SemaphoreType.DMA((len(arrays),)),
        ],
        compiler_params=pltpu.CompilerParams(vmem_limit_bytes=SMALL),
        cost_estimate=LIGHT,
    )(where, *arrays, *earlier)


def halves_kernel(after_ref, before_ref, low_ref, high_ref, sem):
    half = low_ref.shape[0]
    low = pltpu.make_async_copy(after_ref.at[pl.ds(0, half)], low_ref, sem.at[0])
    high = pltpu.make_async_copy(before_ref.at[pl.ds(half, half)], high_ref, sem.at[1])
    low.start()
    high.start()
    low.wait()
    high.wait()


def gather_ring(block, axis, *earlier):
    rows, width = block.shape
    after = ring_move(block, axis, -1)
    before = ring_move(block, axis, 1)
    low, high = pl.pallas_call(
        in_order(halves_kernel, 2, len(earlier)),
        in_specs=[ANY, ANY] + [ANY] * len(earlier),
        out_specs=[VMEM, VMEM],
        out_shape=[jax.ShapeDtypeStruct((rows // 2, width), BF16)] * 2,
        scratch_shapes=[pltpu.SemaphoreType.DMA((2,))],
        compiler_params=pltpu.CompilerParams(vmem_limit_bytes=SMALL),
        cost_estimate=LIGHT,
    )(after, before, *earlier)
    return block, after, ring_move(low, axis, -1), ring_move(high, axis, 1), before


def make_dz(incoming, preact, b_both, c, *earlier):
    rows, width = incoming.shape
    return pl.pallas_call(
        in_order(dz_kernel, 3, len(earlier)),
        grid=(1,),
        in_specs=[
            pl.BlockSpec((rows, width), lambda i: (0, 0)),
            pl.BlockSpec((rows, width), lambda i: (c, 0)),
            pl.BlockSpec((2 * RANK, width), lambda i: (0, 0)),
        ]
        + [ANY] * len(earlier),
        out_specs=[
            pl.BlockSpec((rows, width), lambda i: (0, 0)),
            pl.BlockSpec((RANK, rows), lambda i: (0, 0)),
        ],
        out_shape=[
            jax.ShapeDtypeStruct((rows, width), BF16),
            jax.ShapeDtypeStruct((RANK, rows), F32),
        ],
        compiler_params=pltpu.CompilerParams(vmem_limit_bytes=MEDIUM),
        cost_estimate=LIGHT,
    )(incoming, preact, b_both, *earlier)


def top_product_kernel(rows, where_ref, *refs):
    dz_refs, w_refs = refs[:4], refs[4:9]
    mine_ref, theirs_ref, send_ref, dz_all, w_all, dz_sem, w_sem = refs[9:]

    @pl.when(where_ref[3] == 1)
    def _():
        copies = [
            pltpu.make_async_copy(ref.at[pl.ds(0, rows)], dz_all.at[pl.ds(i * rows, rows)], dz_sem.at[i])
            for i, ref in enumerate(dz_refs)
        ]
        for copy in copies:
            copy.start()
        own, after, far_low, far_high, before = w_refs
        half = far_low.shape[0]
        pltpu.make_async_copy(own, w_all.at[0], w_sem.at[0]).start()
        pltpu.make_async_copy(after, w_all.at[1], w_sem.at[1]).start()
        pltpu.make_async_copy(far_low, w_all.at[2, pl.ds(0, half)], w_sem.at[2]).start()
        pltpu.make_async_copy(far_high, w_all.at[2, pl.ds(half, half)], w_sem.at[2]).start()
        pltpu.make_async_copy(before, w_all.at[3], w_sem.at[3]).start()
        for copy in copies:
            copy.wait()
        z, place = where_ref[0], where_ref[1]

        @pl.loop(0, RING)
        def _(i):
            pltpu.make_async_copy(own, w_all.at[i], w_sem.at[i]).wait()
            value = lax.dot_general(
                dz_all[...], w_all[i], (((1,), (1,)), ((), ())), preferred_element_type=F32
            ).astype(BF16)
            target = lax.rem(z + i, RING)
            own_core = lax.rem(target, 2) == lax.rem(place, 2)
            far = jnp.where(target // 2 == place // 2, 0, 1)

            @pl.when(jnp.logical_and(own_core, far == 0))
            def _():
                mine_ref[...] = value

            @pl.when(jnp.logical_and(own_core, far == 1))
            def _():
                theirs_ref[...] = value

            @pl.when(jnp.logical_not(own_core))
            def _():
                send_ref[far] = value


def top_product(where, rows, dz_pieces, w_pieces, *earlier):
    wide, width = w_pieces[0].shape
    return pl.pallas_call(
        in_order(functools.partial(top_product_kernel, rows), 10, len(earlier)),
        in_specs=[SMEM] + [HBM] * 9 + [ANY] * len(earlier),
        out_specs=[VMEM, VMEM, VMEM],
        out_shape=[jax.ShapeDtypeStruct((RING * rows, wide), BF16)] * 2
        + [jax.ShapeDtypeStruct((2, RING * rows, wide), BF16)],
        scratch_shapes=[
            pltpu.VMEM((RING * rows, width), BF16),
            pltpu.VMEM((RING, wide, width), BF16),
            pltpu.SemaphoreType.DMA((4,)),
            pltpu.SemaphoreType.DMA((RING,)),
        ],
        compiler_params=pltpu.CompilerParams(vmem_limit_bytes=36 * 1024 * 1024),
        cost_estimate=pl.CostEstimate(
            flops=2 * RING * RING * rows * wide * width, bytes_accessed=2 ** 24, transcendentals=0
        ),
    )(where, *dz_pieces, *w_pieces, *earlier)


def low_plan(shard, wide):
    copies, blocks = [], []

    def take(array, row, rows, *names):
        at = sum(rows for *_, rows in copies)
        copies.append((array, row, at, rows))
        blocks.extend(names)

    for base, step in ((0, lambda d, h: (d, 0, h)), (4, lambda d, h: (0, d, h))):
        if base == 0:
            take(0, 0, shard, step(0, 0), step(0, 1))
        take(base + 1, 0, shard, step(1, 0), step(1, 1))
        take(base + 2, 0, wide, step(2, 0))
        take(base + 3, 0, wide, step(2, 1))
        take(base + 4, 0, shard, step(3, 0), step(3, 1))
    corner, y_pair, z_pair = 9, {1: 10, 3: 11}, {1: 12, 3: 13}
    take(corner, 0, shard, (2, 2, 0), (2, 2, 1))
    for d in (1, 3):
        take(y_pair[d], 0, shard, (2, d, 0), (2, d, 1))
        take(z_pair[d], 0, shard, (d, 2, 0), (d, 2, 1))
    slim, rest = wide // 2, shard - wide // 2
    for i, d in enumerate((1, 3)):
        for j, e in enumerate((1, 3)):
            take(y_pair[e], shard + i * slim, slim)
            take(z_pair[d], shard + j * rest, rest, (d, e, 0), (d, e, 1))
    return copies, blocks


def low_product_kernel(plan, where_ref, table_ref, dz_ref, *refs):
    count = len(refs) - 7
    w_refs = refs[:count]
    mine_ref, theirs_ref, send_ref, dz_all, w_all, dz_sem, sem = refs[count:]
    steps, deep = w_all.shape[0], w_all.shape[1]
    wide = deep // 2

    @pl.when(where_ref[3] == 0)
    def _():
        dz_copy = pltpu.make_async_copy(dz_ref, dz_all, dz_sem)
        dz_copy.start()
        for array, row, at, rows in plan:
            while rows:
                part = min(rows, deep - at % deep)
                pltpu.make_async_copy(
                    w_refs[array].at[pl.ds(row, part)],
                    w_all.at[at // deep, pl.ds(at % deep, part)],
                    sem.at[at // deep],
                ).start()
                row, at, rows = row + part, at + part, rows - part
        dz_copy.wait()

        @pl.loop(0, steps)
        def _(step):
            pltpu.make_async_copy(w_refs[0], w_all.at[step], sem.at[step]).wait()
            value = lax.dot_general(
                dz_all[...], w_all[step], (((1,), (1,)), ((), ())), preferred_element_type=F32
            ).astype(BF16)
            for k in range(2):
                entry = table_ref[2 * step + k]
                columns = pl.ds(pl.multiple_of(lax.rem(entry, 2 * RING) * wide, wide), wide)
                far = lax.rem(entry // (2 * RING), 2)
                block = value[:, k * wide:(k + 1) * wide]

                @pl.when(entry < 2 * RING)
                def _():
                    mine_ref[:, columns] = block

                @pl.when(jnp.logical_and(entry >= 2 * RING, entry < 4 * RING))
                def _():
                    theirs_ref[:, columns] = block

                @pl.when(entry >= 4 * RING)
                def _():
                    send_ref[far, :, columns] = block


def low_product(where, z, y, place, dz, w_pieces, *earlier):
    rows, width = dz.shape
    shard = w_pieces[0].shape[0]
    wide = shard // 2
    copies, blocks = low_plan(shard, wide)
    steps = [jnp.array(column, jnp.int32) for column in zip(*blocks)]
    target = (z + steps[0]) % RING
    column = (y + steps[1]) % RING * 2 + steps[2]
    other_core = (target % 2 != place % 2).astype(jnp.int32)
    other_pair = (target // 2 != place // 2).astype(jnp.int32)
    table = (other_core * 2 + other_pair) * 2 * RING + column
    return pl.pallas_call(
        in_order(functools.partial(low_product_kernel, copies), 3 + len(w_pieces), len(earlier)),
        in_specs=[SMEM, SMEM, HBM] + [HBM] * len(w_pieces) + [ANY] * len(earlier),
        out_specs=[VMEM, VMEM, VMEM],
        out_shape=[jax.ShapeDtypeStruct((rows, 2 * RING * wide), BF16)] * 2
        + [jax.ShapeDtypeStruct((2, rows, 2 * RING * wide), BF16)],
        scratch_shapes=[
            pltpu.VMEM((rows, width), BF16),
            pltpu.VMEM((RING * RING, shard, width), BF16),
            pltpu.SemaphoreType.DMA,
            pltpu.SemaphoreType.DMA((RING * RING,)),
        ],
        compiler_params=pltpu.CompilerParams(vmem_limit_bytes=BIG),
        cost_estimate=pl.CostEstimate(
            flops=16 * RING * rows * wide * width, bytes_accessed=2 ** 25, transcendentals=0
        ),
    )(where, table, dz, *w_pieces, *earlier)


def add_kernel(keep_ref, got_ref, out_ref):
    out_ref[...] = (keep_ref[...].astype(F32) + got_ref[0].astype(F32)).astype(BF16)


def add_theirs(keep, got):
    rows, wide = keep.shape
    whole = pl.BlockSpec((rows, wide), lambda i: (0, 0))
    return pl.pallas_call(
        add_kernel,
        grid=(1,),
        in_specs=[whole, pl.BlockSpec((1, rows, wide), lambda i: (1, 0, 0))],
        out_specs=whole,
        out_shape=jax.ShapeDtypeStruct((rows, wide), BF16),
        compiler_params=pltpu.CompilerParams(vmem_limit_bytes=SMALL),
        cost_estimate=LIGHT,
    )(keep, got)


def total_kernel(keep_ref, got_ref, other_ref, *out_refs):
    rows = out_refs[0].shape[0]
    for i, ref in enumerate(out_refs):
        part = pl.ds(i * rows, rows)
        ref[...] = (
            keep_ref[part].astype(F32) + got_ref[0, part].astype(F32) + other_ref[part].astype(F32)
        ).astype(BF16)


def add_mine(keep, got, other, *earlier):
    rows, wide = keep.shape
    whole = pl.BlockSpec((rows, wide), lambda i: (0, 0))
    return pl.pallas_call(
        in_order(total_kernel, 3, len(earlier)),
        grid=(1,),
        in_specs=[whole, pl.BlockSpec((1, rows, wide), lambda i: (0, 0, 0)), whole] + [ANY] * len(earlier),
        out_specs=[pl.BlockSpec((rows // RING, wide), lambda i: (0, 0))] * RING,
        out_shape=[jax.ShapeDtypeStruct((rows // RING, wide), BF16)] * RING,
        compiler_params=pltpu.CompilerParams(vmem_limit_bytes=SMALL),
        cost_estimate=LIGHT,
    )(keep, got, other, *earlier)


def as_row(column):
    square = jnp.broadcast_to(column, (column.shape[0], LANES))
    return jnp.transpose(square)[:8]


def as_column(row):
    square = jnp.concatenate([row] * (LANES // 8), axis=0)
    return jnp.transpose(square)[:, :1]


def scaled_kernel(where_ref, own, after, far, before, mixed_ref, a_ref, gain_ref, hidden_ref, scale_ref, scaled_ref, inner_ref):
    wide = own.shape[1]
    mixed = mixed_ref[...]
    inner = jnp.zeros((own.shape[0], 1), F32)
    for r, piece in enumerate((own, after, far, before)):
        at = pl.ds(pl.multiple_of(lax.rem(where_ref[2] + r, RING) * wide, wide), wide)
        low_rank = lax.dot_general(
            mixed, a_ref[:, at], (((0,), (0,)), ((), ())), precision=HIGH, preferred_element_type=F32
        )
        scaled = gain_ref[:, at] * (piece[...].astype(F32) + low_rank)
        scaled_ref[:, at] = scaled.astype(BF16)
        inner = inner + jnp.sum(scaled * hidden_ref[:, at].astype(F32), axis=1, keepdims=True)
    inner_ref[...] = as_row(inner * scale_ref[...])


def make_scaled(where, pieces, mixed, a_local, gain, hidden, scale):
    rows, width = hidden.shape
    return pl.pallas_call(
        scaled_kernel,
        in_specs=[SMEM] + [VMEM] * 9,
        out_specs=[VMEM, VMEM],
        out_shape=[jax.ShapeDtypeStruct((rows, width), BF16), jax.ShapeDtypeStruct((8, rows), F32)],
        compiler_params=pltpu.CompilerParams(vmem_limit_bytes=MEDIUM),
        cost_estimate=LIGHT,
    )(where, *pieces, mixed, a_local, gain, hidden, scale)


def low_scaled_kernel(keep_ref, got_ref, other_ref, mixed_ref, a_ref, gain_ref, hidden_ref, scale_ref, scaled_ref, inner_ref):
    low_rank = lax.dot_general(
        mixed_ref[...], a_ref[...], (((0,), (0,)), ((), ())), precision=HIGH, preferred_element_type=F32
    )
    total = keep_ref[...].astype(F32) + got_ref[0].astype(F32) + other_ref[...].astype(F32)
    scaled = gain_ref[...] * (total + low_rank)
    scaled_ref[...] = scaled.astype(BF16)
    inner = jnp.sum(scaled * hidden_ref[...].astype(F32), axis=1, keepdims=True)
    inner_ref[...] = as_row(inner * scale_ref[...])


def low_scaled(keep, got, other, mixed, a_local, gain, hidden, scale):
    rows, width = hidden.shape
    whole = lambda shape: pl.BlockSpec(shape, lambda i: (0, 0))
    mine = pl.BlockSpec((1, rows, width), lambda i: (0, 0, 0))
    return pl.pallas_call(
        low_scaled_kernel,
        grid=(1,),
        in_specs=[
            whole((rows, width)), mine, whole((rows, width)), whole((RANK, rows)), whole((RANK, width)),
            whole((1, width)), whole((rows, width)), whole((rows, 1)),
        ],
        out_specs=[whole((rows, width)), whole((8, rows))],
        out_shape=[jax.ShapeDtypeStruct((rows, width), BF16), jax.ShapeDtypeStruct((8, rows), F32)],
        compiler_params=pltpu.CompilerParams(vmem_limit_bytes=MEDIUM),
        cost_estimate=LIGHT,
    )(keep, got, other, mixed, a_local, gain, hidden, scale)


def hidden_gradient(scaled_ref, inner_ref, hidden_ref, scale_ref, incoming_ref):
    scale = scale_ref[...]
    pull = as_column(inner_ref[...]) * scale / MODEL_WIDTH
    return (
        incoming_ref[...].astype(F32)
        + scale * (scaled_ref[...].astype(F32) - hidden_ref[...].astype(F32) * pull)
    ).astype(BF16)


def top_kernel(scaled_ref, inner_ref, hidden_ref, scale_ref, incoming_ref, out_ref):
    out_ref[...] = hidden_gradient(scaled_ref, inner_ref, hidden_ref, scale_ref, incoming_ref)


def low_kernel(where_ref, scaled_ref, inner_ref, hidden_ref, scale_ref, incoming_ref, top_ref, *rest):
    grad = hidden_gradient(scaled_ref, inner_ref, hidden_ref, scale_ref, incoming_ref)
    rest[-1][...] = jnp.where(where_ref[3] == 1, top_ref[...], grad)


def finish_specs(rows, width, c):
    whole = lambda shape: pl.BlockSpec(shape, lambda i: (0, 0))
    return [
        whole((rows, width)),
        whole((8, rows)),
        pl.BlockSpec((rows, width), lambda i: (c, 0)),
        pl.BlockSpec((rows, 1), lambda i: (c, 0)),
    ]


def finish_top(scaled, inner, hidden, scale, grad_top, c):
    rows, width = scaled.shape
    return pl.pallas_call(
        top_kernel,
        grid=(1,),
        in_specs=finish_specs(rows, width, c) + [pl.BlockSpec((rows, width), lambda i: (c, 0))],
        out_specs=pl.BlockSpec((rows, width), lambda i: (0, 0)),
        out_shape=jax.ShapeDtypeStruct((rows, width), BF16),
        compiler_params=pltpu.CompilerParams(vmem_limit_bytes=MEDIUM),
        cost_estimate=LIGHT,
    )(scaled, inner, hidden, scale, grad_top)


def finish_low(where, scaled, inner, hidden, scale, incoming, top):
    rows, width = scaled.shape
    block = pl.BlockSpec((rows, width), lambda i: (0, 0))
    return pl.pallas_call(
        low_kernel,
        grid=(1,),
        in_specs=[SMEM] + finish_specs(rows, width, 0) + [block, block],
        out_specs=block,
        out_shape=jax.ShapeDtypeStruct((rows, width), BF16),
        compiler_params=pltpu.CompilerParams(vmem_limit_bytes=MEDIUM),
        cost_estimate=LIGHT,
    )(where, scaled, inner, hidden, scale, incoming, top)


def grads_kernel(where_ref, hidden_ref, scale_ref, gain_ref, projected_ref, *refs):
    out_ref = refs[-1]
    top = where_ref[3] == 1
    count = (len(refs) - 2) // 3
    total_a, total_b = 0.0, 0.0
    for c in range(count):
        low_dz, top_mixed, low_mixed = [refs[1 + k * count + c] for k in range(3)]
        rows = pl.ds(c * low_dz.shape[0], low_dz.shape[0])
        dz = jnp.where(top, refs[0][rows], low_dz[...])
        mixed = jnp.where(top, top_mixed[...], low_mixed[...])
        x = (hidden_ref[rows].astype(F32) * scale_ref[rows] * gain_ref[...]).astype(BF16)
        projected = projected_ref[:, rows]

        def both(left, right):
            value = lax.dot_general(
                two_halves(left), right, (((1,), (0,)), ((), ())), preferred_element_type=F32
            )
            return value[:RANK] + value[RANK:]

        total_a = total_a + both(mixed, x)
        total_b = total_b + both(projected, dz)
    out_ref[...] = jnp.concatenate([total_a, total_b], axis=0)


def make_grads(where, hidden, scale, gain, projected, lists, *earlier):
    arrays = [array for arrays in lists for array in arrays]
    return pl.pallas_call(
        in_order(grads_kernel, 5 + len(arrays), len(earlier)),
        in_specs=[SMEM] + [VMEM] * (4 + len(arrays)) + [ANY] * len(earlier),
        out_specs=VMEM,
        out_shape=jax.ShapeDtypeStruct((2 * RANK, hidden.shape[1]), F32),
        compiler_params=pltpu.CompilerParams(vmem_limit_bytes=MEDIUM),
        cost_estimate=LIGHT,
    )(where, hidden, scale, gain, projected, *arrays, *earlier)


def ring_total(value, moved):
    after, far, before = moved
    return (value[...] + far[...]) + (after[...] + before[...])


def ring_kernel(value, after, far, before, out_ref):
    out_ref[...] = ring_total(value, (after, far, before))


def bank_kernel(mixing_ref, value, after, far, before, out_ref):
    total = ring_total(value, (after, far, before))
    count = total.shape[1] // SUB
    pieces = jnp.concatenate([total[:, j * SUB:(j + 1) * SUB] for j in range(count)], axis=0)
    out_ref[...] = lax.dot_general(
        mixing_ref[...], pieces, (((0,), (0,)), ((), ())), precision=HIGH, preferred_element_type=F32
    )


def round_kernel(factor, left, right, out_ref):
    out_ref[...] = ((left[...].astype(F32) + right[...].astype(F32)) * factor).astype(out_ref.dtype)


def small_call(kernel, out, operands, *earlier):
    return pl.pallas_call(
        in_order(kernel, len(operands), len(earlier)),
        in_specs=[VMEM] * len(operands) + [ANY] * len(earlier),
        out_specs=VMEM,
        out_shape=out,
        compiler_params=pltpu.CompilerParams(vmem_limit_bytes=SMALL),
        cost_estimate=LIGHT,
    )(*operands, *earlier)


def ring_moves(value, axis):
    return [ring_move(value, axis, d) for d in (-1, 2, 1)]


def shards(hidden_in, preact, norm_gain, weight, bank, mix_index, mix_weight, grad_top):
    section = lax.axis_index("section")
    z, y = lax.axis_index("z"), lax.axis_index("y")
    place = lax.axis_index("pair") * 2 + lax.axis_index("core")
    where = jnp.stack([z, place, y, section]).astype(jnp.int32)
    tensor = ("pair", "core")
    bank_rows = bank.shape[0]

    tokens, local_width = grad_top.shape
    seg_local = local_width // SUB
    seg_row = MODEL_WIDTH // SUB
    own_weight = weight[0]
    shard = own_weight.shape[0]
    half = shard // 2

    first = make_first(where, grad_top, preact[0], own_weight)
    hidden, preact = hidden_in[0], preact[0]

    def local_pieces(array):
        array = array.reshape(2, RANK, seg_row, 2)
        return lax.dynamic_slice_in_dim(array, place * seg_local, seg_local, 2)

    mixing = compose(local_pieces(mix_index[0]), local_pieces(mix_weight[0]), bank_rows)
    mixing = mixing.reshape(2, RANK * seg_local, bank_rows)
    factors = jnp.einsum("fnb,bs->fns", mixing, bank, precision=HIGH)
    a_local = factors[0].reshape(RANK, local_width)
    b_both = two_halves(factors[1].reshape(RANK, local_width))

    hidden_f = hidden.astype(F32)
    sums = lax.psum(
        jnp.concatenate(
            [
                jnp.sum(hidden_f * hidden_f, axis=1)[None],
                jnp.dot(a_local, (hidden_f * norm_gain).T, precision=HIGH),
                jnp.dot(factors[1].reshape(RANK, local_width), first[:tokens].astype(F32).T, precision=HIGH),
            ],
            axis=0,
        ),
        tensor,
    )
    scale_row = lax.rsqrt(sums[:1] / MODEL_WIDTH + epsilon)
    projected = sums[1:1 + RANK] * scale_row
    scale = scale_row.reshape(tokens, 1)
    top_mixed = sums[1 + RANK:]

    z_ring = gather_ring(own_weight, "z", scale)
    y_ring = gather_ring(first, "y", scale)

    _, z_after, z_far_low, z_far_high, z_before = z_ring
    _, y_after, y_far_low, y_far_high, y_before = y_ring
    slim, rest = half // 2, shard - half // 2
    corner = join(where, 0, (z_far_low, z_far_high), ((0, half), (0, half)), y_far_high)
    corner = ring_move(corner, "y", 2, (0,))

    dz_pieces = (y_ring[0], y_ring[1], y_ring[2], y_ring[4])
    mine, keep, send = top_product(where, tokens, dz_pieces, z_ring, y_far_high)
    got = swap(send, "core", (1,))
    theirs = add_theirs(keep, got)
    other = swap(theirs, "pair", (1,))
    along_z = join(
        where, 0, (y_far_low, y_far_high, y_after, y_before),
        ((0, half), (0, half), (slim, rest), (slim, rest)), theirs,
    )
    z_pair = (ring_move(along_z, "z", -1, (0,)), ring_move(along_z, "z", 1, (0,)))
    own, to_after, to_far, to_before = add_mine(mine, got, other, corner)
    from_before = ring_move(to_after, "y", 1, (1,))
    from_far = ring_move(to_far, "y", 2, (1,))
    from_after = ring_move(to_before, "y", -1, (1,))
    along_y = join(
        where, 0, (z_far_low, z_far_high, z_after, z_before),
        ((0, half), (0, half), (0, slim), (0, slim)), from_before, from_far, from_after,
    )
    y_pair = (ring_move(along_y, "y", -1, (0,)), ring_move(along_y, "y", 1, (0,)))
    w_pieces = (*z_ring, *y_ring[1:], corner, *y_pair, *z_pair)

    pieces = (own, from_after, from_far, from_before)
    scaled, inner = make_scaled(where, pieces, top_mixed, a_local, norm_gain, hidden, scale)
    top_grad = finish_top(scaled, lax.psum(inner, tensor), hidden, scale, grad_top, 0)
    low_in = lax.ppermute(top_grad, "section", [(1, 0)])

    low_dz, part = make_dz(low_in, preact, b_both, 0)
    low_mixed = lax.psum(part, tensor)
    mine, keep, send = low_product(where, z, y, place, low_dz, w_pieces, low_mixed)
    got = swap(send, "core", (0,))
    theirs = add_theirs(keep, got)
    other = swap(theirs, "pair", (0,))
    scaled, inner = low_scaled(mine, got, other, low_mixed, a_local, norm_gain, hidden, scale)
    inner = lax.psum(inner, tensor)
    result = finish_low(where, scaled, inner, hidden, scale, low_in, top_grad)

    grads = make_grads(
        where, hidden, scale, norm_gain, projected, ([first], [low_dz], [top_mixed], [low_mixed])
    )
    over_y = ring_moves(grads, "y")
    grads = small_call(ring_kernel, jax.ShapeDtypeStruct(grads.shape, F32), (grads, *over_y), send)
    over_z = ring_moves(grads, "z")
    flat = mixing.reshape(2, RANK, seg_local, bank_rows).transpose(2, 0, 1, 3)
    flat = flat.reshape(2 * RANK * seg_local, bank_rows)
    bank_shape = (bank_rows, SUB)
    share = small_call(bank_kernel, jax.ShapeDtypeStruct(bank_shape, F32), (flat, grads, *over_z), theirs)
    core_share = swap(share, "core")
    half_shape = jax.ShapeDtypeStruct(bank_shape, BF16)
    add_up = functools.partial(round_kernel, 1.0 / math.sqrt(TOKENS))
    share = small_call(add_up, half_shape, (share, core_share))
    pair_share = swap(share, "pair")
    add_up = functools.partial(round_kernel, 1.0)
    share = small_call(add_up, half_shape, (share, pair_share))
    other_share = lax.ppermute(share, "section", [(0, 1), (1, 0)])
    bank_grad = small_call(add_up, jax.ShapeDtypeStruct(bank_shape, F32), (share, other_share), inner)
    return (result[None], bank_grad)


def solution(mesh):
    fine = Mesh(
        mesh.devices.reshape(2, RING, RING, 2, 2), ("section", "z", "y", "pair", "core")
    )
    rows, columns = ("z", "y"), ("pair", "core")
    return jax.shard_map(
        shards,
        mesh=fine,
        in_specs=(
            P("section", rows, columns),
            P("section", rows, columns),
            P("section", columns),
            P("section", rows, columns),
            P(),
            P("section", None, None, None),
            P("section", None, None, None),
            P(rows, columns),
        ),
        out_specs=(P("section", rows, columns), P()),
        check_vma=False,
    )
```

```python
import functools
import math

import jax
import jax.numpy as jnp
from jax import lax
from jax.experimental import pallas as pl
from jax.experimental.pallas import tpu as pltpu
from jax.sharding import Mesh, PartitionSpec as P

MODEL_WIDTH = 8192
RANK = 4
SUB = 256
TOKENS = 4096
RING = 4
LANES = 128

epsilon = 1e-06
HIGH = lax.Precision.HIGHEST
F32 = jnp.float32
BF16 = jnp.bfloat16
ANY = pl.BlockSpec(memory_space=pl.ANY)
SMEM = pl.BlockSpec(memory_space=pltpu.SMEM)
VMEM = pl.BlockSpec(memory_space=pltpu.VMEM)
HBM = pl.BlockSpec(memory_space=pltpu.HBM)
BIG = 48 * 1024 * 1024
MEDIUM = 20 * 1024 * 1024
SMALL = 12 * 1024 * 1024
LIGHT = pl.CostEstimate(flops=0, bytes_accessed=2 ** 20, transcendentals=0)


def ring_route(distance, sections=(0, 1)):
    return [(s * RING + i, s * RING + (i + distance) % RING) for s in sections for i in range(RING)]


def ring_move(block, axis, distance, sections=(0, 1)):
    return lax.ppermute(block, ("section", axis), ring_route(distance, sections))


def swap(block, axis, sections=(0, 1)):
    pairs = [(s * 2 + i, s * 2 + 1 - i) for s in sections for i in range(2)]
    return lax.ppermute(block, ("section", axis), pairs)


def after(value, earlier):
    return lax.optimization_barrier((value, earlier))[0]


def in_order(kernel, operands, extra):
    return lambda *refs: kernel(*refs[:operands], *refs[operands + extra:])


def compose(index_layer, weight_layer, rows):
    columns = lax.broadcasted_iota(jnp.int32, (1, 1, 1, 1, rows), 4)
    onehot = (index_layer[..., None] == columns).astype(F32)
    return jnp.sum(onehot * weight_layer[..., None], axis=3)


def two_halves(value):
    high = value.astype(BF16)
    return jnp.concatenate([high, (value - high.astype(F32)).astype(BF16)], axis=0)


def activation_gradient(incoming_ref, preact_ref):
    value = preact_ref[...].astype(F32)
    sig = jax.nn.sigmoid(value)
    slope = sig * (1.0 + value * (1.0 - sig))
    return (incoming_ref[...].astype(F32) * slope).astype(BF16)


def dz_kernel(incoming_ref, preact_ref, b_ref, dz_ref, mixed_ref):
    dz = activation_gradient(incoming_ref, preact_ref)
    dz_ref[...] = dz
    both = lax.dot_general(b_ref[...], dz, (((1,), (1,)), ((), ())), preferred_element_type=F32)
    mixed_ref[...] = both[:RANK] + both[RANK:]


def first_kernel(where_ref, incoming_ref, preact_ref, weight_ref, out_ref, incoming, preact, sem):
    def fetch(*pairs):
        copies = [pltpu.make_async_copy(*pair, sem.at[i]) for i, pair in enumerate(pairs)]
        for copy in copies:
            copy.start()
        for copy in copies:
            copy.wait()

    @pl.when(where_ref[3] == 1)
    def _():
        fetch((incoming_ref, incoming), (preact_ref, preact))
        out_ref[:incoming.shape[0]] = activation_gradient(incoming, preact)

    @pl.when(where_ref[3] == 0)
    def _():
        fetch((weight_ref, out_ref))


def make_first(where, incoming, preact, weight):
    return pl.pallas_call(
        first_kernel,
        in_specs=[SMEM, HBM, HBM, HBM],
        out_specs=VMEM,
        out_shape=jax.ShapeDtypeStruct(weight.shape, BF16),
        scratch_shapes=[
            pltpu.VMEM(incoming.shape, BF16),
            pltpu.VMEM(incoming.shape, BF16),
            pltpu.SemaphoreType.DMA((2,)),
        ],
        compiler_params=pltpu.CompilerParams(vmem_limit_bytes=MEDIUM),
        cost_estimate=LIGHT,
    )(where, incoming, preact, weight)


def join_kernel(wanted, parts, where_ref, *refs):
    sources, out_ref, held, sem, out_sem = refs[:len(parts)], *refs[-4:]

    @pl.when(where_ref[3] == wanted)
    def _():
        start = 0
        steps = []
        for i, (first, rows) in enumerate(parts):
            here = held.at[pl.ds(start, rows)]
            fetch = pltpu.make_async_copy(sources[i].at[pl.ds(first, rows)], here, sem.at[i])
            store = pltpu.make_async_copy(here, out_ref.at[pl.ds(start, rows)], out_sem.at[i])
            steps.append((fetch, store))
            start += rows
        for fetch, _ in steps:
            fetch.start()
        for fetch, store in steps:
            fetch.wait()
            store.start()
        for _, store in steps:
            store.wait()


def join(where, wanted, arrays, parts, *earlier):
    rows, width = sum(count for _, count in parts), arrays[0].shape[1]
    return pl.pallas_call(
        in_order(functools.partial(join_kernel, wanted, parts), 1 + len(arrays), len(earlier)),
        in_specs=[SMEM] + [ANY] * (len(arrays) + len(earlier)),
        out_specs=HBM,
        out_shape=jax.ShapeDtypeStruct((rows, width), BF16),
        scratch_shapes=[
            pltpu.VMEM((rows, width), BF16),
            pltpu.SemaphoreType.DMA((len(arrays),)),
            pltpu.SemaphoreType.DMA((len(arrays),)),
        ],
        compiler_params=pltpu.CompilerParams(vmem_limit_bytes=SMALL),
        cost_estimate=LIGHT,
    )(where, *arrays, *earlier)


def halves_kernel(after_ref, before_ref, low_ref, high_ref, sem):
    half = low_ref.shape[0]
    low = pltpu.make_async_copy(after_ref.at[pl.ds(0, half)], low_ref, sem.at[0])
    high = pltpu.make_async_copy(before_ref.at[pl.ds(half, half)], high_ref, sem.at[1])
    low.start()
    high.start()
    low.wait()
    high.wait()


def gather_ring(block, axis, *earlier):
    rows, width = block.shape
    after = ring_move(block, axis, -1)
    before = ring_move(block, axis, 1)
    low, high = pl.pallas_call(
        in_order(halves_kernel, 2, len(earlier)),
        in_specs=[ANY, ANY] + [ANY] * len(earlier),
        out_specs=[VMEM, VMEM],
        out_shape=[jax.ShapeDtypeStruct((rows // 2, width), BF16)] * 2,
        scratch_shapes=[pltpu.SemaphoreType.DMA((2,))],
        compiler_params=pltpu.CompilerParams(vmem_limit_bytes=SMALL),
        cost_estimate=LIGHT,
    )(after, before, *earlier)
    return block, after, ring_move(low, axis, -1), ring_move(high, axis, 1), before


def make_dz(incoming, preact, b_both, c, *earlier):
    rows, width = incoming.shape
    return pl.pallas_call(
        in_order(dz_kernel, 3, len(earlier)),
        grid=(1,),
        in_specs=[
            pl.BlockSpec((rows, width), lambda i: (0, 0)),
            pl.BlockSpec((rows, width), lambda i: (c, 0)),
            pl.BlockSpec((2 * RANK, width), lambda i: (0, 0)),
        ]
        + [ANY] * len(earlier),
        out_specs=[
            pl.BlockSpec((rows, width), lambda i: (0, 0)),
            pl.BlockSpec((RANK, rows), lambda i: (0, 0)),
        ],
        out_shape=[
            jax.ShapeDtypeStruct((rows, width), BF16),
            jax.ShapeDtypeStruct((RANK, rows), F32),
        ],
        compiler_params=pltpu.CompilerParams(vmem_limit_bytes=MEDIUM),
        cost_estimate=LIGHT,
    )(incoming, preact, b_both, *earlier)


def top_product_kernel(rows, where_ref, *refs):
    dz_refs, w_refs = refs[:4], refs[4:9]
    mine_ref, theirs_ref, send_ref, dz_all, w_all, dz_sem, w_sem = refs[9:]

    @pl.when(where_ref[3] == 1)
    def _():
        copies = [
            pltpu.make_async_copy(ref.at[pl.ds(0, rows)], dz_all.at[pl.ds(i * rows, rows)], dz_sem.at[i])
            for i, ref in enumerate(dz_refs)
        ]
        for copy in copies:
            copy.start()
        own, after, far_low, far_high, before = w_refs
        half = far_low.shape[0]
        pltpu.make_async_copy(own, w_all.at[0], w_sem.at[0]).start()
        pltpu.make_async_copy(after, w_all.at[1], w_sem.at[1]).start()
        pltpu.make_async_copy(far_low, w_all.at[2, pl.ds(0, half)], w_sem.at[2]).start()
        pltpu.make_async_copy(far_high, w_all.at[2, pl.ds(half, half)], w_sem.at[2]).start()
        pltpu.make_async_copy(before, w_all.at[3], w_sem.at[3]).start()
        for copy in copies:
            copy.wait()
        z, place = where_ref[0], where_ref[1]

        @pl.loop(0, RING)
        def _(i):
            pltpu.make_async_copy(own, w_all.at[i], w_sem.at[i]).wait()
            value = lax.dot_general(
                dz_all[...], w_all[i], (((1,), (1,)), ((), ())), preferred_element_type=F32
            ).astype(BF16)
            target = lax.rem(z + i, RING)
            own_core = lax.rem(target, 2) == lax.rem(place, 2)
            far = jnp.where(target // 2 == place // 2, 0, 1)

            @pl.when(jnp.logical_and(own_core, far == 0))
            def _():
                mine_ref[...] = value

            @pl.when(jnp.logical_and(own_core, far == 1))
            def _():
                theirs_ref[...] = value

            @pl.when(jnp.logical_not(own_core))
            def _():
                send_ref[far] = value


def top_product(where, rows, dz_pieces, w_pieces, *earlier):
    wide, width = w_pieces[0].shape
    return pl.pallas_call(
        in_order(functools.partial(top_product_kernel, rows), 10, len(earlier)),
        in_specs=[SMEM] + [HBM] * 9 + [ANY] * len(earlier),
        out_specs=[VMEM, VMEM, VMEM],
        out_shape=[jax.ShapeDtypeStruct((RING * rows, wide), BF16)] * 2
        + [jax.ShapeDtypeStruct((2, RING * rows, wide), BF16)],
        scratch_shapes=[
            pltpu.VMEM((RING * rows, width), BF16),
            pltpu.VMEM((RING, wide, width), BF16),
            pltpu.SemaphoreType.DMA((4,)),
            pltpu.SemaphoreType.DMA((RING,)),
        ],
        compiler_params=pltpu.CompilerParams(vmem_limit_bytes=36 * 1024 * 1024),
        cost_estimate=pl.CostEstimate(
            flops=2 * RING * RING * rows * wide * width, bytes_accessed=2 ** 24, transcendentals=0
        ),
    )(where, *dz_pieces, *w_pieces, *earlier)


def low_plan(shard, wide):
    copies, blocks = [], []

    def take(array, row, rows, *names):
        at = sum(rows for *_, rows in copies)
        copies.append((array, row, at, rows))
        blocks.extend(names)

    for base, step in ((0, lambda d, h: (d, 0, h)), (4, lambda d, h: (0, d, h))):
        if base == 0:
            take(0, 0, shard, step(0, 0), step(0, 1))
        take(base + 1, 0, shard, step(1, 0), step(1, 1))
        take(base + 2, 0, wide, step(2, 0))
        take(base + 3, 0, wide, step(2, 1))
        take(base + 4, 0, shard, step(3, 0), step(3, 1))
    corner, y_pair, z_pair = 9, {1: 10, 3: 11}, {1: 12, 3: 13}
    take(corner, 0, shard, (2, 2, 0), (2, 2, 1))
    for d in (1, 3):
        take(y_pair[d], 0, shard, (2, d, 0), (2, d, 1))
        take(z_pair[d], 0, shard, (d, 2, 0), (d, 2, 1))
    slim = 3 * wide // 8
    rest = shard - slim
    for i, d in enumerate((1, 3)):
        for j, e in enumerate((1, 3)):
            take(y_pair[e], shard + i * slim, slim)
            take(z_pair[d], shard + j * rest, rest, (d, e, 0), (d, e, 1))
    return copies, blocks


def low_product_kernel(plan, where_ref, table_ref, dz_ref, *refs):
    count = len(refs) - 7
    w_refs = refs[:count]
    mine_ref, theirs_ref, send_ref, dz_all, w_all, dz_sem, sem = refs[count:]
    steps, deep = w_all.shape[0], w_all.shape[1]
    wide = deep // 2

    @pl.when(where_ref[3] == 0)
    def _():
        dz_copy = pltpu.make_async_copy(dz_ref, dz_all, dz_sem)
        dz_copy.start()
        for array, row, at, rows in plan:
            while rows:
                part = min(rows, deep - at % deep)
                pltpu.make_async_copy(
                    w_refs[array].at[pl.ds(row, part)],
                    w_all.at[at // deep, pl.ds(at % deep, part)],
                    sem.at[at // deep],
                ).start()
                row, at, rows = row + part, at + part, rows - part
        dz_copy.wait()

        @pl.loop(0, steps)
        def _(step):
            pltpu.make_async_copy(w_refs[0], w_all.at[step], sem.at[step]).wait()
            value = lax.dot_general(
                dz_all[...], w_all[step], (((1,), (1,)), ((), ())), preferred_element_type=F32
            ).astype(BF16)
            for k in range(2):
                entry = table_ref[2 * step + k]
                columns = pl.ds(pl.multiple_of(lax.rem(entry, 2 * RING) * wide, wide), wide)
                far = lax.rem(entry // (2 * RING), 2)
                block = value[:, k * wide:(k + 1) * wide]

                @pl.when(entry < 2 * RING)
                def _():
                    mine_ref[:, columns] = block

                @pl.when(jnp.logical_and(entry >= 2 * RING, entry < 4 * RING))
                def _():
                    theirs_ref[:, columns] = block

                @pl.when(entry >= 4 * RING)
                def _():
                    send_ref[far, :, columns] = block


def low_product(where, z, y, place, dz, w_pieces, *earlier):
    rows, width = dz.shape
    shard = w_pieces[0].shape[0]
    wide = shard // 2
    copies, blocks = low_plan(shard, wide)
    steps = [jnp.array(column, jnp.int32) for column in zip(*blocks)]
    target = (z + steps[0]) % RING
    column = (y + steps[1]) % RING * 2 + steps[2]
    other_core = (target % 2 != place % 2).astype(jnp.int32)
    other_pair = (target // 2 != place // 2).astype(jnp.int32)
    table = (other_core * 2 + other_pair) * 2 * RING + column
    return pl.pallas_call(
        in_order(functools.partial(low_product_kernel, copies), 3 + len(w_pieces), len(earlier)),
        in_specs=[SMEM, SMEM, HBM] + [HBM] * len(w_pieces) + [ANY] * len(earlier),
        out_specs=[VMEM, VMEM, VMEM],
        out_shape=[jax.ShapeDtypeStruct((rows, 2 * RING * wide), BF16)] * 2
        + [jax.ShapeDtypeStruct((2, rows, 2 * RING * wide), BF16)],
        scratch_shapes=[
            pltpu.VMEM((rows, width), BF16),
            pltpu.VMEM((RING * RING, shard, width), BF16),
            pltpu.SemaphoreType.DMA,
            pltpu.SemaphoreType.DMA((RING * RING,)),
        ],
        compiler_params=pltpu.CompilerParams(vmem_limit_bytes=BIG),
        cost_estimate=pl.CostEstimate(
            flops=16 * RING * rows * wide * width, bytes_accessed=2 ** 25, transcendentals=0
        ),
    )(where, table, dz, *w_pieces, *earlier)


def add_kernel(keep_ref, got_ref, out_ref):
    out_ref[...] = (keep_ref[...].astype(F32) + got_ref[0].astype(F32)).astype(BF16)


def add_theirs(keep, got):
    rows, wide = keep.shape
    whole = pl.BlockSpec((rows, wide), lambda i: (0, 0))
    return pl.pallas_call(
        add_kernel,
        grid=(1,),
        in_specs=[whole, pl.BlockSpec((1, rows, wide), lambda i: (1, 0, 0))],
        out_specs=whole,
        out_shape=jax.ShapeDtypeStruct((rows, wide), BF16),
        compiler_params=pltpu.CompilerParams(vmem_limit_bytes=SMALL),
        cost_estimate=LIGHT,
    )(keep, got)


def total_kernel(keep_ref, got_ref, other_ref, *out_refs):
    rows = out_refs[0].shape[0]
    for i, ref in enumerate(out_refs):
        part = pl.ds(i * rows, rows)
        ref[...] = (
            keep_ref[part].astype(F32) + got_ref[0, part].astype(F32) + other_ref[part].astype(F32)
        ).astype(BF16)


def add_mine(keep, got, other, *earlier):
    rows, wide = keep.shape
    whole = pl.BlockSpec((rows, wide), lambda i: (0, 0))
    return pl.pallas_call(
        in_order(total_kernel, 3, len(earlier)),
        grid=(1,),
        in_specs=[whole, pl.BlockSpec((1, rows, wide), lambda i: (0, 0, 0)), whole] + [ANY] * len(earlier),
        out_specs=[pl.BlockSpec((rows // RING, wide), lambda i: (0, 0))] * RING,
        out_shape=[jax.ShapeDtypeStruct((rows // RING, wide), BF16)] * RING,
        compiler_params=pltpu.CompilerParams(vmem_limit_bytes=SMALL),
        cost_estimate=LIGHT,
    )(keep, got, other, *earlier)


def as_row(column):
    square = jnp.broadcast_to(column, (column.shape[0], LANES))
    return jnp.transpose(square)[:8]


def as_column(row):
    square = jnp.concatenate([row] * (LANES // 8), axis=0)
    return jnp.transpose(square)[:, :1]


def scaled_kernel(where_ref, own, after, far, before, mixed_ref, a_ref, gain_ref, hidden_ref, scale_ref, scaled_ref, inner_ref):
    wide = own.shape[1]
    mixed = mixed_ref[...]
    inner = jnp.zeros((own.shape[0], 1), F32)
    for r, piece in enumerate((own, after, far, before)):
        at = pl.ds(pl.multiple_of(lax.rem(where_ref[2] + r, RING) * wide, wide), wide)
        low_rank = lax.dot_general(
            mixed, a_ref[:, at], (((0,), (0,)), ((), ())), precision=HIGH, preferred_element_type=F32
        )
        scaled = gain_ref[:, at] * (piece[...].astype(F32) + low_rank)
        scaled_ref[:, at] = scaled.astype(BF16)
        inner = inner + jnp.sum(scaled * hidden_ref[:, at].astype(F32), axis=1, keepdims=True)
    inner_ref[...] = as_row(inner * scale_ref[...])


def make_scaled(where, pieces, mixed, a_local, gain, hidden, scale):
    rows, width = hidden.shape
    return pl.pallas_call(
        scaled_kernel,
        in_specs=[SMEM] + [VMEM] * 9,
        out_specs=[VMEM, VMEM],
        out_shape=[jax.ShapeDtypeStruct((rows, width), BF16), jax.ShapeDtypeStruct((8, rows), F32)],
        compiler_params=pltpu.CompilerParams(vmem_limit_bytes=MEDIUM),
        cost_estimate=LIGHT,
    )(where, *pieces, mixed, a_local, gain, hidden, scale)


def low_scaled_kernel(keep_ref, got_ref, other_ref, mixed_ref, a_ref, gain_ref, hidden_ref, scale_ref, scaled_ref, inner_ref):
    low_rank = lax.dot_general(
        mixed_ref[...], a_ref[...], (((0,), (0,)), ((), ())), precision=HIGH, preferred_element_type=F32
    )
    total = keep_ref[...].astype(F32) + got_ref[0].astype(F32) + other_ref[...].astype(F32)
    scaled = gain_ref[...] * (total + low_rank)
    scaled_ref[...] = scaled.astype(BF16)
    inner = jnp.sum(scaled * hidden_ref[...].astype(F32), axis=1, keepdims=True)
    inner_ref[...] = as_row(inner * scale_ref[...])


def low_scaled(keep, got, other, mixed, a_local, gain, hidden, scale):
    rows, width = hidden.shape
    whole = lambda shape: pl.BlockSpec(shape, lambda i: (0, 0))
    mine = pl.BlockSpec((1, rows, width), lambda i: (0, 0, 0))
    return pl.pallas_call(
        low_scaled_kernel,
        grid=(1,),
        in_specs=[
            whole((rows, width)), mine, whole((rows, width)), whole((RANK, rows)), whole((RANK, width)),
            whole((1, width)), whole((rows, width)), whole((rows, 1)),
        ],
        out_specs=[whole((rows, width)), whole((8, rows))],
        out_shape=[jax.ShapeDtypeStruct((rows, width), BF16), jax.ShapeDtypeStruct((8, rows), F32)],
        compiler_params=pltpu.CompilerParams(vmem_limit_bytes=MEDIUM),
        cost_estimate=LIGHT,
    )(keep, got, other, mixed, a_local, gain, hidden, scale)


def hidden_gradient(scaled_ref, inner_ref, hidden_ref, scale_ref, incoming_ref):
    scale = scale_ref[...]
    pull = as_column(inner_ref[...]) * scale / MODEL_WIDTH
    return (
        incoming_ref[...].astype(F32)
        + scale * (scaled_ref[...].astype(F32) - hidden_ref[...].astype(F32) * pull)
    ).astype(BF16)


def top_kernel(scaled_ref, inner_ref, hidden_ref, scale_ref, incoming_ref, out_ref):
    out_ref[...] = hidden_gradient(scaled_ref, inner_ref, hidden_ref, scale_ref, incoming_ref)


def low_kernel(
    where_ref, scaled_ref, inner_ref, hidden_ref, scale_ref, incoming_ref, share_ref, other_ref, top_ref,
    out_ref, bank_ref, sem,
):
    bank_ref[...] = share_ref[...].astype(F32) + other_ref[...].astype(F32)

    @pl.when(where_ref[3] == 0)
    def _():
        out_ref[...] = hidden_gradient(scaled_ref, inner_ref, hidden_ref, scale_ref, incoming_ref)

    @pl.when(where_ref[3] == 1)
    def _():
        copy = pltpu.make_async_copy(top_ref, out_ref, sem)
        copy.start()
        copy.wait()


def finish_specs(rows, width, c):
    whole = lambda shape: pl.BlockSpec(shape, lambda i: (0, 0))
    return [
        whole((rows, width)),
        whole((8, rows)),
        pl.BlockSpec((rows, width), lambda i: (c, 0)),
        pl.BlockSpec((rows, 1), lambda i: (c, 0)),
    ]


def finish_top(scaled, inner, hidden, scale, grad_top, c):
    rows, width = scaled.shape
    return pl.pallas_call(
        top_kernel,
        grid=(1,),
        in_specs=finish_specs(rows, width, c) + [pl.BlockSpec((rows, width), lambda i: (c, 0))],
        out_specs=pl.BlockSpec((rows, width), lambda i: (0, 0)),
        out_shape=jax.ShapeDtypeStruct((rows, width), BF16),
        compiler_params=pltpu.CompilerParams(vmem_limit_bytes=MEDIUM),
        cost_estimate=LIGHT,
    )(scaled, inner, hidden, scale, grad_top)


def finish_low(where, scaled, inner, hidden, scale, incoming, share, other, top):
    rows, width = scaled.shape
    block = pl.BlockSpec((rows, width), lambda i: (0, 0))
    bank = pl.BlockSpec(share.shape, lambda i: (0, 0))
    return pl.pallas_call(
        low_kernel,
        grid=(1,),
        in_specs=[SMEM] + finish_specs(rows, width, 0) + [block, bank, bank, HBM],
        out_specs=[block, bank],
        out_shape=[jax.ShapeDtypeStruct((rows, width), BF16), jax.ShapeDtypeStruct(share.shape, F32)],
        scratch_shapes=[pltpu.SemaphoreType.DMA],
        compiler_params=pltpu.CompilerParams(vmem_limit_bytes=MEDIUM),
        cost_estimate=LIGHT,
    )(where, scaled, inner, hidden, scale, incoming, share, other, top)


def grads_kernel(where_ref, hidden_ref, scale_ref, gain_ref, projected_ref, *refs):
    out_ref = refs[-1]
    top = where_ref[3] == 1
    count = (len(refs) - 2) // 3
    total_a, total_b = 0.0, 0.0
    for c in range(count):
        low_dz, top_mixed, low_mixed = [refs[1 + k * count + c] for k in range(3)]
        rows = pl.ds(c * low_dz.shape[0], low_dz.shape[0])
        dz = jnp.where(top, refs[0][rows], low_dz[...])
        mixed = jnp.where(top, top_mixed[...], low_mixed[...])
        x = (hidden_ref[rows].astype(F32) * scale_ref[rows] * gain_ref[...]).astype(BF16)
        projected = projected_ref[:, rows]

        def both(left, right):
            value = lax.dot_general(
                two_halves(left), right, (((1,), (0,)), ((), ())), preferred_element_type=F32
            )
            return value[:RANK] + value[RANK:]

        total_a = total_a + both(mixed, x)
        total_b = total_b + both(projected, dz)
    out_ref[...] = jnp.concatenate([total_a, total_b], axis=0)


def make_grads(where, hidden, scale, gain, projected, lists, *earlier):
    arrays = [array for arrays in lists for array in arrays]
    return pl.pallas_call(
        in_order(grads_kernel, 5 + len(arrays), len(earlier)),
        in_specs=[SMEM] + [VMEM] * (4 + len(arrays)) + [ANY] * len(earlier),
        out_specs=VMEM,
        out_shape=jax.ShapeDtypeStruct((2 * RANK, hidden.shape[1]), F32),
        compiler_params=pltpu.CompilerParams(vmem_limit_bytes=MEDIUM),
        cost_estimate=LIGHT,
    )(where, hidden, scale, gain, projected, *arrays, *earlier)


def ring_total(value, moved):
    after, far, before = moved
    return (value[...] + far[...]) + (after[...] + before[...])


def ring_kernel(value, after, far, before, out_ref):
    out_ref[...] = ring_total(value, (after, far, before))


def bank_kernel(mixing_ref, value, after, far, before, out_ref):
    total = ring_total(value, (after, far, before))
    count = total.shape[1] // SUB
    pieces = jnp.concatenate([total[:, j * SUB:(j + 1) * SUB] for j in range(count)], axis=0)
    out_ref[...] = lax.dot_general(
        mixing_ref[...], pieces, (((0,), (0,)), ((), ())), precision=HIGH, preferred_element_type=F32
    )


def round_kernel(factor, left, right, out_ref):
    out_ref[...] = ((left[...].astype(F32) + right[...].astype(F32)) * factor).astype(out_ref.dtype)


def small_call(kernel, out, operands, *earlier):
    return pl.pallas_call(
        in_order(kernel, len(operands), len(earlier)),
        in_specs=[VMEM] * len(operands) + [ANY] * len(earlier),
        out_specs=VMEM,
        out_shape=out,
        compiler_params=pltpu.CompilerParams(vmem_limit_bytes=SMALL),
        cost_estimate=LIGHT,
    )(*operands, *earlier)


def ring_moves(value, axis):
    return [ring_move(value, axis, d) for d in (-1, 2, 1)]


def shards(hidden_in, preact, norm_gain, weight, bank, mix_index, mix_weight, grad_top):
    section = lax.axis_index("section")
    z, y = lax.axis_index("z"), lax.axis_index("y")
    place = lax.axis_index("pair") * 2 + lax.axis_index("core")
    where = jnp.stack([z, place, y, section]).astype(jnp.int32)
    tensor = ("pair", "core")
    bank_rows = bank.shape[0]

    tokens, local_width = grad_top.shape
    seg_local = local_width // SUB
    seg_row = MODEL_WIDTH // SUB
    own_weight = weight[0]
    shard = own_weight.shape[0]
    half = shard // 2

    first = make_first(where, grad_top, preact[0], own_weight)
    hidden, preact = hidden_in[0], preact[0]

    def local_pieces(array):
        array = array.reshape(2, RANK, seg_row, 2)
        return lax.dynamic_slice_in_dim(array, place * seg_local, seg_local, 2)

    mixing = compose(local_pieces(mix_index[0]), local_pieces(mix_weight[0]), bank_rows)
    mixing = mixing.reshape(2, RANK * seg_local, bank_rows)
    factors = jnp.einsum("fnb,bs->fns", mixing, bank, precision=HIGH)
    a_local = factors[0].reshape(RANK, local_width)
    b_both = two_halves(factors[1].reshape(RANK, local_width))

    hidden_f = hidden.astype(F32)
    sums = lax.psum(
        jnp.concatenate(
            [
                jnp.sum(hidden_f * hidden_f, axis=1)[None],
                jnp.dot(a_local, (hidden_f * norm_gain).T, precision=HIGH),
                jnp.dot(factors[1].reshape(RANK, local_width), first[:tokens].astype(F32).T, precision=HIGH),
            ],
            axis=0,
        ),
        tensor,
    )
    scale_row = lax.rsqrt(sums[:1] / MODEL_WIDTH + epsilon)
    projected = sums[1:1 + RANK] * scale_row
    scale = scale_row.reshape(tokens, 1)
    top_mixed = sums[1 + RANK:]

    z_ring = gather_ring(own_weight, "z", scale)
    y_ring = gather_ring(first, "y", scale)

    _, z_after, z_far_low, z_far_high, z_before = z_ring
    _, y_after, y_far_low, y_far_high, y_before = y_ring
    slim = 3 * half // 8
    rest = shard - slim
    corner = join(where, 0, (z_far_low, z_far_high), ((0, half), (0, half)), y_far_high)
    corner = ring_move(corner, "y", 2, (0,))

    dz_pieces = (y_ring[0], y_ring[1], y_ring[2], y_ring[4])
    mine, keep, send = top_product(where, tokens, dz_pieces, z_ring, y_far_high)
    got = swap(send, "core", (1,))
    theirs = add_theirs(keep, got)
    other = swap(theirs, "pair", (1,))
    along_z = join(
        where, 0, (y_far_low, y_far_high, y_after, y_before),
        ((0, half), (0, half), (slim, rest), (slim, rest)), theirs,
    )
    z_pair = (ring_move(along_z, "z", -1), ring_move(along_z, "z", 1))
    own, to_after, to_far, to_before = add_mine(mine, got, other, corner)
    from_before = ring_move(to_after, "y", 1, (1,))
    from_far = ring_move(to_far, "y", 2, (1,))
    from_after = ring_move(to_before, "y", -1, (1,))
    along_y = join(
        where, 0, (z_far_low, z_far_high, z_after, z_before),
        ((0, half), (0, half), (0, slim), (0, slim)), theirs,
    )
    along_y = after(along_y, (from_before, from_far, from_after))
    y_pair = (ring_move(along_y, "y", -1, (0,)), ring_move(along_y, "y", 1, (0,)))
    w_pieces = (*z_ring, *y_ring[1:], corner, *y_pair, *z_pair)

    pieces = (own, from_after, from_far, from_before)
    scaled, inner = make_scaled(where, pieces, top_mixed, a_local, norm_gain, hidden, scale)
    top_grad = finish_top(scaled, lax.psum(inner, tensor), hidden, scale, grad_top, 0)
    low_in = lax.ppermute(top_grad, "section", [(1, 0)])

    low_dz, part = make_dz(low_in, preact, b_both, 0)
    low_mixed = lax.psum(part, tensor)
    mine, keep, send = low_product(where, z, y, place, low_dz, w_pieces, low_mixed)
    got = swap(send, "core", (0,))
    theirs = add_theirs(keep, got)
    other = swap(theirs, "pair", (0,))
    scaled, inner = low_scaled(mine, got, other, low_mixed, a_local, norm_gain, hidden, scale)
    inner = lax.psum(inner, tensor)
    grads = make_grads(
        where, hidden, scale, norm_gain, projected, ([first], [low_dz], [top_mixed], [low_mixed])
    )
    over_y = ring_moves(grads, "y")
    grads = small_call(ring_kernel, jax.ShapeDtypeStruct(grads.shape, F32), (grads, *over_y), send)
    over_z = ring_moves(grads, "z")
    flat = mixing.reshape(2, RANK, seg_local, bank_rows).transpose(2, 0, 1, 3)
    flat = flat.reshape(2 * RANK * seg_local, bank_rows)
    bank_shape = (bank_rows, SUB)
    share = small_call(bank_kernel, jax.ShapeDtypeStruct(bank_shape, F32), (flat, grads, *over_z), theirs)
    core_share = swap(share, "core")
    half_shape = jax.ShapeDtypeStruct(bank_shape, BF16)
    add_up = functools.partial(round_kernel, 1.0 / math.sqrt(TOKENS))
    share = small_call(add_up, half_shape, (share, core_share))
    pair_share = swap(share, "pair")
    add_up = functools.partial(round_kernel, 1.0)
    share = small_call(add_up, half_shape, (share, pair_share))
    other_share = lax.ppermute(share, "section", [(0, 1), (1, 0)])
    result, bank_grad = finish_low(
        where, scaled, inner, hidden, scale, low_in, share, other_share, top_grad
    )
    return (result[None], bank_grad)


def solution(mesh):
    fine = Mesh(
        mesh.devices.reshape(2, RING, RING, 2, 2), ("section", "z", "y", "pair", "core")
    )
    rows, columns = ("z", "y"), ("pair", "core")
    return jax.shard_map(
        shards,
        mesh=fine,
        in_specs=(
            P("section", rows, columns),
            P("section", rows, columns),
            P("section", columns),
            P("section", rows, columns),
            P(),
            P("section", None, None, None),
            P("section", None, None, None),
            P(rows, columns),
        ),
        out_specs=(P("section", rows, columns), P()),
        check_vma=False,
    )
```

```python
import functools
import math

import jax
import jax.numpy as jnp
from jax import lax
from jax.experimental import pallas as pl
from jax.experimental.pallas import tpu as pltpu
from jax.sharding import Mesh, PartitionSpec as P

MODEL_WIDTH = 8192
RANK = 4
SUB = 256
TOKENS = 4096
RING = 4
LANES = 128

epsilon = 1e-06
HIGH = lax.Precision.HIGHEST
F32 = jnp.float32
BF16 = jnp.bfloat16
ANY = pl.BlockSpec(memory_space=pl.ANY)
SMEM = pl.BlockSpec(memory_space=pltpu.SMEM)
VMEM = pl.BlockSpec(memory_space=pltpu.VMEM)
HBM = pl.BlockSpec(memory_space=pltpu.HBM)
BIG = 48 * 1024 * 1024
MEDIUM = 20 * 1024 * 1024
SMALL = 12 * 1024 * 1024
LIGHT = pl.CostEstimate(flops=0, bytes_accessed=2 ** 20, transcendentals=0)


def ring_route(distance, sections=(0, 1)):
    return [(s * RING + i, s * RING + (i + distance) % RING) for s in sections for i in range(RING)]


def ring_move(block, axis, distance, sections=(0, 1)):
    return lax.ppermute(block, ("section", axis), ring_route(distance, sections))


def swap(block, axis, sections=(0, 1)):
    pairs = [(s * 2 + i, s * 2 + 1 - i) for s in sections for i in range(2)]
    return lax.ppermute(block, ("section", axis), pairs)


def after(value, earlier):
    return lax.optimization_barrier((value, earlier))[0]


def in_order(kernel, operands, extra):
    return lambda *refs: kernel(*refs[:operands], *refs[operands + extra:])


def compose(index_layer, weight_layer, rows):
    columns = lax.broadcasted_iota(jnp.int32, (1, 1, 1, 1, rows), 4)
    onehot = (index_layer[..., None] == columns).astype(F32)
    return jnp.sum(onehot * weight_layer[..., None], axis=3)


def two_halves(value):
    high = value.astype(BF16)
    return jnp.concatenate([high, (value - high.astype(F32)).astype(BF16)], axis=0)


def activation_gradient(incoming_ref, preact_ref):
    value = preact_ref[...].astype(F32)
    sig = jax.nn.sigmoid(value)
    slope = sig * (1.0 + value * (1.0 - sig))
    return (incoming_ref[...].astype(F32) * slope).astype(BF16)


def dz_kernel(incoming_ref, preact_ref, b_ref, dz_ref, mixed_ref):
    dz = activation_gradient(incoming_ref, preact_ref)
    dz_ref[...] = dz
    both = lax.dot_general(b_ref[...], dz, (((1,), (1,)), ((), ())), preferred_element_type=F32)
    mixed_ref[...] = both[:RANK] + both[RANK:]


def first_kernel(where_ref, incoming_ref, preact_ref, weight_ref, out_ref, incoming, preact, sem):
    def fetch(*pairs):
        copies = [pltpu.make_async_copy(*pair, sem.at[i]) for i, pair in enumerate(pairs)]
        for copy in copies:
            copy.start()
        for copy in copies:
            copy.wait()

    @pl.when(where_ref[3] == 1)
    def _():
        fetch((incoming_ref, incoming), (preact_ref, preact))
        out_ref[:incoming.shape[0]] = activation_gradient(incoming, preact)

    @pl.when(where_ref[3] == 0)
    def _():
        fetch((weight_ref, out_ref))


def make_first(where, incoming, preact, weight):
    return pl.pallas_call(
        first_kernel,
        in_specs=[SMEM, HBM, HBM, HBM],
        out_specs=VMEM,
        out_shape=jax.ShapeDtypeStruct(weight.shape, BF16),
        scratch_shapes=[
            pltpu.VMEM(incoming.shape, BF16),
            pltpu.VMEM(incoming.shape, BF16),
            pltpu.SemaphoreType.DMA((2,)),
        ],
        compiler_params=pltpu.CompilerParams(vmem_limit_bytes=MEDIUM),
        cost_estimate=LIGHT,
    )(where, incoming, preact, weight)


def join_kernel(wanted, parts, where_ref, *refs):
    sources, out_ref, held, sem, out_sem = refs[:len(parts)], *refs[-4:]

    @pl.when(where_ref[3] == wanted)
    def _():
        start = 0
        steps = []
        for i, (first, rows) in enumerate(parts):
            here = held.at[pl.ds(start, rows)]
            fetch = pltpu.make_async_copy(sources[i].at[pl.ds(first, rows)], here, sem.at[i])
            store = pltpu.make_async_copy(here, out_ref.at[pl.ds(start, rows)], out_sem.at[i])
            steps.append((fetch, store))
            start += rows
        for fetch, _ in steps:
            fetch.start()
        for fetch, store in steps:
            fetch.wait()
            store.start()
        for _, store in steps:
            store.wait()


def join(where, wanted, arrays, parts, *earlier):
    rows, width = sum(count for _, count in parts), arrays[0].shape[1]
    return pl.pallas_call(
        in_order(functools.partial(join_kernel, wanted, parts), 1 + len(arrays), len(earlier)),
        in_specs=[SMEM] + [ANY] * (len(arrays) + len(earlier)),
        out_specs=HBM,
        out_shape=jax.ShapeDtypeStruct((rows, width), BF16),
        scratch_shapes=[
            pltpu.VMEM((rows, width), BF16),
            pltpu.SemaphoreType.DMA((len(arrays),)),
            pltpu.SemaphoreType.DMA((len(arrays),)),
        ],
        compiler_params=pltpu.CompilerParams(vmem_limit_bytes=SMALL),
        cost_estimate=LIGHT,
    )(where, *arrays, *earlier)


def halves_kernel(after_ref, before_ref, low_ref, high_ref, sem):
    half = low_ref.shape[0]
    low = pltpu.make_async_copy(after_ref.at[pl.ds(0, half)], low_ref, sem.at[0])
    high = pltpu.make_async_copy(before_ref.at[pl.ds(half, half)], high_ref, sem.at[1])
    low.start()
    high.start()
    low.wait()
    high.wait()


def gather_ring(block, axis, *earlier):
    rows, width = block.shape
    after = ring_move(block, axis, -1)
    before = ring_move(block, axis, 1)
    low, high = pl.pallas_call(
        in_order(halves_kernel, 2, len(earlier)),
        in_specs=[ANY, ANY] + [ANY] * len(earlier),
        out_specs=[VMEM, VMEM],
        out_shape=[jax.ShapeDtypeStruct((rows // 2, width), BF16)] * 2,
        scratch_shapes=[pltpu.SemaphoreType.DMA((2,))],
        compiler_params=pltpu.CompilerParams(vmem_limit_bytes=SMALL),
        cost_estimate=LIGHT,
    )(after, before, *earlier)
    return block, after, ring_move(low, axis, -1), ring_move(high, axis, 1), before


def make_dz(incoming, preact, b_both, c, *earlier):
    rows, width = incoming.shape
    return pl.pallas_call(
        in_order(dz_kernel, 3, len(earlier)),
        grid=(1,),
        in_specs=[
            pl.BlockSpec((rows, width), lambda i: (0, 0)),
            pl.BlockSpec((rows, width), lambda i: (c, 0)),
            pl.BlockSpec((2 * RANK, width), lambda i: (0, 0)),
        ]
        + [ANY] * len(earlier),
        out_specs=[
            pl.BlockSpec((rows, width), lambda i: (0, 0)),
            pl.BlockSpec((RANK, rows), lambda i: (0, 0)),
        ],
        out_shape=[
            jax.ShapeDtypeStruct((rows, width), BF16),
            jax.ShapeDtypeStruct((RANK, rows), F32),
        ],
        compiler_params=pltpu.CompilerParams(vmem_limit_bytes=MEDIUM),
        cost_estimate=LIGHT,
    )(incoming, preact, b_both, *earlier)


def top_product_kernel(rows, where_ref, *refs):
    dz_refs, w_refs = refs[:4], refs[4:9]
    mine_ref, theirs_ref, send_ref, dz_all, w_all, dz_sem, w_sem = refs[9:]

    @pl.when(where_ref[3] == 1)
    def _():
        copies = [
            pltpu.make_async_copy(ref.at[pl.ds(0, rows)], dz_all.at[pl.ds(i * rows, rows)], dz_sem.at[i])
            for i, ref in enumerate(dz_refs)
        ]
        for copy in copies:
            copy.start()
        own, after, far_low, far_high, before = w_refs
        half = far_low.shape[0]
        pltpu.make_async_copy(own, w_all.at[0], w_sem.at[0]).start()
        pltpu.make_async_copy(after, w_all.at[1], w_sem.at[1]).start()
        pltpu.make_async_copy(far_low, w_all.at[2, pl.ds(0, half)], w_sem.at[2]).start()
        pltpu.make_async_copy(far_high, w_all.at[2, pl.ds(half, half)], w_sem.at[2]).start()
        pltpu.make_async_copy(before, w_all.at[3], w_sem.at[3]).start()
        for copy in copies:
            copy.wait()
        z, place = where_ref[0], where_ref[1]

        @pl.loop(0, RING)
        def _(i):
            pltpu.make_async_copy(own, w_all.at[i], w_sem.at[i]).wait()
            value = lax.dot_general(
                dz_all[...], w_all[i], (((1,), (1,)), ((), ())), preferred_element_type=F32
            ).astype(BF16)
            target = lax.rem(z + i, RING)
            own_core = lax.rem(target, 2) == lax.rem(place, 2)
            far = jnp.where(target // 2 == place // 2, 0, 1)

            @pl.when(jnp.logical_and(own_core, far == 0))
            def _():
                mine_ref[...] = value

            @pl.when(jnp.logical_and(own_core, far == 1))
            def _():
                theirs_ref[...] = value

            @pl.when(jnp.logical_not(own_core))
            def _():
                send_ref[far] = value


def top_product(where, rows, dz_pieces, w_pieces, *earlier):
    wide, width = w_pieces[0].shape
    return pl.pallas_call(
        in_order(functools.partial(top_product_kernel, rows), 10, len(earlier)),
        in_specs=[SMEM] + [HBM] * 9 + [ANY] * len(earlier),
        out_specs=[VMEM, VMEM, VMEM],
        out_shape=[jax.ShapeDtypeStruct((RING * rows, wide), BF16)] * 2
        + [jax.ShapeDtypeStruct((2, RING * rows, wide), BF16)],
        scratch_shapes=[
            pltpu.VMEM((RING * rows, width), BF16),
            pltpu.VMEM((RING, wide, width), BF16),
            pltpu.SemaphoreType.DMA((4,)),
            pltpu.SemaphoreType.DMA((RING,)),
        ],
        compiler_params=pltpu.CompilerParams(vmem_limit_bytes=36 * 1024 * 1024),
        cost_estimate=pl.CostEstimate(
            flops=2 * RING * RING * rows * wide * width, bytes_accessed=2 ** 24, transcendentals=0
        ),
    )(where, *dz_pieces, *w_pieces, *earlier)


def low_plan(shard, wide):
    copies, blocks = [], []

    def take(array, row, rows, *names):
        at = sum(rows for *_, rows in copies)
        copies.append((array, row, at, rows))
        blocks.extend(names)

    for base, step in ((0, lambda d, h: (d, 0, h)), (4, lambda d, h: (0, d, h))):
        if base == 0:
            take(0, 0, shard, step(0, 0), step(0, 1))
        take(base + 1, 0, shard, step(1, 0), step(1, 1))
        take(base + 2, 0, wide, step(2, 0))
        take(base + 3, 0, wide, step(2, 1))
        take(base + 4, 0, shard, step(3, 0), step(3, 1))
    corner, y_pair, z_pair = 9, {1: 10, 3: 11}, {1: 12, 3: 13}
    take(corner, 0, shard, (2, 2, 0), (2, 2, 1))
    for d in (1, 3):
        take(y_pair[d], 0, shard, (2, d, 0), (2, d, 1))
        take(z_pair[d], 0, shard, (d, 2, 0), (d, 2, 1))
    slim = 112
    rest = shard - slim
    for i, d in enumerate((1, 3)):
        for j, e in enumerate((1, 3)):
            take(y_pair[e], shard + i * slim, slim)
            take(z_pair[d], shard + j * rest, rest, (d, e, 0), (d, e, 1))
    return copies, blocks


def low_product_kernel(plan, where_ref, table_ref, dz_ref, *refs):
    count = len(refs) - 7
    w_refs = refs[:count]
    mine_ref, theirs_ref, send_ref, dz_all, w_all, dz_sem, sem = refs[count:]
    steps, deep = w_all.shape[0], w_all.shape[1]
    wide = deep // 2

    @pl.when(where_ref[3] == 0)
    def _():
        dz_copy = pltpu.make_async_copy(dz_ref, dz_all, dz_sem)
        dz_copy.start()
        for array, row, at, rows in plan:
            while rows:
                part = min(rows, deep - at % deep)
                pltpu.make_async_copy(
                    w_refs[array].at[pl.ds(row, part)],
                    w_all.at[at // deep, pl.ds(at % deep, part)],
                    sem.at[at // deep],
                ).start()
                row, at, rows = row + part, at + part, rows - part
        dz_copy.wait()

        @pl.loop(0, steps)
        def _(step):
            pltpu.make_async_copy(w_refs[0], w_all.at[step], sem.at[step]).wait()
            value = lax.dot_general(
                dz_all[...], w_all[step], (((1,), (1,)), ((), ())), preferred_element_type=F32
            ).astype(BF16)
            for k in range(2):
                entry = table_ref[2 * step + k]
                columns = pl.ds(pl.multiple_of(lax.rem(entry, 2 * RING) * wide, wide), wide)
                far = lax.rem(entry // (2 * RING), 2)
                block = value[:, k * wide:(k + 1) * wide]

                @pl.when(entry < 2 * RING)
                def _():
                    mine_ref[:, columns] = block

                @pl.when(jnp.logical_and(entry >= 2 * RING, entry < 4 * RING))
                def _():
                    theirs_ref[:, columns] = block

                @pl.when(entry >= 4 * RING)
                def _():
                    send_ref[far, :, columns] = block


def low_product(where, z, y, place, dz, w_pieces, *earlier):
    rows, width = dz.shape
    shard = w_pieces[0].shape[0]
    wide = shard // 2
    copies, blocks = low_plan(shard, wide)
    steps = [jnp.array(column, jnp.int32) for column in zip(*blocks)]
    target = (z + steps[0]) % RING
    column = (y + steps[1]) % RING * 2 + steps[2]
    other_core = (target % 2 != place % 2).astype(jnp.int32)
    other_pair = (target // 2 != place // 2).astype(jnp.int32)
    table = (other_core * 2 + other_pair) * 2 * RING + column
    return pl.pallas_call(
        in_order(functools.partial(low_product_kernel, copies), 3 + len(w_pieces), len(earlier)),
        in_specs=[SMEM, SMEM, HBM] + [HBM] * len(w_pieces) + [ANY] * len(earlier),
        out_specs=[VMEM, VMEM, VMEM],
        out_shape=[jax.ShapeDtypeStruct((rows, 2 * RING * wide), BF16)] * 2
        + [jax.ShapeDtypeStruct((2, rows, 2 * RING * wide), BF16)],
        scratch_shapes=[
            pltpu.VMEM((rows, width), BF16),
            pltpu.VMEM((RING * RING, shard, width), BF16),
            pltpu.SemaphoreType.DMA,
            pltpu.SemaphoreType.DMA((RING * RING,)),
        ],
        compiler_params=pltpu.CompilerParams(vmem_limit_bytes=BIG),
        cost_estimate=pl.CostEstimate(
            flops=16 * RING * rows * wide * width, bytes_accessed=2 ** 25, transcendentals=0
        ),
    )(where, table, dz, *w_pieces, *earlier)


def add_kernel(keep_ref, got_ref, out_ref):
    out_ref[...] = (keep_ref[...].astype(F32) + got_ref[0].astype(F32)).astype(BF16)


def add_theirs(keep, got):
    rows, wide = keep.shape
    whole = pl.BlockSpec((rows, wide), lambda i: (0, 0))
    return pl.pallas_call(
        add_kernel,
        grid=(1,),
        in_specs=[whole, pl.BlockSpec((1, rows, wide), lambda i: (1, 0, 0))],
        out_specs=whole,
        out_shape=jax.ShapeDtypeStruct((rows, wide), BF16),
        compiler_params=pltpu.CompilerParams(vmem_limit_bytes=SMALL),
        cost_estimate=LIGHT,
    )(keep, got)


def total_kernel(keep_ref, got_ref, other_ref, *out_refs):
    rows = out_refs[0].shape[0]
    for i, ref in enumerate(out_refs):
        part = pl.ds(i * rows, rows)
        ref[...] = (
            keep_ref[part].astype(F32) + got_ref[0, part].astype(F32) + other_ref[part].astype(F32)
        ).astype(BF16)


def add_mine(keep, got, other, *earlier):
    rows, wide = keep.shape
    whole = pl.BlockSpec((rows, wide), lambda i: (0, 0))
    return pl.pallas_call(
        in_order(total_kernel, 3, len(earlier)),
        grid=(1,),
        in_specs=[whole, pl.BlockSpec((1, rows, wide), lambda i: (0, 0, 0)), whole] + [ANY] * len(earlier),
        out_specs=[pl.BlockSpec((rows // RING, wide), lambda i: (0, 0))] * RING,
        out_shape=[jax.ShapeDtypeStruct((rows // RING, wide), BF16)] * RING,
        compiler_params=pltpu.CompilerParams(vmem_limit_bytes=SMALL),
        cost_estimate=LIGHT,
    )(keep, got, other, *earlier)


def as_row(column):
    square = jnp.broadcast_to(column, (column.shape[0], LANES))
    return jnp.transpose(square)[:8]


def as_column(row):
    square = jnp.concatenate([row] * (LANES // 8), axis=0)
    return jnp.transpose(square)[:, :1]


def scaled_kernel(where_ref, own, after, far, before, mixed_ref, a_ref, gain_ref, hidden_ref, scale_ref, scaled_ref, inner_ref):
    wide = own.shape[1]
    mixed = mixed_ref[...]
    inner = jnp.zeros((own.shape[0], 1), F32)
    for r, piece in enumerate((own, after, far, before)):
        at = pl.ds(pl.multiple_of(lax.rem(where_ref[2] + r, RING) * wide, wide), wide)
        low_rank = lax.dot_general(
            mixed, a_ref[:, at], (((0,), (0,)), ((), ())), precision=HIGH, preferred_element_type=F32
        )
        scaled = gain_ref[:, at] * (piece[...].astype(F32) + low_rank)
        scaled_ref[:, at] = scaled.astype(BF16)
        inner = inner + jnp.sum(scaled * hidden_ref[:, at].astype(F32), axis=1, keepdims=True)
    inner_ref[...] = as_row(inner * scale_ref[...])


def make_scaled(where, pieces, mixed, a_local, gain, hidden, scale):
    rows, width = hidden.shape
    return pl.pallas_call(
        scaled_kernel,
        in_specs=[SMEM] + [VMEM] * 9,
        out_specs=[VMEM, VMEM],
        out_shape=[jax.ShapeDtypeStruct((rows, width), BF16), jax.ShapeDtypeStruct((8, rows), F32)],
        compiler_params=pltpu.CompilerParams(vmem_limit_bytes=MEDIUM),
        cost_estimate=LIGHT,
    )(where, *pieces, mixed, a_local, gain, hidden, scale)


def low_scaled_kernel(keep_ref, got_ref, other_ref, mixed_ref, a_ref, gain_ref, hidden_ref, scale_ref, scaled_ref, inner_ref):
    low_rank = lax.dot_general(
        mixed_ref[...], a_ref[...], (((0,), (0,)), ((), ())), precision=HIGH, preferred_element_type=F32
    )
    total = keep_ref[...].astype(F32) + got_ref[0].astype(F32) + other_ref[...].astype(F32)
    scaled = gain_ref[...] * (total + low_rank)
    scaled_ref[...] = scaled.astype(BF16)
    inner = jnp.sum(scaled * hidden_ref[...].astype(F32), axis=1, keepdims=True)
    inner_ref[...] = as_row(inner * scale_ref[...])


def low_scaled(keep, got, other, mixed, a_local, gain, hidden, scale):
    rows, width = hidden.shape
    whole = lambda shape: pl.BlockSpec(shape, lambda i: (0, 0))
    mine = pl.BlockSpec((1, rows, width), lambda i: (0, 0, 0))
    return pl.pallas_call(
        low_scaled_kernel,
        grid=(1,),
        in_specs=[
            whole((rows, width)), mine, whole((rows, width)), whole((RANK, rows)), whole((RANK, width)),
            whole((1, width)), whole((rows, width)), whole((rows, 1)),
        ],
        out_specs=[whole((rows, width)), whole((8, rows))],
        out_shape=[jax.ShapeDtypeStruct((rows, width), BF16), jax.ShapeDtypeStruct((8, rows), F32)],
        compiler_params=pltpu.CompilerParams(vmem_limit_bytes=MEDIUM),
        cost_estimate=LIGHT,
    )(keep, got, other, mixed, a_local, gain, hidden, scale)


def hidden_gradient(scaled_ref, inner_ref, hidden_ref, scale_ref, incoming_ref):
    scale = scale_ref[...]
    pull = as_column(inner_ref[...]) * scale / MODEL_WIDTH
    return (
        incoming_ref[...].astype(F32)
        + scale * (scaled_ref[...].astype(F32) - hidden_ref[...].astype(F32) * pull)
    ).astype(BF16)


def top_kernel(scaled_ref, inner_ref, hidden_ref, scale_ref, incoming_ref, out_ref):
    out_ref[...] = hidden_gradient(scaled_ref, inner_ref, hidden_ref, scale_ref, incoming_ref)


def low_kernel(
    where_ref, scaled_ref, inner_ref, hidden_ref, scale_ref, incoming_ref, share_ref, other_ref, top_ref,
    out_ref, bank_ref, sem,
):
    bank_ref[...] = share_ref[...].astype(F32) + other_ref[...].astype(F32)

    @pl.when(where_ref[3] == 0)
    def _():
        out_ref[...] = hidden_gradient(scaled_ref, inner_ref, hidden_ref, scale_ref, incoming_ref)

    @pl.when(where_ref[3] == 1)
    def _():
        copy = pltpu.make_async_copy(top_ref, out_ref, sem)
        copy.start()
        copy.wait()


def finish_specs(rows, width, c):
    whole = lambda shape: pl.BlockSpec(shape, lambda i: (0, 0))
    return [
        whole((rows, width)),
        whole((8, rows)),
        pl.BlockSpec((rows, width), lambda i: (c, 0)),
        pl.BlockSpec((rows, 1), lambda i: (c, 0)),
    ]


def finish_top(scaled, inner, hidden, scale, grad_top, c):
    rows, width = scaled.shape
    return pl.pallas_call(
        top_kernel,
        grid=(1,),
        in_specs=finish_specs(rows, width, c) + [pl.BlockSpec((rows, width), lambda i: (c, 0))],
        out_specs=pl.BlockSpec((rows, width), lambda i: (0, 0)),
        out_shape=jax.ShapeDtypeStruct((rows, width), BF16),
        compiler_params=pltpu.CompilerParams(vmem_limit_bytes=MEDIUM),
        cost_estimate=LIGHT,
    )(scaled, inner, hidden, scale, grad_top)


def finish_low(where, scaled, inner, hidden, scale, incoming, share, other, top):
    rows, width = scaled.shape
    block = pl.BlockSpec((rows, width), lambda i: (0, 0))
    bank = pl.BlockSpec(share.shape, lambda i: (0, 0))
    return pl.pallas_call(
        low_kernel,
        grid=(1,),
        in_specs=[SMEM] + finish_specs(rows, width, 0) + [block, bank, bank, HBM],
        out_specs=[block, bank],
        out_shape=[jax.ShapeDtypeStruct((rows, width), BF16), jax.ShapeDtypeStruct(share.shape, F32)],
        scratch_shapes=[pltpu.SemaphoreType.DMA],
        compiler_params=pltpu.CompilerParams(vmem_limit_bytes=MEDIUM),
        cost_estimate=LIGHT,
    )(where, scaled, inner, hidden, scale, incoming, share, other, top)


def grads_kernel(where_ref, hidden_ref, scale_ref, gain_ref, projected_ref, *refs):
    out_ref = refs[-1]
    top = where_ref[3] == 1
    count = (len(refs) - 2) // 3
    total_a, total_b = 0.0, 0.0
    for c in range(count):
        low_dz, top_mixed, low_mixed = [refs[1 + k * count + c] for k in range(3)]
        rows = pl.ds(c * low_dz.shape[0], low_dz.shape[0])
        dz = jnp.where(top, refs[0][rows], low_dz[...])
        mixed = jnp.where(top, top_mixed[...], low_mixed[...])
        x = (hidden_ref[rows].astype(F32) * scale_ref[rows] * gain_ref[...]).astype(BF16)
        projected = projected_ref[:, rows]

        def both(left, right):
            value = lax.dot_general(
                two_halves(left), right, (((1,), (0,)), ((), ())), preferred_element_type=F32
            )
            return value[:RANK] + value[RANK:]

        total_a = total_a + both(mixed, x)
        total_b = total_b + both(projected, dz)
    out_ref[...] = jnp.concatenate([total_a, total_b], axis=0)


def make_grads(where, hidden, scale, gain, projected, lists, *earlier):
    arrays = [array for arrays in lists for array in arrays]
    return pl.pallas_call(
        in_order(grads_kernel, 5 + len(arrays), len(earlier)),
        in_specs=[SMEM] + [VMEM] * (4 + len(arrays)) + [ANY] * len(earlier),
        out_specs=VMEM,
        out_shape=jax.ShapeDtypeStruct((2 * RANK, hidden.shape[1]), F32),
        compiler_params=pltpu.CompilerParams(vmem_limit_bytes=MEDIUM),
        cost_estimate=LIGHT,
    )(where, hidden, scale, gain, projected, *arrays, *earlier)


def ring_total(value, moved):
    after, far, before = moved
    return (value[...] + far[...]) + (after[...] + before[...])


def ring_kernel(value, after, far, before, out_ref):
    out_ref[...] = ring_total(value, (after, far, before))


def bank_kernel(mixing_ref, value, after, far, before, out_ref):
    total = ring_total(value, (after, far, before))
    count = total.shape[1] // SUB
    pieces = jnp.concatenate([total[:, j * SUB:(j + 1) * SUB] for j in range(count)], axis=0)
    out_ref[...] = lax.dot_general(
        mixing_ref[...], pieces, (((0,), (0,)), ((), ())), precision=HIGH, preferred_element_type=F32
    )


def round_kernel(factor, left, right, out_ref):
    out_ref[...] = ((left[...].astype(F32) + right[...].astype(F32)) * factor).astype(out_ref.dtype)


def small_call(kernel, out, operands, *earlier):
    return pl.pallas_call(
        in_order(kernel, len(operands), len(earlier)),
        in_specs=[VMEM] * len(operands) + [ANY] * len(earlier),
        out_specs=VMEM,
        out_shape=out,
        compiler_params=pltpu.CompilerParams(vmem_limit_bytes=SMALL),
        cost_estimate=LIGHT,
    )(*operands, *earlier)


def ring_moves(value, axis):
    return [ring_move(value, axis, d) for d in (-1, 2, 1)]


def shards(hidden_in, preact, norm_gain, weight, bank, mix_index, mix_weight, grad_top):
    section = lax.axis_index("section")
    z, y = lax.axis_index("z"), lax.axis_index("y")
    place = lax.axis_index("pair") * 2 + lax.axis_index("core")
    where = jnp.stack([z, place, y, section]).astype(jnp.int32)
    tensor = ("pair", "core")
    bank_rows = bank.shape[0]

    tokens, local_width = grad_top.shape
    seg_local = local_width // SUB
    seg_row = MODEL_WIDTH // SUB
    own_weight = weight[0]
    shard = own_weight.shape[0]
    half = shard // 2

    first = make_first(where, grad_top, preact[0], own_weight)
    hidden, preact = hidden_in[0], preact[0]

    def local_pieces(array):
        array = array.reshape(2, RANK, seg_row, 2)
        return lax.dynamic_slice_in_dim(array, place * seg_local, seg_local, 2)

    mixing = compose(local_pieces(mix_index[0]), local_pieces(mix_weight[0]), bank_rows)
    mixing = mixing.reshape(2, RANK * seg_local, bank_rows)
    factors = jnp.einsum("fnb,bs->fns", mixing, bank, precision=HIGH)
    a_local = factors[0].reshape(RANK, local_width)
    b_both = two_halves(factors[1].reshape(RANK, local_width))

    hidden_f = hidden.astype(F32)
    sums = lax.psum(
        jnp.concatenate(
            [
                jnp.sum(hidden_f * hidden_f, axis=1)[None],
                jnp.dot(a_local, (hidden_f * norm_gain).T, precision=HIGH),
                jnp.dot(factors[1].reshape(RANK, local_width), first[:tokens].astype(F32).T, precision=HIGH),
            ],
            axis=0,
        ),
        tensor,
    )
    scale_row = lax.rsqrt(sums[:1] / MODEL_WIDTH + epsilon)
    projected = sums[1:1 + RANK] * scale_row
    scale = scale_row.reshape(tokens, 1)
    top_mixed = sums[1 + RANK:]

    z_ring = gather_ring(own_weight, "z", scale)
    y_ring = gather_ring(first, "y", scale)

    _, z_after, z_far_low, z_far_high, z_before = z_ring
    _, y_after, y_far_low, y_far_high, y_before = y_ring
    slim = 112
    rest = shard - slim
    corner_parts = join(where, 0, (z_far_low, z_far_high), ((0, half), (0, half)), y_far_high)
    corner = ring_move(corner_parts, "y", 2, (0,))

    dz_pieces = (y_ring[0], y_ring[1], y_ring[2], y_ring[4])
    mine, keep, send = top_product(where, tokens, dz_pieces, z_ring, y_far_high)
    got = swap(send, "core", (1,))
    theirs = add_theirs(keep, got)
    other = swap(theirs, "pair", (1,))
    along_z = join(
        where, 0, (y_far_low, y_far_high, y_after, y_before),
        ((0, half), (0, half), (slim, rest), (slim, rest)), theirs,
    )
    z_pair = (ring_move(along_z, "z", -1), ring_move(along_z, "z", 1))
    along_y = join(
        where, 0, (z_far_low, z_far_high, z_after, z_before),
        ((0, half), (0, half), (0, slim), (0, slim)), theirs,
    )
    own, to_after, to_far, to_before = add_mine(mine, got, other, corner, along_y)
    from_before = ring_move(to_after, "y", 1, (1,))
    from_far = ring_move(to_far, "y", 2, (1,))
    from_after = ring_move(to_before, "y", -1, (1,))
    along_y = after(along_y, (from_before, from_far, from_after))
    y_pair = (ring_move(along_y, "y", -1, (0,)), ring_move(along_y, "y", 1, (0,)))
    w_pieces = (*z_ring, *y_ring[1:], corner, *y_pair, *z_pair)

    pieces = (own, from_after, from_far, from_before)
    scaled, inner = make_scaled(where, pieces, top_mixed, a_local, norm_gain, hidden, scale)
    top_grad = finish_top(scaled, lax.psum(inner, tensor), hidden, scale, grad_top, 0)
    low_in = lax.ppermute(top_grad, "section", [(1, 0)])

    low_dz, part = make_dz(low_in, preact, b_both, 0)
    low_mixed = lax.psum(part, tensor)
    mine, keep, send = low_product(where, z, y, place, low_dz, w_pieces, low_mixed)
    got = swap(send, "core", (0,))
    theirs = add_theirs(keep, got)
    other = swap(theirs, "pair", (0,))
    scaled, inner = low_scaled(mine, got, other, low_mixed, a_local, norm_gain, hidden, scale)
    inner = lax.psum(inner, tensor)
    grads = make_grads(
        where, hidden, scale, norm_gain, projected, ([first], [low_dz], [top_mixed], [low_mixed])
    )
    over_y = ring_moves(grads, "y")
    grads = small_call(ring_kernel, jax.ShapeDtypeStruct(grads.shape, F32), (grads, *over_y), send)
    over_z = ring_moves(grads, "z")
    flat = mixing.reshape(2, RANK, seg_local, bank_rows).transpose(2, 0, 1, 3)
    flat = flat.reshape(2 * RANK * seg_local, bank_rows)
    bank_shape = (bank_rows, SUB)
    share = small_call(bank_kernel, jax.ShapeDtypeStruct(bank_shape, F32), (flat, grads, *over_z), theirs)
    core_share = swap(share, "core")
    half_shape = jax.ShapeDtypeStruct(bank_shape, BF16)
    add_up = functools.partial(round_kernel, 1.0 / math.sqrt(TOKENS))
    share = small_call(add_up, half_shape, (share, core_share))
    pair_share = swap(share, "pair")
    add_up = functools.partial(round_kernel, 1.0)
    share = small_call(add_up, half_shape, (share, pair_share))
    other_share = lax.ppermute(share, "section", [(0, 1), (1, 0)])
    result, bank_grad = finish_low(
        where, scaled, inner, hidden, scale, low_in, share, other_share, top_grad
    )
    return (result[None], bank_grad)


def solution(mesh):
    fine = Mesh(
        mesh.devices.reshape(2, RING, RING, 2, 2), ("section", "z", "y", "pair", "core")
    )
    rows, columns = ("z", "y"), ("pair", "core")
    return jax.shard_map(
        shards,
        mesh=fine,
        in_specs=(
            P("section", rows, columns),
            P("section", rows, columns),
            P("section", columns),
            P("section", rows, columns),
            P(),
            P("section", None, None, None),
            P("section", None, None, None),
            P(rows, columns),
        ),
        out_specs=(P("section", rows, columns), P()),
        check_vma=False,
    )
```

```python
import functools
import math

import jax
import jax.numpy as jnp
from jax import lax
from jax.experimental import pallas as pl
from jax.experimental.pallas import tpu as pltpu
from jax.sharding import Mesh, PartitionSpec as P

MODEL_WIDTH = 8192
RANK = 4
SUB = 256
TOKENS = 4096
RING = 4
LANES = 128

epsilon = 1e-06
HIGH = lax.Precision.HIGHEST
F32 = jnp.float32
BF16 = jnp.bfloat16
ANY = pl.BlockSpec(memory_space=pl.ANY)
SMEM = pl.BlockSpec(memory_space=pltpu.SMEM)
VMEM = pl.BlockSpec(memory_space=pltpu.VMEM)
HBM = pl.BlockSpec(memory_space=pltpu.HBM)
BIG = 48 * 1024 * 1024
MEDIUM = 20 * 1024 * 1024
SMALL = 12 * 1024 * 1024
LIGHT = pl.CostEstimate(flops=0, bytes_accessed=2 ** 20, transcendentals=0)


def ring_route(distance, sections=(0, 1)):
    return [(s * RING + i, s * RING + (i + distance) % RING) for s in sections for i in range(RING)]


def ring_move(block, axis, distance, sections=(0, 1)):
    return lax.ppermute(block, ("section", axis), ring_route(distance, sections))


def swap(block, axis, sections=(0, 1)):
    pairs = [(s * 2 + i, s * 2 + 1 - i) for s in sections for i in range(2)]
    return lax.ppermute(block, ("section", axis), pairs)


def after(value, earlier):
    return lax.optimization_barrier((value, earlier))[0]


def in_order(kernel, operands, extra):
    return lambda *refs: kernel(*refs[:operands], *refs[operands + extra:])


def compose(index_layer, weight_layer, rows):
    columns = lax.broadcasted_iota(jnp.int32, (1, 1, 1, 1, rows), 4)
    onehot = (index_layer[..., None] == columns).astype(F32)
    return jnp.sum(onehot * weight_layer[..., None], axis=3)


def two_halves(value):
    high = value.astype(BF16)
    return jnp.concatenate([high, (value - high.astype(F32)).astype(BF16)], axis=0)


def activation_gradient(incoming_ref, preact_ref):
    value = preact_ref[...].astype(F32)
    sig = jax.nn.sigmoid(value)
    slope = sig * (1.0 + value * (1.0 - sig))
    return (incoming_ref[...].astype(F32) * slope).astype(BF16)


def dz_kernel(incoming_ref, preact_ref, b_ref, dz_ref, mixed_ref):
    dz = activation_gradient(incoming_ref, preact_ref)
    dz_ref[...] = dz
    both = lax.dot_general(b_ref[...], dz, (((1,), (1,)), ((), ())), preferred_element_type=F32)
    mixed_ref[...] = both[:RANK] + both[RANK:]


def first_kernel(where_ref, incoming_ref, preact_ref, weight_ref, out_ref, incoming, preact, sem):
    def fetch(*pairs):
        copies = [pltpu.make_async_copy(*pair, sem.at[i]) for i, pair in enumerate(pairs)]
        for copy in copies:
            copy.start()
        for copy in copies:
            copy.wait()

    @pl.when(where_ref[3] == 1)
    def _():
        fetch((incoming_ref, incoming), (preact_ref, preact))
        out_ref[:incoming.shape[0]] = activation_gradient(incoming, preact)

    @pl.when(where_ref[3] == 0)
    def _():
        fetch((weight_ref, out_ref))


def make_first(where, incoming, preact, weight):
    return pl.pallas_call(
        first_kernel,
        in_specs=[SMEM, HBM, HBM, HBM],
        out_specs=VMEM,
        out_shape=jax.ShapeDtypeStruct(weight.shape, BF16),
        scratch_shapes=[
            pltpu.VMEM(incoming.shape, BF16),
            pltpu.VMEM(incoming.shape, BF16),
            pltpu.SemaphoreType.DMA((2,)),
        ],
        compiler_params=pltpu.CompilerParams(vmem_limit_bytes=MEDIUM),
        cost_estimate=LIGHT,
    )(where, incoming, preact, weight)


def join_kernel(wanted, parts, where_ref, *refs):
    sources, out_ref, held, sem, out_sem = refs[:len(parts)], *refs[-4:]

    @pl.when(where_ref[3] == wanted)
    def _():
        start = 0
        steps = []
        for i, (first, rows) in enumerate(parts):
            here = held.at[pl.ds(start, rows)]
            fetch = pltpu.make_async_copy(sources[i].at[pl.ds(first, rows)], here, sem.at[i])
            store = pltpu.make_async_copy(here, out_ref.at[pl.ds(start, rows)], out_sem.at[i])
            steps.append((fetch, store))
            start += rows
        for fetch, _ in steps:
            fetch.start()
        for fetch, store in steps:
            fetch.wait()
            store.start()
        for _, store in steps:
            store.wait()


def join(where, wanted, arrays, parts, *earlier):
    rows, width = sum(count for _, count in parts), arrays[0].shape[1]
    return pl.pallas_call(
        in_order(functools.partial(join_kernel, wanted, parts), 1 + len(arrays), len(earlier)),
        in_specs=[SMEM] + [ANY] * (len(arrays) + len(earlier)),
        out_specs=HBM,
        out_shape=jax.ShapeDtypeStruct((rows, width), BF16),
        scratch_shapes=[
            pltpu.VMEM((rows, width), BF16),
            pltpu.SemaphoreType.DMA((len(arrays),)),
            pltpu.SemaphoreType.DMA((len(arrays),)),
        ],
        compiler_params=pltpu.CompilerParams(vmem_limit_bytes=SMALL),
        cost_estimate=LIGHT,
    )(where, *arrays, *earlier)


def halves_kernel(after_ref, before_ref, low_ref, high_ref, sem):
    half = low_ref.shape[0]
    low = pltpu.make_async_copy(after_ref.at[pl.ds(0, half)], low_ref, sem.at[0])
    high = pltpu.make_async_copy(before_ref.at[pl.ds(half, half)], high_ref, sem.at[1])
    low.start()
    high.start()
    low.wait()
    high.wait()


def gather_ring(block, axis, *earlier):
    rows, width = block.shape
    after = ring_move(block, axis, -1)
    before = ring_move(block, axis, 1)
    low, high = pl.pallas_call(
        in_order(halves_kernel, 2, len(earlier)),
        in_specs=[ANY, ANY] + [ANY] * len(earlier),
        out_specs=[VMEM, VMEM],
        out_shape=[jax.ShapeDtypeStruct((rows // 2, width), BF16)] * 2,
        scratch_shapes=[pltpu.SemaphoreType.DMA((2,))],
        compiler_params=pltpu.CompilerParams(vmem_limit_bytes=SMALL),
        cost_estimate=LIGHT,
    )(after, before, *earlier)
    return block, after, ring_move(low, axis, -1), ring_move(high, axis, 1), before


def make_dz(incoming, preact, b_both, c, *earlier):
    rows, width = incoming.shape
    return pl.pallas_call(
        in_order(dz_kernel, 3, len(earlier)),
        grid=(1,),
        in_specs=[
            pl.BlockSpec((rows, width), lambda i: (0, 0)),
            pl.BlockSpec((rows, width), lambda i: (c, 0)),
            pl.BlockSpec((2 * RANK, width), lambda i: (0, 0)),
        ]
        + [ANY] * len(earlier),
        out_specs=[
            pl.BlockSpec((rows, width), lambda i: (0, 0)),
            pl.BlockSpec((RANK, rows), lambda i: (0, 0)),
        ],
        out_shape=[
            jax.ShapeDtypeStruct((rows, width), BF16),
            jax.ShapeDtypeStruct((RANK, rows), F32),
        ],
        compiler_params=pltpu.CompilerParams(vmem_limit_bytes=MEDIUM),
        cost_estimate=LIGHT,
    )(incoming, preact, b_both, *earlier)


def top_product_kernel(rows, where_ref, *refs):
    dz_refs, w_refs = refs[:4], refs[4:9]
    mine_ref, theirs_ref, send_ref, dz_all, w_all, dz_sem, w_sem = refs[9:]

    @pl.when(where_ref[3] == 1)
    def _():
        copies = [
            pltpu.make_async_copy(ref.at[pl.ds(0, rows)], dz_all.at[pl.ds(i * rows, rows)], dz_sem.at[i])
            for i, ref in enumerate(dz_refs)
        ]
        for copy in copies:
            copy.start()
        own, after, far_low, far_high, before = w_refs
        half = far_low.shape[0]
        pltpu.make_async_copy(own, w_all.at[0], w_sem.at[0]).start()
        pltpu.make_async_copy(after, w_all.at[1], w_sem.at[1]).start()
        pltpu.make_async_copy(far_low, w_all.at[2, pl.ds(0, half)], w_sem.at[2]).start()
        pltpu.make_async_copy(far_high, w_all.at[2, pl.ds(half, half)], w_sem.at[2]).start()
        pltpu.make_async_copy(before, w_all.at[3], w_sem.at[3]).start()
        for copy in copies:
            copy.wait()
        z, place = where_ref[0], where_ref[1]

        @pl.loop(0, RING)
        def _(i):
            pltpu.make_async_copy(own, w_all.at[i], w_sem.at[i]).wait()
            value = lax.dot_general(
                dz_all[...], w_all[i], (((1,), (1,)), ((), ())), preferred_element_type=F32
            ).astype(BF16)
            target = lax.rem(z + i, RING)
            own_core = lax.rem(target, 2) == lax.rem(place, 2)
            far = jnp.where(target // 2 == place // 2, 0, 1)

            @pl.when(jnp.logical_and(own_core, far == 0))
            def _():
                mine_ref[...] = value

            @pl.when(jnp.logical_and(own_core, far == 1))
            def _():
                theirs_ref[...] = value

            @pl.when(jnp.logical_not(own_core))
            def _():
                send_ref[far] = value


def top_product(where, rows, dz_pieces, w_pieces, *earlier):
    wide, width = w_pieces[0].shape
    return pl.pallas_call(
        in_order(functools.partial(top_product_kernel, rows), 10, len(earlier)),
        in_specs=[SMEM] + [HBM] * 9 + [ANY] * len(earlier),
        out_specs=[VMEM, VMEM, VMEM],
        out_shape=[jax.ShapeDtypeStruct((RING * rows, wide), BF16)] * 2
        + [jax.ShapeDtypeStruct((2, RING * rows, wide), BF16)],
        scratch_shapes=[
            pltpu.VMEM((RING * rows, width), BF16),
            pltpu.VMEM((RING, wide, width), BF16),
            pltpu.SemaphoreType.DMA((4,)),
            pltpu.SemaphoreType.DMA((RING,)),
        ],
        compiler_params=pltpu.CompilerParams(vmem_limit_bytes=36 * 1024 * 1024),
        cost_estimate=pl.CostEstimate(
            flops=2 * RING * RING * rows * wide * width, bytes_accessed=2 ** 24, transcendentals=0
        ),
    )(where, *dz_pieces, *w_pieces, *earlier)


def low_plan(shard, wide):
    copies, blocks = [], []

    def take(array, row, rows, *names):
        at = sum(rows for *_, rows in copies)
        copies.append((array, row, at, rows))
        blocks.extend(names)

    for base, step in ((0, lambda d, h: (d, 0, h)), (4, lambda d, h: (0, d, h))):
        if base == 0:
            take(0, 0, shard, step(0, 0), step(0, 1))
        take(base + 1, 0, shard, step(1, 0), step(1, 1))
        take(base + 2, 0, wide, step(2, 0))
        take(base + 3, 0, wide, step(2, 1))
        take(base + 4, 0, shard, step(3, 0), step(3, 1))
    corner, y_pair, z_pair = 9, {1: 10, 3: 11}, {1: 12, 3: 13}
    take(corner, 0, shard, (2, 2, 0), (2, 2, 1))
    for d in (1, 3):
        take(y_pair[d], 0, shard, (2, d, 0), (2, d, 1))
        take(z_pair[d], 0, shard, (d, 2, 0), (d, 2, 1))
    slim = 112
    rest = shard - slim
    for i, d in enumerate((1, 3)):
        for j, e in enumerate((1, 3)):
            take(y_pair[e], shard + i * slim, slim)
            take(z_pair[d], shard + j * rest, rest, (d, e, 0), (d, e, 1))
    return copies, blocks


def low_product_kernel(plan, where_ref, table_ref, dz_ref, *refs):
    count = len(refs) - 7
    w_refs = refs[:count]
    mine_ref, theirs_ref, send_ref, dz_all, w_all, dz_sem, sem = refs[count:]
    steps, deep = w_all.shape[0], w_all.shape[1]
    wide = deep // 2

    @pl.when(where_ref[3] == 0)
    def _():
        dz_copy = pltpu.make_async_copy(dz_ref, dz_all, dz_sem)
        dz_copy.start()
        for array, row, at, rows in plan:
            while rows:
                part = min(rows, deep - at % deep)
                pltpu.make_async_copy(
                    w_refs[array].at[pl.ds(row, part)],
                    w_all.at[at // deep, pl.ds(at % deep, part)],
                    sem.at[at // deep],
                ).start()
                row, at, rows = row + part, at + part, rows - part
        dz_copy.wait()

        @pl.loop(0, steps)
        def _(step):
            pltpu.make_async_copy(w_refs[0], w_all.at[step], sem.at[step]).wait()
            value = lax.dot_general(
                dz_all[...], w_all[step], (((1,), (1,)), ((), ())), preferred_element_type=F32
            ).astype(BF16)
            for k in range(2):
                entry = table_ref[2 * step + k]
                columns = pl.ds(pl.multiple_of(lax.rem(entry, 2 * RING) * wide, wide), wide)
                far = lax.rem(entry // (2 * RING), 2)
                block = value[:, k * wide:(k + 1) * wide]

                @pl.when(entry < 2 * RING)
                def _():
                    mine_ref[:, columns] = block

                @pl.when(jnp.logical_and(entry >= 2 * RING, entry < 4 * RING))
                def _():
                    theirs_ref[:, columns] = block

                @pl.when(entry >= 4 * RING)
                def _():
                    send_ref[far, :, columns] = block


def low_product(where, z, y, place, dz, w_pieces, *earlier):
    rows, width = dz.shape
    shard = w_pieces[0].shape[0]
    wide = shard // 2
    copies, blocks = low_plan(shard, wide)
    steps = [jnp.array(column, jnp.int32) for column in zip(*blocks)]
    target = (z + steps[0]) % RING
    column = (y + steps[1]) % RING * 2 + steps[2]
    other_core = (target % 2 != place % 2).astype(jnp.int32)
    other_pair = (target // 2 != place // 2).astype(jnp.int32)
    table = (other_core * 2 + other_pair) * 2 * RING + column
    return pl.pallas_call(
        in_order(functools.partial(low_product_kernel, copies), 3 + len(w_pieces), len(earlier)),
        in_specs=[SMEM, SMEM, HBM] + [HBM] * len(w_pieces) + [ANY] * len(earlier),
        out_specs=[VMEM, VMEM, VMEM],
        out_shape=[jax.ShapeDtypeStruct((rows, 2 * RING * wide), BF16)] * 2
        + [jax.ShapeDtypeStruct((2, rows, 2 * RING * wide), BF16)],
        scratch_shapes=[
            pltpu.VMEM((rows, width), BF16),
            pltpu.VMEM((RING * RING, shard, width), BF16),
            pltpu.SemaphoreType.DMA,
            pltpu.SemaphoreType.DMA((RING * RING,)),
        ],
        compiler_params=pltpu.CompilerParams(vmem_limit_bytes=BIG),
        cost_estimate=pl.CostEstimate(
            flops=16 * RING * rows * wide * width, bytes_accessed=2 ** 25, transcendentals=0
        ),
    )(where, table, dz, *w_pieces, *earlier)


def add_kernel(keep_ref, got_ref, out_ref):
    out_ref[...] = (keep_ref[...].astype(F32) + got_ref[0].astype(F32)).astype(BF16)


def add_theirs(keep, got):
    rows, wide = keep.shape
    whole = pl.BlockSpec((rows, wide), lambda i: (0, 0))
    return pl.pallas_call(
        add_kernel,
        grid=(1,),
        in_specs=[whole, pl.BlockSpec((1, rows, wide), lambda i: (1, 0, 0))],
        out_specs=whole,
        out_shape=jax.ShapeDtypeStruct((rows, wide), BF16),
        compiler_params=pltpu.CompilerParams(vmem_limit_bytes=SMALL),
        cost_estimate=LIGHT,
    )(keep, got)


def total_kernel(keep_ref, got_ref, other_ref, *out_refs):
    rows = out_refs[0].shape[0]
    for i, ref in enumerate(out_refs):
        part = pl.ds(i * rows, rows)
        ref[...] = (
            keep_ref[part].astype(F32) + got_ref[0, part].astype(F32) + other_ref[part].astype(F32)
        ).astype(BF16)


def add_mine(keep, got, other, *earlier):
    rows, wide = keep.shape
    whole = pl.BlockSpec((rows, wide), lambda i: (0, 0))
    return pl.pallas_call(
        in_order(total_kernel, 3, len(earlier)),
        grid=(1,),
        in_specs=[whole, pl.BlockSpec((1, rows, wide), lambda i: (0, 0, 0)), whole] + [ANY] * len(earlier),
        out_specs=[pl.BlockSpec((rows // RING, wide), lambda i: (0, 0))] * RING,
        out_shape=[jax.ShapeDtypeStruct((rows // RING, wide), BF16)] * RING,
        compiler_params=pltpu.CompilerParams(vmem_limit_bytes=SMALL),
        cost_estimate=LIGHT,
    )(keep, got, other, *earlier)


def as_row(column):
    square = jnp.broadcast_to(column, (column.shape[0], LANES))
    return jnp.transpose(square)[:8]


def as_column(row):
    square = jnp.concatenate([row] * (LANES // 8), axis=0)
    return jnp.transpose(square)[:, :1]


def scaled_kernel(where_ref, own, after, far, before, mixed_ref, a_ref, gain_ref, hidden_ref, scale_ref, scaled_ref, inner_ref):
    wide = own.shape[1]
    mixed = mixed_ref[...]
    inner = jnp.zeros((own.shape[0], 1), F32)
    for r, piece in enumerate((own, after, far, before)):
        at = pl.ds(pl.multiple_of(lax.rem(where_ref[2] + r, RING) * wide, wide), wide)
        low_rank = lax.dot_general(
            mixed, a_ref[:, at], (((0,), (0,)), ((), ())), precision=HIGH, preferred_element_type=F32
        )
        scaled = gain_ref[:, at] * (piece[...].astype(F32) + low_rank)
        scaled_ref[:, at] = scaled.astype(BF16)
        inner = inner + jnp.sum(scaled * hidden_ref[:, at].astype(F32), axis=1, keepdims=True)
    inner_ref[...] = as_row(inner * scale_ref[...])


def make_scaled(where, pieces, mixed, a_local, gain, hidden, scale):
    rows, width = hidden.shape
    return pl.pallas_call(
        scaled_kernel,
        in_specs=[SMEM] + [VMEM] * 9,
        out_specs=[VMEM, VMEM],
        out_shape=[jax.ShapeDtypeStruct((rows, width), BF16), jax.ShapeDtypeStruct((8, rows), F32)],
        compiler_params=pltpu.CompilerParams(vmem_limit_bytes=MEDIUM),
        cost_estimate=LIGHT,
    )(where, *pieces, mixed, a_local, gain, hidden, scale)


def low_scaled_kernel(keep_ref, got_ref, other_ref, mixed_ref, a_ref, gain_ref, hidden_ref, scale_ref, scaled_ref, inner_ref):
    low_rank = lax.dot_general(
        mixed_ref[...], a_ref[...], (((0,), (0,)), ((), ())), precision=HIGH, preferred_element_type=F32
    )
    total = keep_ref[...].astype(F32) + got_ref[0].astype(F32) + other_ref[...].astype(F32)
    scaled = gain_ref[...] * (total + low_rank)
    scaled_ref[...] = scaled.astype(BF16)
    inner = jnp.sum(scaled * hidden_ref[...].astype(F32), axis=1, keepdims=True)
    inner_ref[...] = as_row(inner * scale_ref[...])


def low_scaled(keep, got, other, mixed, a_local, gain, hidden, scale):
    rows, width = hidden.shape
    whole = lambda shape: pl.BlockSpec(shape, lambda i: (0, 0))
    mine = pl.BlockSpec((1, rows, width), lambda i: (0, 0, 0))
    return pl.pallas_call(
        low_scaled_kernel,
        grid=(1,),
        in_specs=[
            whole((rows, width)), mine, whole((rows, width)), whole((RANK, rows)), whole((RANK, width)),
            whole((1, width)), whole((rows, width)), whole((rows, 1)),
        ],
        out_specs=[whole((rows, width)), whole((8, rows))],
        out_shape=[jax.ShapeDtypeStruct((rows, width), BF16), jax.ShapeDtypeStruct((8, rows), F32)],
        compiler_params=pltpu.CompilerParams(vmem_limit_bytes=MEDIUM),
        cost_estimate=LIGHT,
    )(keep, got, other, mixed, a_local, gain, hidden, scale)


def hidden_gradient(scaled_ref, inner_ref, hidden_ref, scale_ref, incoming_ref):
    scale = scale_ref[...]
    pull = as_column(inner_ref[...]) * scale / MODEL_WIDTH
    return (
        incoming_ref[...].astype(F32)
        + scale * (scaled_ref[...].astype(F32) - hidden_ref[...].astype(F32) * pull)
    ).astype(BF16)


def top_kernel(scaled_ref, inner_ref, hidden_ref, scale_ref, incoming_ref, out_ref):
    out_ref[...] = hidden_gradient(scaled_ref, inner_ref, hidden_ref, scale_ref, incoming_ref)


def low_kernel(
    where_ref, scaled_ref, inner_ref, hidden_ref, scale_ref, incoming_ref, share_ref, other_ref, top_ref,
    out_ref, bank_ref, sem,
):
    bank_ref[...] = share_ref[...].astype(F32) + other_ref[...].astype(F32)

    @pl.when(where_ref[3] == 0)
    def _():
        out_ref[...] = hidden_gradient(scaled_ref, inner_ref, hidden_ref, scale_ref, incoming_ref)

    @pl.when(where_ref[3] == 1)
    def _():
        copy = pltpu.make_async_copy(top_ref, out_ref, sem)
        copy.start()
        copy.wait()


def finish_specs(rows, width, c):
    whole = lambda shape: pl.BlockSpec(shape, lambda i: (0, 0))
    return [
        whole((rows, width)),
        whole((8, rows)),
        pl.BlockSpec((rows, width), lambda i: (c, 0)),
        pl.BlockSpec((rows, 1), lambda i: (c, 0)),
    ]


def finish_top(scaled, inner, hidden, scale, grad_top, c):
    rows, width = scaled.shape
    return pl.pallas_call(
        top_kernel,
        grid=(1,),
        in_specs=finish_specs(rows, width, c) + [pl.BlockSpec((rows, width), lambda i: (c, 0))],
        out_specs=pl.BlockSpec((rows, width), lambda i: (0, 0)),
        out_shape=jax.ShapeDtypeStruct((rows, width), BF16),
        compiler_params=pltpu.CompilerParams(vmem_limit_bytes=MEDIUM),
        cost_estimate=LIGHT,
    )(scaled, inner, hidden, scale, grad_top)


def finish_low(where, scaled, inner, hidden, scale, incoming, share, other, top):
    rows, width = scaled.shape
    block = pl.BlockSpec((rows, width), lambda i: (0, 0))
    bank = pl.BlockSpec(share.shape, lambda i: (0, 0))
    return pl.pallas_call(
        low_kernel,
        grid=(1,),
        in_specs=[SMEM] + finish_specs(rows, width, 0) + [block, bank, bank, HBM],
        out_specs=[block, bank],
        out_shape=[jax.ShapeDtypeStruct((rows, width), BF16), jax.ShapeDtypeStruct(share.shape, F32)],
        scratch_shapes=[pltpu.SemaphoreType.DMA],
        compiler_params=pltpu.CompilerParams(vmem_limit_bytes=MEDIUM),
        cost_estimate=LIGHT,
    )(where, scaled, inner, hidden, scale, incoming, share, other, top)


def grads_kernel(where_ref, hidden_ref, scale_ref, gain_ref, projected_ref, *refs):
    out_ref = refs[-1]
    top = where_ref[3] == 1
    count = (len(refs) - 2) // 3
    total_a, total_b = 0.0, 0.0
    for c in range(count):
        low_dz, top_mixed, low_mixed = [refs[1 + k * count + c] for k in range(3)]
        rows = pl.ds(c * low_dz.shape[0], low_dz.shape[0])
        dz = jnp.where(top, refs[0][rows], low_dz[...])
        mixed = jnp.where(top, top_mixed[...], low_mixed[...])
        x = (hidden_ref[rows].astype(F32) * scale_ref[rows] * gain_ref[...]).astype(BF16)
        projected = projected_ref[:, rows]

        def both(left, right):
            value = lax.dot_general(
                two_halves(left), right, (((1,), (0,)), ((), ())), preferred_element_type=F32
            )
            return value[:RANK] + value[RANK:]

        total_a = total_a + both(mixed, x)
        total_b = total_b + both(projected, dz)
    out_ref[...] = jnp.concatenate([total_a, total_b], axis=0)


def make_grads(where, hidden, scale, gain, projected, lists, *earlier):
    arrays = [array for arrays in lists for array in arrays]
    return pl.pallas_call(
        in_order(grads_kernel, 5 + len(arrays), len(earlier)),
        in_specs=[SMEM] + [VMEM] * (4 + len(arrays)) + [ANY] * len(earlier),
        out_specs=VMEM,
        out_shape=jax.ShapeDtypeStruct((2 * RANK, hidden.shape[1]), F32),
        compiler_params=pltpu.CompilerParams(vmem_limit_bytes=MEDIUM),
        cost_estimate=LIGHT,
    )(where, hidden, scale, gain, projected, *arrays, *earlier)


def ring_total(value, moved):
    after, far, before = moved
    return (value[...] + far[...]) + (after[...] + before[...])


def ring_kernel(value, after, far, before, out_ref):
    out_ref[...] = ring_total(value, (after, far, before))


def bank_kernel(mixing_ref, value, after, far, before, out_ref):
    total = ring_total(value, (after, far, before))
    count = total.shape[1] // SUB
    pieces = jnp.concatenate([total[:, j * SUB:(j + 1) * SUB] for j in range(count)], axis=0)
    out_ref[...] = lax.dot_general(
        mixing_ref[...], pieces, (((0,), (0,)), ((), ())), precision=HIGH, preferred_element_type=F32
    )


def round_kernel(factor, left, right, out_ref):
    out_ref[...] = ((left[...].astype(F32) + right[...].astype(F32)) * factor).astype(out_ref.dtype)


def small_call(kernel, out, operands, *earlier):
    return pl.pallas_call(
        in_order(kernel, len(operands), len(earlier)),
        in_specs=[VMEM] * len(operands) + [ANY] * len(earlier),
        out_specs=VMEM,
        out_shape=out,
        compiler_params=pltpu.CompilerParams(vmem_limit_bytes=SMALL),
        cost_estimate=LIGHT,
    )(*operands, *earlier)


def ring_moves(value, axis):
    return [ring_move(value, axis, d) for d in (-1, 2, 1)]


def shards(hidden_in, preact, norm_gain, weight, bank, mix_index, mix_weight, grad_top):
    section = lax.axis_index("section")
    z, y = lax.axis_index("z"), lax.axis_index("y")
    place = lax.axis_index("pair") * 2 + lax.axis_index("core")
    where = jnp.stack([z, place, y, section]).astype(jnp.int32)
    tensor = ("pair", "core")
    bank_rows = bank.shape[0]

    tokens, local_width = grad_top.shape
    seg_local = local_width // SUB
    seg_row = MODEL_WIDTH // SUB
    own_weight = weight[0]
    shard = own_weight.shape[0]
    half = shard // 2

    first = make_first(where, grad_top, preact[0], own_weight)
    hidden, preact = hidden_in[0], preact[0]

    def local_pieces(array):
        array = array.reshape(2, RANK, seg_row, 2)
        return lax.dynamic_slice_in_dim(array, place * seg_local, seg_local, 2)

    mixing = compose(local_pieces(mix_index[0]), local_pieces(mix_weight[0]), bank_rows)
    mixing = mixing.reshape(2, RANK * seg_local, bank_rows)
    factors = jnp.einsum("fnb,bs->fns", mixing, bank, precision=HIGH)
    a_local = factors[0].reshape(RANK, local_width)
    b_both = two_halves(factors[1].reshape(RANK, local_width))

    hidden_f = hidden.astype(F32)
    sums = lax.psum(
        jnp.concatenate(
            [
                jnp.sum(hidden_f * hidden_f, axis=1)[None],
                jnp.dot(a_local, (hidden_f * norm_gain).T, precision=HIGH),
                jnp.dot(factors[1].reshape(RANK, local_width), first[:tokens].astype(F32).T, precision=HIGH),
            ],
            axis=0,
        ),
        tensor,
    )
    scale_row = lax.rsqrt(sums[:1] / MODEL_WIDTH + epsilon)
    projected = sums[1:1 + RANK] * scale_row
    scale = scale_row.reshape(tokens, 1)
    top_mixed = sums[1 + RANK:]

    z_ring = gather_ring(own_weight, "z", scale)
    y_ring = gather_ring(first, "y", scale)

    _, z_after, z_far_low, z_far_high, z_before = z_ring
    _, y_after, y_far_low, y_far_high, y_before = y_ring
    slim = 112
    rest = shard - slim
    corner_parts = join(where, 0, (z_far_low, z_far_high), ((0, half), (0, half)), y_far_high)
    corner = ring_move(corner_parts, "y", 2, (0,))

    dz_pieces = (y_ring[0], y_ring[1], y_ring[2], y_ring[4])
    mine, keep, send = top_product(where, tokens, dz_pieces, z_ring, y_far_high)
    got = swap(send, "core", (1,))
    theirs = add_theirs(keep, got)
    other = swap(theirs, "pair", (1,))
    along_z = join(
        where, 0, (y_far_low, y_far_high, y_after, y_before),
        ((0, half), (0, half), (slim, rest), (slim, rest)), theirs,
    )
    z_pair = (ring_move(along_z, "z", -1), ring_move(along_z, "z", 1))
    along_y = join(
        where, 0, (z_far_low, z_far_high, z_after, z_before),
        ((0, half), (0, half), (0, slim), (0, slim)), theirs,
    )
    own, to_after, to_far, to_before = add_mine(mine, got, other, corner, along_y)
    from_before = ring_move(to_after, "y", 1, (1,))
    from_far = ring_move(to_far, "y", 2, (1,))
    from_after = ring_move(to_before, "y", -1, (1,))
    along_y = after(along_y, (from_before, from_far, from_after))
    y_pair = (ring_move(along_y, "y", -1, (0,)), ring_move(along_y, "y", 1, (0,)))
    w_pieces = (*z_ring, *y_ring[1:], corner, *y_pair, *z_pair)

    pieces = (own, from_after, from_far, from_before)
    scaled, inner = make_scaled(where, pieces, top_mixed, a_local, norm_gain, hidden, scale)
    top_grad = finish_top(scaled, lax.psum(inner, tensor), hidden, scale, grad_top, 0)
    low_in = lax.ppermute(top_grad, "section", [(1, 0)])

    flat = mixing.reshape(2, RANK, seg_local, bank_rows).transpose(2, 0, 1, 3)
    flat = flat.reshape(2 * RANK * seg_local, bank_rows)
    low_dz, part = make_dz(low_in, preact, b_both, 0, flat)
    low_mixed = lax.psum(part, tensor)
    mine, keep, send = low_product(where, z, y, place, low_dz, w_pieces, low_mixed)
    got = swap(send, "core", (0,))
    theirs = add_theirs(keep, got)
    other = swap(theirs, "pair", (0,))
    scaled, inner = low_scaled(mine, got, other, low_mixed, a_local, norm_gain, hidden, scale)
    inner = lax.psum(inner, tensor)
    grads = make_grads(
        where, hidden, scale, norm_gain, projected, ([first], [low_dz], [top_mixed], [low_mixed])
    )
    over_y = ring_moves(grads, "y")
    grads = small_call(ring_kernel, jax.ShapeDtypeStruct(grads.shape, F32), (grads, *over_y), send)
    over_z = ring_moves(grads, "z")
    bank_shape = (bank_rows, SUB)
    share = small_call(bank_kernel, jax.ShapeDtypeStruct(bank_shape, F32), (flat, grads, *over_z), theirs)
    core_share = swap(share, "core")
    half_shape = jax.ShapeDtypeStruct(bank_shape, BF16)
    add_up = functools.partial(round_kernel, 1.0 / math.sqrt(TOKENS))
    share = small_call(add_up, half_shape, (share, core_share))
    pair_share = swap(share, "pair")
    add_up = functools.partial(round_kernel, 1.0)
    share = small_call(add_up, half_shape, (share, pair_share))
    other_share = lax.ppermute(share, "section", [(0, 1), (1, 0)])
    result, bank_grad = finish_low(
        where, scaled, inner, hidden, scale, low_in, share, other_share, top_grad
    )
    return (result[None], bank_grad)


def solution(mesh):
    fine = Mesh(
        mesh.devices.reshape(2, RING, RING, 2, 2), ("section", "z", "y", "pair", "core")
    )
    rows, columns = ("z", "y"), ("pair", "core")
    return jax.shard_map(
        shards,
        mesh=fine,
        in_specs=(
            P("section", rows, columns),
            P("section", rows, columns),
            P("section", columns),
            P("section", rows, columns),
            P(),
            P("section", None, None, None),
            P("section", None, None, None),
            P(rows, columns),
        ),
        out_specs=(P("section", rows, columns), P()),
        check_vma=False,
    )
```

```python
import functools
import math

import jax
import jax.numpy as jnp
from jax import lax
from jax.experimental import pallas as pl
from jax.experimental.pallas import tpu as pltpu
from jax.sharding import Mesh, PartitionSpec as P

MODEL_WIDTH = 8192
RANK = 4
SUB = 256
TOKENS = 4096
RING = 4
LANES = 128

epsilon = 1e-06
HIGH = lax.Precision.HIGHEST
F32 = jnp.float32
BF16 = jnp.bfloat16
ANY = pl.BlockSpec(memory_space=pl.ANY)
SMEM = pl.BlockSpec(memory_space=pltpu.SMEM)
VMEM = pl.BlockSpec(memory_space=pltpu.VMEM)
HBM = pl.BlockSpec(memory_space=pltpu.HBM)
BIG = 48 * 1024 * 1024
MEDIUM = 20 * 1024 * 1024
SMALL = 12 * 1024 * 1024
LIGHT = pl.CostEstimate(flops=0, bytes_accessed=2 ** 20, transcendentals=0)


def ring_route(distance, sections=(0, 1)):
    return [(s * RING + i, s * RING + (i + distance) % RING) for s in sections for i in range(RING)]


def ring_move(block, axis, distance, sections=(0, 1)):
    return lax.ppermute(block, ("section", axis), ring_route(distance, sections))


def swap(block, axis, sections=(0, 1)):
    pairs = [(s * 2 + i, s * 2 + 1 - i) for s in sections for i in range(2)]
    return lax.ppermute(block, ("section", axis), pairs)


def after(value, earlier):
    return lax.optimization_barrier((value, earlier))[0]


def in_order(kernel, operands, extra):
    return lambda *refs: kernel(*refs[:operands], *refs[operands + extra:])


def compose(index_layer, weight_layer, rows):
    columns = lax.broadcasted_iota(jnp.int32, (1, 1, 1, 1, rows), 4)
    onehot = (index_layer[..., None] == columns).astype(F32)
    return jnp.sum(onehot * weight_layer[..., None], axis=3)


def two_halves(value):
    high = value.astype(BF16)
    return jnp.concatenate([high, (value - high.astype(F32)).astype(BF16)], axis=0)


def activation_gradient(incoming_ref, preact_ref):
    value = preact_ref[...].astype(F32)
    sig = jax.nn.sigmoid(value)
    slope = sig * (1.0 + value * (1.0 - sig))
    return (incoming_ref[...].astype(F32) * slope).astype(BF16)


def dz_kernel(incoming_ref, preact_ref, b_ref, dz_ref, mixed_ref):
    dz = activation_gradient(incoming_ref, preact_ref)
    dz_ref[...] = dz
    both = lax.dot_general(b_ref[...], dz, (((1,), (1,)), ((), ())), preferred_element_type=F32)
    mixed_ref[...] = both[:RANK] + both[RANK:]


def first_kernel(where_ref, incoming_ref, preact_ref, weight_ref, out_ref, incoming, preact, sem):
    def fetch(*pairs):
        copies = [pltpu.make_async_copy(*pair, sem.at[i]) for i, pair in enumerate(pairs)]
        for copy in copies:
            copy.start()
        for copy in copies:
            copy.wait()

    @pl.when(where_ref[3] == 1)
    def _():
        fetch((incoming_ref, incoming), (preact_ref, preact))
        out_ref[:incoming.shape[0]] = activation_gradient(incoming, preact)

    @pl.when(where_ref[3] == 0)
    def _():
        fetch((weight_ref, out_ref))


def make_first(where, incoming, preact, weight):
    return pl.pallas_call(
        first_kernel,
        in_specs=[SMEM, HBM, HBM, HBM],
        out_specs=VMEM,
        out_shape=jax.ShapeDtypeStruct(weight.shape, BF16),
        scratch_shapes=[
            pltpu.VMEM(incoming.shape, BF16),
            pltpu.VMEM(incoming.shape, BF16),
            pltpu.SemaphoreType.DMA((2,)),
        ],
        compiler_params=pltpu.CompilerParams(vmem_limit_bytes=MEDIUM),
        cost_estimate=LIGHT,
    )(where, incoming, preact, weight)


def join_kernel(wanted, parts, where_ref, *refs):
    sources, out_ref, held, sem, out_sem = refs[:len(parts)], *refs[-4:]

    @pl.when(where_ref[3] == wanted)
    def _():
        start = 0
        steps = []
        for i, (first, rows) in enumerate(parts):
            here = held.at[pl.ds(start, rows)]
            fetch = pltpu.make_async_copy(sources[i].at[pl.ds(first, rows)], here, sem.at[i])
            store = pltpu.make_async_copy(here, out_ref.at[pl.ds(start, rows)], out_sem.at[i])
            steps.append((fetch, store))
            start += rows
        for fetch, _ in steps:
            fetch.start()
        for fetch, store in steps:
            fetch.wait()
            store.start()
        for _, store in steps:
            store.wait()


def join(where, wanted, arrays, parts, *earlier):
    rows, width = sum(count for _, count in parts), arrays[0].shape[1]
    return pl.pallas_call(
        in_order(functools.partial(join_kernel, wanted, parts), 1 + len(arrays), len(earlier)),
        in_specs=[SMEM] + [ANY] * (len(arrays) + len(earlier)),
        out_specs=HBM,
        out_shape=jax.ShapeDtypeStruct((rows, width), BF16),
        scratch_shapes=[
            pltpu.VMEM((rows, width), BF16),
            pltpu.SemaphoreType.DMA((len(arrays),)),
            pltpu.SemaphoreType.DMA((len(arrays),)),
        ],
        compiler_params=pltpu.CompilerParams(vmem_limit_bytes=SMALL),
        cost_estimate=LIGHT,
    )(where, *arrays, *earlier)


def halves_kernel(after_ref, before_ref, low_ref, high_ref, sem):
    half = low_ref.shape[0]
    low = pltpu.make_async_copy(after_ref.at[pl.ds(0, half)], low_ref, sem.at[0])
    high = pltpu.make_async_copy(before_ref.at[pl.ds(half, half)], high_ref, sem.at[1])
    low.start()
    high.start()
    low.wait()
    high.wait()


def gather_ring(block, axis, *earlier):
    rows, width = block.shape
    after = ring_move(block, axis, -1)
    before = ring_move(block, axis, 1)
    low, high = pl.pallas_call(
        in_order(halves_kernel, 2, len(earlier)),
        in_specs=[ANY, ANY] + [ANY] * len(earlier),
        out_specs=[VMEM, VMEM],
        out_shape=[jax.ShapeDtypeStruct((rows // 2, width), BF16)] * 2,
        scratch_shapes=[pltpu.SemaphoreType.DMA((2,))],
        compiler_params=pltpu.CompilerParams(vmem_limit_bytes=SMALL),
        cost_estimate=LIGHT,
    )(after, before, *earlier)
    return block, after, ring_move(low, axis, -1), ring_move(high, axis, 1), before


def make_dz(incoming, preact, b_both, c, *earlier):
    rows, width = incoming.shape
    return pl.pallas_call(
        in_order(dz_kernel, 3, len(earlier)),
        grid=(1,),
        in_specs=[
            pl.BlockSpec((rows, width), lambda i: (0, 0)),
            pl.BlockSpec((rows, width), lambda i: (c, 0)),
            pl.BlockSpec((2 * RANK, width), lambda i: (0, 0)),
        ]
        + [ANY] * len(earlier),
        out_specs=[
            pl.BlockSpec((rows, width), lambda i: (0, 0)),
            pl.BlockSpec((RANK, rows), lambda i: (0, 0)),
        ],
        out_shape=[
            jax.ShapeDtypeStruct((rows, width), BF16),
            jax.ShapeDtypeStruct((RANK, rows), F32),
        ],
        compiler_params=pltpu.CompilerParams(vmem_limit_bytes=MEDIUM),
        cost_estimate=LIGHT,
    )(incoming, preact, b_both, *earlier)


def top_product_kernel(rows, where_ref, *refs):
    dz_refs, w_refs = refs[:4], refs[4:9]
    mine_ref, theirs_ref, send_ref, dz_all, w_all, dz_sem, w_sem = refs[9:]

    @pl.when(where_ref[3] == 1)
    def _():
        copies = [
            pltpu.make_async_copy(ref.at[pl.ds(0, rows)], dz_all.at[pl.ds(i * rows, rows)], dz_sem.at[i])
            for i, ref in enumerate(dz_refs)
        ]
        for copy in copies:
            copy.start()
        own, after, far_low, far_high, before = w_refs
        half = far_low.shape[0]
        pltpu.make_async_copy(own, w_all.at[0], w_sem.at[0]).start()
        pltpu.make_async_copy(after, w_all.at[1], w_sem.at[1]).start()
        pltpu.make_async_copy(far_low, w_all.at[2, pl.ds(0, half)], w_sem.at[2]).start()
        pltpu.make_async_copy(far_high, w_all.at[2, pl.ds(half, half)], w_sem.at[2]).start()
        pltpu.make_async_copy(before, w_all.at[3], w_sem.at[3]).start()
        for copy in copies:
            copy.wait()
        z, place = where_ref[0], where_ref[1]

        @pl.loop(0, RING)
        def _(i):
            pltpu.make_async_copy(own, w_all.at[i], w_sem.at[i]).wait()
            value = lax.dot_general(
                dz_all[...], w_all[i], (((1,), (1,)), ((), ())), preferred_element_type=F32
            ).astype(BF16)
            target = lax.rem(z + i, RING)
            own_core = lax.rem(target, 2) == lax.rem(place, 2)
            far = jnp.where(target // 2 == place // 2, 0, 1)

            @pl.when(jnp.logical_and(own_core, far == 0))
            def _():
                mine_ref[...] = value

            @pl.when(jnp.logical_and(own_core, far == 1))
            def _():
                theirs_ref[...] = value

            @pl.when(jnp.logical_not(own_core))
            def _():
                send_ref[far] = value


def top_product(where, rows, dz_pieces, w_pieces, *earlier):
    wide, width = w_pieces[0].shape
    return pl.pallas_call(
        in_order(functools.partial(top_product_kernel, rows), 10, len(earlier)),
        in_specs=[SMEM] + [HBM] * 9 + [ANY] * len(earlier),
        out_specs=[VMEM, VMEM, VMEM],
        out_shape=[jax.ShapeDtypeStruct((RING * rows, wide), BF16)] * 2
        + [jax.ShapeDtypeStruct((2, RING * rows, wide), BF16)],
        scratch_shapes=[
            pltpu.VMEM((RING * rows, width), BF16),
            pltpu.VMEM((RING, wide, width), BF16),
            pltpu.SemaphoreType.DMA((4,)),
            pltpu.SemaphoreType.DMA((RING,)),
        ],
        compiler_params=pltpu.CompilerParams(vmem_limit_bytes=36 * 1024 * 1024),
        cost_estimate=pl.CostEstimate(
            flops=2 * RING * RING * rows * wide * width, bytes_accessed=2 ** 24, transcendentals=0
        ),
    )(where, *dz_pieces, *w_pieces, *earlier)


def low_plan(shard, wide):
    copies, blocks = [], []

    def take(array, row, rows, *names):
        at = sum(rows for *_, rows in copies)
        copies.append((array, row, at, rows))
        blocks.extend(names)

    for base, step in ((0, lambda d, h: (d, 0, h)), (4, lambda d, h: (0, d, h))):
        if base == 0:
            take(0, 0, shard, step(0, 0), step(0, 1))
        take(base + 1, 0, shard, step(1, 0), step(1, 1))
        take(base + 2, 0, wide, step(2, 0))
        take(base + 3, 0, wide, step(2, 1))
        take(base + 4, 0, shard, step(3, 0), step(3, 1))
    corner, y_pair, z_pair = 9, {1: 10, 3: 11}, {1: 12, 3: 13}
    take(corner, 0, shard, (2, 2, 0), (2, 2, 1))
    for d in (1, 3):
        take(y_pair[d], 0, shard, (2, d, 0), (2, d, 1))
        take(z_pair[d], 0, shard, (d, 2, 0), (d, 2, 1))
    slim = 112
    rest = shard - slim
    for i, d in enumerate((1, 3)):
        for j, e in enumerate((1, 3)):
            take(y_pair[e], shard + i * slim, slim)
            take(z_pair[d], shard + j * rest, rest, (d, e, 0), (d, e, 1))
    return copies, blocks


def low_product_kernel(plan, where_ref, table_ref, dz_ref, *refs):
    count = len(refs) - 7
    w_refs = refs[:count]
    mine_ref, theirs_ref, send_ref, dz_all, w_all, dz_sem, sem = refs[count:]
    steps, deep = w_all.shape[0], w_all.shape[1]
    wide = deep // 2

    @pl.when(where_ref[3] == 0)
    def _():
        dz_copy = pltpu.make_async_copy(dz_ref, dz_all, dz_sem)
        dz_copy.start()
        for array, row, at, rows in plan:
            while rows:
                part = min(rows, deep - at % deep)
                pltpu.make_async_copy(
                    w_refs[array].at[pl.ds(row, part)],
                    w_all.at[at // deep, pl.ds(at % deep, part)],
                    sem.at[at // deep],
                ).start()
                row, at, rows = row + part, at + part, rows - part
        dz_copy.wait()

        @pl.loop(0, steps)
        def _(step):
            pltpu.make_async_copy(w_refs[0], w_all.at[step], sem.at[step]).wait()
            value = lax.dot_general(
                dz_all[...], w_all[step], (((1,), (1,)), ((), ())), preferred_element_type=F32
            ).astype(BF16)
            for k in range(2):
                entry = table_ref[2 * step + k]
                columns = pl.ds(pl.multiple_of(lax.rem(entry, 2 * RING) * wide, wide), wide)
                far = lax.rem(entry // (2 * RING), 2)
                block = value[:, k * wide:(k + 1) * wide]

                @pl.when(entry < 2 * RING)
                def _():
                    mine_ref[:, columns] = block

                @pl.when(jnp.logical_and(entry >= 2 * RING, entry < 4 * RING))
                def _():
                    theirs_ref[:, columns] = block

                @pl.when(entry >= 4 * RING)
                def _():
                    send_ref[far, :, columns] = block


def low_product(where, z, y, place, dz, w_pieces, *earlier):
    rows, width = dz.shape
    shard = w_pieces[0].shape[0]
    wide = shard // 2
    copies, blocks = low_plan(shard, wide)
    steps = [jnp.array(column, jnp.int32) for column in zip(*blocks)]
    target = (z + steps[0]) % RING
    column = (y + steps[1]) % RING * 2 + steps[2]
    other_core = (target % 2 != place % 2).astype(jnp.int32)
    other_pair = (target // 2 != place // 2).astype(jnp.int32)
    table = (other_core * 2 + other_pair) * 2 * RING + column
    return pl.pallas_call(
        in_order(functools.partial(low_product_kernel, copies), 3 + len(w_pieces), len(earlier)),
        in_specs=[SMEM, SMEM, HBM] + [HBM] * len(w_pieces) + [ANY] * len(earlier),
        out_specs=[VMEM, VMEM, VMEM],
        out_shape=[jax.ShapeDtypeStruct((rows, 2 * RING * wide), BF16)] * 2
        + [jax.ShapeDtypeStruct((2, rows, 2 * RING * wide), BF16)],
        scratch_shapes=[
            pltpu.VMEM((rows, width), BF16),
            pltpu.VMEM((RING * RING, shard, width), BF16),
            pltpu.SemaphoreType.DMA,
            pltpu.SemaphoreType.DMA((RING * RING,)),
        ],
        compiler_params=pltpu.CompilerParams(vmem_limit_bytes=BIG),
        cost_estimate=pl.CostEstimate(
            flops=16 * RING * rows * wide * width, bytes_accessed=2 ** 25, transcendentals=0
        ),
    )(where, table, dz, *w_pieces, *earlier)


def add_kernel(keep_ref, got_ref, out_ref):
    out_ref[...] = (keep_ref[...].astype(F32) + got_ref[0].astype(F32)).astype(BF16)


def add_theirs(keep, got):
    rows, wide = keep.shape
    whole = pl.BlockSpec((rows, wide), lambda i: (0, 0))
    return pl.pallas_call(
        add_kernel,
        grid=(1,),
        in_specs=[whole, pl.BlockSpec((1, rows, wide), lambda i: (1, 0, 0))],
        out_specs=whole,
        out_shape=jax.ShapeDtypeStruct((rows, wide), BF16),
        compiler_params=pltpu.CompilerParams(vmem_limit_bytes=SMALL),
        cost_estimate=LIGHT,
    )(keep, got)


def total_kernel(keep_ref, got_ref, other_ref, *out_refs):
    rows = out_refs[0].shape[0]
    for i, ref in enumerate(out_refs):
        part = pl.ds(i * rows, rows)
        ref[...] = (
            keep_ref[part].astype(F32) + got_ref[0, part].astype(F32) + other_ref[part].astype(F32)
        ).astype(BF16)


def add_mine(keep, got, other, *earlier):
    rows, wide = keep.shape
    whole = pl.BlockSpec((rows, wide), lambda i: (0, 0))
    return pl.pallas_call(
        in_order(total_kernel, 3, len(earlier)),
        grid=(1,),
        in_specs=[whole, pl.BlockSpec((1, rows, wide), lambda i: (0, 0, 0)), whole] + [ANY] * len(earlier),
        out_specs=[pl.BlockSpec((rows // RING, wide), lambda i: (0, 0))] * RING,
        out_shape=[jax.ShapeDtypeStruct((rows // RING, wide), BF16)] * RING,
        compiler_params=pltpu.CompilerParams(vmem_limit_bytes=SMALL),
        cost_estimate=LIGHT,
    )(keep, got, other, *earlier)


def as_row(column):
    square = jnp.broadcast_to(column, (column.shape[0], LANES))
    return jnp.transpose(square)[:8]


def as_column(row):
    square = jnp.concatenate([row] * (LANES // 8), axis=0)
    return jnp.transpose(square)[:, :1]


def scaled_kernel(where_ref, own, after, far, before, mixed_ref, a_ref, gain_ref, hidden_ref, scale_ref, scaled_ref, inner_ref):
    wide = own.shape[1]
    mixed = mixed_ref[...]
    inner = jnp.zeros((own.shape[0], 1), F32)
    for r, piece in enumerate((own, after, far, before)):
        at = pl.ds(pl.multiple_of(lax.rem(where_ref[2] + r, RING) * wide, wide), wide)
        low_rank = lax.dot_general(
            mixed, a_ref[:, at], (((0,), (0,)), ((), ())), precision=HIGH, preferred_element_type=F32
        )
        scaled = gain_ref[:, at] * (piece[...].astype(F32) + low_rank)
        scaled_ref[:, at] = scaled.astype(BF16)
        inner = inner + jnp.sum(scaled * hidden_ref[:, at].astype(F32), axis=1, keepdims=True)
    inner_ref[...] = as_row(inner * scale_ref[...])


def make_scaled(where, pieces, mixed, a_local, gain, hidden, scale):
    rows, width = hidden.shape
    return pl.pallas_call(
        scaled_kernel,
        in_specs=[SMEM] + [VMEM] * 9,
        out_specs=[VMEM, VMEM],
        out_shape=[jax.ShapeDtypeStruct((rows, width), BF16), jax.ShapeDtypeStruct((8, rows), F32)],
        compiler_params=pltpu.CompilerParams(vmem_limit_bytes=MEDIUM),
        cost_estimate=LIGHT,
    )(where, *pieces, mixed, a_local, gain, hidden, scale)


def low_scaled_kernel(keep_ref, got_ref, other_ref, mixed_ref, a_ref, gain_ref, hidden_ref, scale_ref, scaled_ref, inner_ref):
    low_rank = lax.dot_general(
        mixed_ref[...], a_ref[...], (((0,), (0,)), ((), ())), precision=HIGH, preferred_element_type=F32
    )
    total = keep_ref[...].astype(F32) + got_ref[0].astype(F32) + other_ref[...].astype(F32)
    scaled = gain_ref[...] * (total + low_rank)
    scaled_ref[...] = scaled.astype(BF16)
    inner = jnp.sum(scaled * hidden_ref[...].astype(F32), axis=1, keepdims=True)
    inner_ref[...] = as_row(inner * scale_ref[...])


def low_scaled(keep, got, other, mixed, a_local, gain, hidden, scale):
    rows, width = hidden.shape
    whole = lambda shape: pl.BlockSpec(shape, lambda i: (0, 0))
    mine = pl.BlockSpec((1, rows, width), lambda i: (0, 0, 0))
    return pl.pallas_call(
        low_scaled_kernel,
        grid=(1,),
        in_specs=[
            whole((rows, width)), mine, whole((rows, width)), whole((RANK, rows)), whole((RANK, width)),
            whole((1, width)), whole((rows, width)), whole((rows, 1)),
        ],
        out_specs=[whole((rows, width)), whole((8, rows))],
        out_shape=[jax.ShapeDtypeStruct((rows, width), BF16), jax.ShapeDtypeStruct((8, rows), F32)],
        compiler_params=pltpu.CompilerParams(vmem_limit_bytes=MEDIUM),
        cost_estimate=LIGHT,
    )(keep, got, other, mixed, a_local, gain, hidden, scale)


def hidden_gradient(scaled_ref, inner_ref, hidden_ref, scale_ref, incoming_ref):
    scale = scale_ref[...]
    pull = as_column(inner_ref[...]) * scale / MODEL_WIDTH
    return (
        incoming_ref[...].astype(F32)
        + scale * (scaled_ref[...].astype(F32) - hidden_ref[...].astype(F32) * pull)
    ).astype(BF16)


def top_kernel(scaled_ref, inner_ref, hidden_ref, scale_ref, incoming_ref, out_ref):
    out_ref[...] = hidden_gradient(scaled_ref, inner_ref, hidden_ref, scale_ref, incoming_ref)


def low_kernel(
    where_ref, scaled_ref, inner_ref, hidden_ref, scale_ref, incoming_ref, share_ref, other_ref, top_ref,
    out_ref, bank_ref, sem,
):
    bank_ref[...] = share_ref[...].astype(F32) + other_ref[...].astype(F32)

    @pl.when(where_ref[3] == 0)
    def _():
        out_ref[...] = hidden_gradient(scaled_ref, inner_ref, hidden_ref, scale_ref, incoming_ref)

    @pl.when(where_ref[3] == 1)
    def _():
        copy = pltpu.make_async_copy(top_ref, out_ref, sem)
        copy.start()
        copy.wait()


def finish_specs(rows, width, c):
    whole = lambda shape: pl.BlockSpec(shape, lambda i: (0, 0))
    return [
        whole((rows, width)),
        whole((8, rows)),
        pl.BlockSpec((rows, width), lambda i: (c, 0)),
        pl.BlockSpec((rows, 1), lambda i: (c, 0)),
    ]


def finish_top(scaled, inner, hidden, scale, grad_top, c):
    rows, width = scaled.shape
    return pl.pallas_call(
        top_kernel,
        grid=(1,),
        in_specs=finish_specs(rows, width, c) + [pl.BlockSpec((rows, width), lambda i: (c, 0))],
        out_specs=pl.BlockSpec((rows, width), lambda i: (0, 0)),
        out_shape=jax.ShapeDtypeStruct((rows, width), BF16),
        compiler_params=pltpu.CompilerParams(vmem_limit_bytes=MEDIUM),
        cost_estimate=LIGHT,
    )(scaled, inner, hidden, scale, grad_top)


def finish_low(where, scaled, inner, hidden, scale, incoming, share, other, top):
    rows, width = scaled.shape
    block = pl.BlockSpec((rows, width), lambda i: (0, 0))
    bank = pl.BlockSpec(share.shape, lambda i: (0, 0))
    return pl.pallas_call(
        low_kernel,
        grid=(1,),
        in_specs=[SMEM] + finish_specs(rows, width, 0) + [block, bank, bank, HBM],
        out_specs=[block, bank],
        out_shape=[jax.ShapeDtypeStruct((rows, width), BF16), jax.ShapeDtypeStruct(share.shape, F32)],
        scratch_shapes=[pltpu.SemaphoreType.DMA],
        compiler_params=pltpu.CompilerParams(vmem_limit_bytes=MEDIUM),
        cost_estimate=LIGHT,
    )(where, scaled, inner, hidden, scale, incoming, share, other, top)


def grads_kernel(
    where_ref, hidden_ref, scale_ref, gain_ref, projected_ref, top_mixed, low_mixed, top_dz, low_dz,
    out_ref, dz_ref, sem,
):
    top = where_ref[3] == 1
    rows = dz_ref.shape[0]

    @pl.when(top)
    def _():
        pltpu.make_async_copy(top_dz.at[pl.ds(0, rows)], dz_ref, sem).start()

    @pl.when(jnp.logical_not(top))
    def _():
        pltpu.make_async_copy(low_dz, dz_ref, sem).start()

    def both(left, right):
        value = lax.dot_general(
            two_halves(left), right, (((1,), (0,)), ((), ())), preferred_element_type=F32
        )
        return value[:RANK] + value[RANK:]

    mixed = jnp.where(top, top_mixed[...], low_mixed[...])
    x = (hidden_ref[...].astype(F32) * scale_ref[...] * gain_ref[...]).astype(BF16)
    out_ref[:RANK] = both(mixed, x)
    pltpu.make_async_copy(low_dz, dz_ref, sem).wait()
    out_ref[RANK:] = both(projected_ref[...], dz_ref[...])


def make_grads(where, hidden, scale, gain, projected, top_mixed, low_mixed, top_dz, low_dz):
    return pl.pallas_call(
        grads_kernel,
        in_specs=[SMEM] + [VMEM] * 6 + [HBM] * 2,
        out_specs=VMEM,
        out_shape=jax.ShapeDtypeStruct((2 * RANK, hidden.shape[1]), F32),
        scratch_shapes=[pltpu.VMEM(low_dz.shape, BF16), pltpu.SemaphoreType.DMA],
        compiler_params=pltpu.CompilerParams(vmem_limit_bytes=MEDIUM),
        cost_estimate=LIGHT,
    )(where, hidden, scale, gain, projected, top_mixed, low_mixed, top_dz, low_dz)


def ring_total(value, moved):
    after, far, before = moved
    return (value[...] + far[...]) + (after[...] + before[...])


def ring_kernel(value, after, far, before, out_ref):
    out_ref[...] = ring_total(value, (after, far, before))


def bank_kernel(mixing_ref, value, after, far, before, out_ref):
    total = ring_total(value, (after, far, before))
    count = total.shape[1] // SUB
    pieces = jnp.concatenate([total[:, j * SUB:(j + 1) * SUB] for j in range(count)], axis=0)
    out_ref[...] = lax.dot_general(
        mixing_ref[...], pieces, (((0,), (0,)), ((), ())), precision=HIGH, preferred_element_type=F32
    )


def round_kernel(factor, left, right, out_ref):
    out_ref[...] = ((left[...].astype(F32) + right[...].astype(F32)) * factor).astype(out_ref.dtype)


def small_call(kernel, out, operands, *earlier):
    return pl.pallas_call(
        in_order(kernel, len(operands), len(earlier)),
        in_specs=[VMEM] * len(operands) + [ANY] * len(earlier),
        out_specs=VMEM,
        out_shape=out,
        compiler_params=pltpu.CompilerParams(vmem_limit_bytes=SMALL),
        cost_estimate=LIGHT,
    )(*operands, *earlier)


def ring_moves(value, axis):
    return [ring_move(value, axis, d) for d in (-1, 2, 1)]


def shards(hidden_in, preact, norm_gain, weight, bank, mix_index, mix_weight, grad_top):
    section = lax.axis_index("section")
    z, y = lax.axis_index("z"), lax.axis_index("y")
    place = lax.axis_index("pair") * 2 + lax.axis_index("core")
    where = jnp.stack([z, place, y, section]).astype(jnp.int32)
    tensor = ("pair", "core")
    bank_rows = bank.shape[0]

    tokens, local_width = grad_top.shape
    seg_local = local_width // SUB
    seg_row = MODEL_WIDTH // SUB
    own_weight = weight[0]
    shard = own_weight.shape[0]
    half = shard // 2

    first = make_first(where, grad_top, preact[0], own_weight)
    hidden, preact = hidden_in[0], preact[0]

    def local_pieces(array):
        array = array.reshape(2, RANK, seg_row, 2)
        return lax.dynamic_slice_in_dim(array, place * seg_local, seg_local, 2)

    mixing = compose(local_pieces(mix_index[0]), local_pieces(mix_weight[0]), bank_rows)
    mixing = mixing.reshape(2, RANK * seg_local, bank_rows)
    factors = jnp.einsum("fnb,bs->fns", mixing, bank, precision=HIGH)
    a_local = factors[0].reshape(RANK, local_width)
    b_both = two_halves(factors[1].reshape(RANK, local_width))

    hidden_f = hidden.astype(F32)
    sums = lax.psum(
        jnp.concatenate(
            [
                jnp.sum(hidden_f * hidden_f, axis=1)[None],
                jnp.dot(a_local, (hidden_f * norm_gain).T, precision=HIGH),
                jnp.dot(factors[1].reshape(RANK, local_width), first[:tokens].astype(F32).T, precision=HIGH),
            ],
            axis=0,
        ),
        tensor,
    )
    scale_row = lax.rsqrt(sums[:1] / MODEL_WIDTH + epsilon)
    projected = sums[1:1 + RANK] * scale_row
    scale = scale_row.reshape(tokens, 1)
    top_mixed = sums[1 + RANK:]

    z_ring = gather_ring(own_weight, "z", scale)
    y_ring = gather_ring(first, "y", scale)

    _, z_after, z_far_low, z_far_high, z_before = z_ring
    _, y_after, y_far_low, y_far_high, y_before = y_ring
    slim = 112
    rest = shard - slim
    corner_parts = join(where, 0, (z_far_low, z_far_high), ((0, half), (0, half)), y_far_high)
    corner = ring_move(corner_parts, "y", 2, (0,))

    dz_pieces = (y_ring[0], y_ring[1], y_ring[2], y_ring[4])
    mine, keep, send = top_product(where, tokens, dz_pieces, z_ring, y_far_high)
    got = swap(send, "core", (1,))
    theirs = add_theirs(keep, got)
    other = swap(theirs, "pair", (1,))
    along_z = join(
        where, 0, (y_far_low, y_far_high, y_after, y_before),
        ((0, half), (0, half), (slim, rest), (slim, rest)), theirs,
    )
    z_pair = (ring_move(along_z, "z", -1), ring_move(along_z, "z", 1))
    along_y = join(
        where, 0, (z_far_low, z_far_high, z_after, z_before),
        ((0, half), (0, half), (0, slim), (0, slim)), theirs,
    )
    own, to_after, to_far, to_before = add_mine(mine, got, other, corner, along_y)
    from_before = ring_move(to_after, "y", 1, (1,))
    from_far = ring_move(to_far, "y", 2, (1,))
    from_after = ring_move(to_before, "y", -1, (1,))
    along_y = after(along_y, (from_before, from_far, from_after))
    y_pair = (ring_move(along_y, "y", -1, (0,)), ring_move(along_y, "y", 1, (0,)))
    w_pieces = (*z_ring, *y_ring[1:], corner, *y_pair, *z_pair)

    pieces = (own, from_after, from_far, from_before)
    scaled, inner = make_scaled(where, pieces, top_mixed, a_local, norm_gain, hidden, scale)
    top_grad = finish_top(scaled, lax.psum(inner, tensor), hidden, scale, grad_top, 0)
    low_in = lax.ppermute(top_grad, "section", [(1, 0)])

    flat = mixing.reshape(2, RANK, seg_local, bank_rows).transpose(2, 0, 1, 3)
    flat = flat.reshape(2 * RANK * seg_local, bank_rows)
    low_dz, part = make_dz(low_in, preact, b_both, 0, flat)
    low_mixed = lax.psum(part, tensor)
    mine, keep, send = low_product(where, z, y, place, low_dz, w_pieces, low_mixed)
    got = swap(send, "core", (0,))
    theirs = add_theirs(keep, got)
    other = swap(theirs, "pair", (0,))
    scaled, inner = low_scaled(mine, got, other, low_mixed, a_local, norm_gain, hidden, scale)
    inner = lax.psum(inner, tensor)
    grads = make_grads(where, hidden, scale, norm_gain, projected, top_mixed, low_mixed, first, low_dz)
    over_y = ring_moves(grads, "y")
    grads = small_call(ring_kernel, jax.ShapeDtypeStruct(grads.shape, F32), (grads, *over_y), send)
    over_z = ring_moves(grads, "z")
    bank_shape = (bank_rows, SUB)
    share = small_call(bank_kernel, jax.ShapeDtypeStruct(bank_shape, F32), (flat, grads, *over_z), theirs)
    core_share = swap(share, "core")
    half_shape = jax.ShapeDtypeStruct(bank_shape, BF16)
    add_up = functools.partial(round_kernel, 1.0 / math.sqrt(TOKENS))
    share = small_call(add_up, half_shape, (share, core_share))
    pair_share = swap(share, "pair")
    add_up = functools.partial(round_kernel, 1.0)
    share = small_call(add_up, half_shape, (share, pair_share))
    other_share = lax.ppermute(share, "section", [(0, 1), (1, 0)])
    result, bank_grad = finish_low(
        where, scaled, inner, hidden, scale, low_in, share, other_share, top_grad
    )
    return (result[None], bank_grad)


def solution(mesh):
    fine = Mesh(
        mesh.devices.reshape(2, RING, RING, 2, 2), ("section", "z", "y", "pair", "core")
    )
    rows, columns = ("z", "y"), ("pair", "core")
    return jax.shard_map(
        shards,
        mesh=fine,
        in_specs=(
            P("section", rows, columns),
            P("section", rows, columns),
            P("section", columns),
            P("section", rows, columns),
            P(),
            P("section", None, None, None),
            P("section", None, None, None),
            P(rows, columns),
        ),
        out_specs=(P("section", rows, columns), P()),
        check_vma=False,
    )
```
